128 devices in a mesh: pipe: 2 (over x_hi), dp: 16 (over y, z), tensor: 4 (over x_lo, core).
Axes of the slice: x: 4 (x_hi: 2, x_lo: 2; x = x_hi * 2 + x_lo), y: 4, z: 4, core: 2. Of those that a mesh axis runs over, the one named last changes fastest.
Arguments:
- inputs: bfloat16 [8192, 1024], P('dp'), may hold values from -6 to 6
- memories: bfloat16 [2, 16, 512, 1024], P('pipe', 'dp'), may hold values from -6 to 6
- compressed: bfloat16 [2, 16, 512, 1024], P('pipe', 'dp'), may hold values from -6 to 6
- documents: int32 [16, 1536], P('dp'), may hold values from 0 to 3, as said below
- cotangent: bfloat16 [8192, 1024], P('dp'), may hold values from -6 to 6
- compressed_cotangent: bfloat16 [2, 16, 256, 1024], P('pipe', 'dp', None, 'tensor'), may hold values from -6 to 6
- query_weight: bfloat16 [2, 1024, 1024], P('pipe', None, 'tensor'), may hold values from -0.1875 to 0.1875
- key_weight: bfloat16 [2, 1024, 1024], P('pipe', None, 'tensor'), may hold values from -0.1875 to 0.1875
- value_weight: bfloat16 [2, 1024, 1024], P('pipe', None, 'tensor'), may hold values from -0.1875 to 0.1875
- output_weight: bfloat16 [2, 1024, 1024], P('pipe', 'tensor'), may hold values from -3 to 3
- output_bias: bfloat16 [2, 1024], P('pipe'), may hold values from -2 to 2
- inner_weight: bfloat16 [2, 1024, 4096], P('pipe', None, 'tensor'), may hold values from -0.1875 to 0.1875
- inner_bias: bfloat16 [2, 4096], P('pipe', 'tensor'), may hold values from -2 to 2
- outer_weight: bfloat16 [2, 4096, 1024], P('pipe', 'tensor'), may hold values from -0.09375 to 0.09375
- outer_bias: bfloat16 [2, 1024], P('pipe'), may hold values from -2 to 2
- conv_weight: bfloat16 [2, 2, 1024, 1024], P('pipe', None, None, 'tensor'), may hold values from -0.125 to 0.125
- conv_bias: bfloat16 [2, 1024], P('pipe', 'tensor'), may hold values from -2 to 2
- attn_gain: bfloat16 [2, 1024], P('pipe'), may hold values from 0.5 to 1.5
- attn_shift: bfloat16 [2, 1024], P('pipe'), may hold values from -2 to 2
- ffn_gain: bfloat16 [2, 1024], P('pipe'), may hold values from 0.5 to 1.5
- ffn_shift: bfloat16 [2, 1024], P('pipe'), may hold values from -2 to 2
Outputs:
- hidden_states: float32 [2, 8192, 1024], P('pipe', 'dp')
- new_compressed: bfloat16 [2, 16, 512, 1024], P('pipe', 'dp', None, 'tensor')
- input_grads: float32 [2, 8192, 1024], P('pipe', 'dp')
- query_grad: float32 [2, 1024, 1024], P('pipe', None, 'tensor')
- key_grad: float32 [2, 1024, 1024], P('pipe', None, 'tensor')
- value_grad: float32 [2, 1024, 1024], P('pipe', None, 'tensor')
- output_grad: float32 [2, 1024, 1024], P('pipe', 'tensor')
- output_bias_grad: float32 [2, 1024], P('pipe')
- inner_grad: float32 [2, 1024, 4096], P('pipe', None, 'tensor')
- inner_bias_grad: float32 [2, 4096], P('pipe', 'tensor')
- outer_grad: float32 [2, 4096, 1024], P('pipe', 'tensor')
- outer_bias_grad: float32 [2, 1024], P('pipe')
- conv_grad: float32 [2, 2, 1024, 1024], P('pipe', None, None, 'tensor')
- conv_bias_grad: float32 [2, 1024], P('pipe', 'tensor')
- attn_gain_grad: float32 [2, 1024], P('pipe')
- attn_shift_grad: float32 [2, 1024], P('pipe')
- ffn_gain_grad: float32 [2, 1024], P('pipe')
- ffn_shift_grad: float32 [2, 1024], P('pipe')
The draws below stay inside these ranges and needn't reach their ends.
Inputs may be any that keep to these rules, and one draw needn't show every extreme that they name: Each row of documents starts at 0, never falls from one position to the next, and holds exactly four documents.
All inputs are finite; a program needn't handle non-finite values.
Results may differ from the reference program's by a relative error of at most 0.015.
Values sent between devices are 32-bit elements; how exact they have to be, the bound alone decides.
No kernel may reach another device: no remote copies, remote signals or barrier semaphores. Data moves between devices by JAX's collectives and lax.ppermute only.
A program may use at most 256 MiB of HBM per device.

```python
import jax
import jax.numpy as jnp
from jax import lax

D = 1024
HEADS = 8
HEAD_DIM = 128
FF = 4096
SEG = 512
MEM = 512
CMEM = 512
RATE = 2
LAYERS = 2
BATCH = 16
TOKENS = 8192
COMP = 256
CTX = 1536


def one_row_documents(row_key):
    order = jax.random.permutation(row_key, CTX - 1) + 1
    cuts = order[:3].astype(jnp.int32)
    positions = jnp.arange(CTX, dtype=jnp.int32)
    return jnp.sum((positions[None, :] >= cuts[:, None]).astype(jnp.int32), axis=0).astype(jnp.int32)


def draw_documents(key, part):
    key = jax.random.fold_in(key, 11)
    row_keys = jax.random.split(key, BATCH)
    return jax.vmap(one_row_documents)(row_keys).astype(jnp.int32)


def block_scale(own_key, shape, cuts, least, high):
    factor_of, own = 1.0, jax.random.fold_in(own_key, 6)
    for dim, shards_of in cuts:
        draws = jnp.exp(jax.random.uniform(jax.random.fold_in(own, dim), (shards_of,), jnp.float32, least / len(cuts), high / len(cuts)))
        factor_of = factor_of * jnp.repeat(draws, shape[dim] // shards_of).reshape([-1 if axis == dim else 1 for axis in range(len(shape))])
    return factor_of


def normal_values(rng, shape, scale, limit, shards=(), held_as=jnp.bfloat16):
    values = jax.random.normal(rng, shape, jnp.float32) * scale
    if len(shards) > 0:
        values = block_scale(rng, shape, shards, -0.22, 0.18) * values
    return jnp.clip(values, min=-limit, max=limit).astype(held_as)


def setup_inputs(seed: int = 0) -> dict:
    streams_of = jax.random.split(jax.random.key(seed), 22)
    inputs = normal_values(streams_of[0], (TOKENS, D), 1.0, 6.0, ((0, 16),))
    memories = normal_values(streams_of[1], (LAYERS, BATCH, MEM, D), 1.0, 6.0, ((0, 2), (1, 16)))
    compressed = normal_values(streams_of[2], (LAYERS, BATCH, CMEM, D), 1.0, 6.0, ((0, 2), (1, 16)))
    documents = draw_documents(jax.random.fold_in(streams_of[21], 71), 0)
    cotangent = normal_values(streams_of[4], (TOKENS, D), 1.0, 6.0, ((0, 16),))
    compressed_cotangent = normal_values(streams_of[5], (LAYERS, BATCH, COMP, D), 1.0, 6.0, ((0, 2), (1, 16), (3, 4)))
    query_weight = normal_values(streams_of[6], (LAYERS, D, D), D ** -0.5, 0.1875, ((0, 2), (2, 4)))
    key_weight = normal_values(streams_of[7], (LAYERS, D, D), D ** -0.5, 0.1875, ((0, 2), (2, 4)))
    value_weight = normal_values(streams_of[8], (LAYERS, D, D), D ** -0.5, 0.1875, ((0, 2), (2, 4)))
    output_weight = normal_values(streams_of[9], (LAYERS, D, D), (max(D // 256, 4)) ** -0.5, 3.0, ((0, 2), (1, 4)))
    output_bias = normal_values(streams_of[10], (LAYERS, D), 0.3, 2.0, ((0, 2),))
    inner_weight = normal_values(streams_of[11], (LAYERS, D, FF), D ** -0.5, 0.1875, ((0, 2), (2, 4)))
    inner_bias = normal_values(streams_of[12], (LAYERS, FF), 0.3, 2.0, ((0, 2), (1, 4)))
    outer_weight = normal_values(streams_of[13], (LAYERS, FF, D), FF ** -0.5, 0.09375, ((0, 2), (1, 4)))
    outer_bias = normal_values(streams_of[14], (LAYERS, D), 0.3, 2.0, ((0, 2),))
    conv_weight = normal_values(streams_of[15], (LAYERS, RATE, D, D), (RATE * D) ** -0.5, 0.125, ((0, 2), (3, 4)))
    conv_bias = normal_values(streams_of[16], (LAYERS, D), 0.3, 2.0, ((0, 2), (1, 4)))
    attn_gain = jnp.clip(1.0 + 0.1 * jax.random.normal(streams_of[17], (LAYERS, D), jnp.float32), 0.5, 1.5).astype(jnp.bfloat16)
    attn_shift = normal_values(streams_of[18], (LAYERS, D), 0.3, 2.0, ((0, 2),))
    ffn_gain = jnp.clip(1.0 + 0.1 * jax.random.normal(streams_of[19], (LAYERS, D), jnp.float32), 0.5, 1.5).astype(jnp.bfloat16)
    ffn_shift = normal_values(streams_of[20], (LAYERS, D), 0.3, 2.0, ((0, 2),))
    return dict(inputs=inputs, memories=memories, compressed=compressed, documents=documents, cotangent=cotangent, compressed_cotangent=compressed_cotangent, query_weight=query_weight, key_weight=key_weight, value_weight=value_weight, output_weight=output_weight, output_bias=output_bias, inner_weight=inner_weight, inner_bias=inner_bias, outer_weight=outer_weight, outer_bias=outer_bias, conv_weight=conv_weight, conv_bias=conv_bias, attn_gain=attn_gain, attn_shift=attn_shift, ffn_gain=ffn_gain, ffn_shift=ffn_shift)


@jax.custom_vjp
def low(v):
    return lax.optimization_barrier(v.astype(jnp.bfloat16)).astype(jnp.float32)

@jax.custom_vjp
def low_back(v):
    return v

def low_keep(v):
    return (low(v), None)

def low_pass(kept, grad):
    return (grad,)

def back_keep(v):
    return (v, None)

def back_low(kept, grad):
    return (low(grad),)
low.defvjp(low_keep, low_pass)
low_back.defvjp(back_keep, back_low)

def standardize(values):
    centered = values - lax.optimization_barrier(jnp.mean(values, -1, keepdims=True))
    variance = lax.optimization_barrier(jnp.mean(centered * centered, -1, keepdims=True))
    return centered * lax.rsqrt(variance + 1e-05)

def one_layer(inputs, held_rows, documents, taken):
    highest = lax.Precision.HIGHEST
    query_w, key_w, value_w, output_w, output_b = (taken[0], taken[1], taken[2], taken[3], taken[4])
    inner_w, inner_b, outer_w, outer_b = (taken[5], taken[6], taken[7], taken[8])
    attn_g, attn_s, ffn_g, ffn_s = (taken[11], taken[12], taken[13], taken[14])
    held = CMEM + MEM
    context = jnp.concatenate([held_rows, inputs], 0)
    normed = low(standardize(context) * attn_g + attn_s)
    queries = low_back(low(jnp.dot(normed[held:], query_w, precision=highest))).reshape(SEG, HEADS, HEAD_DIM)
    keys = low_back(low(jnp.dot(normed, key_w, precision=highest))).reshape(CTX, HEADS, HEAD_DIM)
    values = low_back(low(jnp.dot(normed, value_w, precision=highest))).reshape(CTX, HEADS, HEAD_DIM)
    scores = low_back(jnp.einsum('qhe,khe->hqk', queries, keys, precision=highest) * HEAD_DIM ** (-0.5))
    positions = jnp.arange(CTX, dtype=jnp.int32)
    allowed = (positions[None, :] <= positions[held:, None]) & (documents[held:, None] == documents[None, :])
    scores = jnp.where(allowed[None], scores, -1e+30)
    probs = low(jax.nn.softmax(scores, axis=-1))
    mixed = low_back(low(jnp.einsum('hqk,khe->qhe', probs, values, precision=highest))).reshape(SEG, D)
    attended = low_back(jnp.dot(mixed, output_w, precision=highest) + output_b)
    hidden = inputs + attended
    normed_f = low(standardize(hidden) * ffn_g + ffn_s)
    pre = low_back(jnp.dot(normed_f, inner_w, precision=highest) + inner_b)
    acts = low(jax.nn.gelu(pre))
    branch = low_back(jnp.dot(acts, outer_w, precision=highest) + outer_b)
    return hidden + branch

def segment_forward(params, offsets, inputs, memory, compressed, documents):
    highest = lax.Precision.HIGHEST
    current = inputs
    outputs = []
    squeezed = []
    for layer_index in range(LAYERS):
        taken = [item[layer_index] for item in params]
        held_rows = jnp.concatenate([compressed[layer_index], memory[layer_index]], 0)
        current = one_layer(current + offsets[layer_index], held_rows, documents, taken)
        outputs.append(current)
        rows = memory[layer_index][:COMP * RATE].reshape(COMP, RATE * D)
        squeezed.append(jnp.dot(rows, taken[9].reshape(RATE * D, D), precision=highest) + taken[10])
    return (jnp.stack(outputs), jnp.stack(squeezed))

def reference(inputs, memories, compressed, documents, cotangent, compressed_cotangent, query_weight, key_weight, value_weight, output_weight, output_bias, inner_weight, inner_bias, outer_weight, outer_bias, conv_weight, conv_bias, attn_gain, attn_shift, ffn_gain, ffn_shift):
    weights = tuple((item.astype(jnp.float32) for item in (query_weight, key_weight, value_weight, output_weight, output_bias, inner_weight, inner_bias, outer_weight, outer_bias, conv_weight, conv_bias, attn_gain, attn_shift, ffn_gain, ffn_shift)))

    def per_segment(totals, index):
        seg_inputs = lax.dynamic_slice_in_dim(inputs, index * SEG, SEG, 0).astype(jnp.float32)
        seg_cot = lax.dynamic_slice_in_dim(cotangent, index * SEG, SEG, 0).astype(jnp.float32)
        seg_memory = lax.dynamic_index_in_dim(memories, index, 1, keepdims=False).astype(jnp.float32)
        seg_compressed = lax.dynamic_index_in_dim(compressed, index, 1, keepdims=False).astype(jnp.float32)
        seg_docs = lax.dynamic_index_in_dim(documents, index, 0, keepdims=False)
        squeeze_cot = lax.dynamic_index_in_dim(compressed_cotangent, index, 1, keepdims=False).astype(jnp.float32)

        def forward(params, offsets, start):
            return segment_forward(params, offsets, start, seg_memory, seg_compressed, seg_docs)
        offsets = jnp.zeros((LAYERS, SEG, D), jnp.float32)
        (hidden, squeezed), pull = jax.vjp(forward, weights, offsets, seg_inputs)
        out_cot = jnp.concatenate([jnp.zeros((LAYERS - 1, SEG, D), jnp.float32), seg_cot[None]], 0)
        param_grads, offset_grads, unused = pull((out_cot, squeeze_cot))
        totals = tuple((total + extra for total, extra in zip(totals, param_grads)))
        return (totals, (hidden, squeezed, offset_grads))
    initial = tuple((jnp.zeros_like(item) for item in weights))
    totals, (hidden, squeezed, offset_grads) = lax.scan(per_segment, initial, jnp.arange(BATCH, dtype=jnp.int32))
    hidden_states = jnp.transpose(hidden, (1, 0, 2, 3)).reshape(LAYERS, BATCH * SEG, D)
    input_grads = jnp.transpose(offset_grads, (1, 0, 2, 3)).reshape(LAYERS, BATCH * SEG, D)
    new_compressed = jnp.concatenate([compressed[:, :, COMP:].astype(jnp.float32), jnp.transpose(squeezed, (1, 0, 2, 3))], 2).astype(jnp.bfloat16)
    return (hidden_states, new_compressed, input_grads, totals[0], totals[1], totals[2], totals[3], totals[4], totals[5], totals[6], totals[7], totals[8], totals[9], totals[10], totals[11], totals[12], totals[13], totals[14])
```

```python
import jax
import jax.numpy as jnp
from jax import lax
from jax.sharding import PartitionSpec as P

HEAD_DIM = 128
SEG = 512
RATE = 2
COMP = 256
AXES = ("pipe", "dp", "tensor")


def pairs(move):
    found = []
    for p in range(2):
        for y in range(4):
            for z in range(4):
                for x in range(2):
                    for c in range(2):
                        there = move(p, y, z, x, c)
                        if there is None:
                            continue
                        q, v, w, u, d = there
                        source = ((p * 4 + y) * 4 + z) * 4 + x * 2 + c
                        target = ((q * 4 + v % 4) * 4 + w % 4) * 4 + u * 2 + d
                        found.append((source, target))
    return found


CORE = pairs(lambda p, y, z, x, c: (p, y, z, x, 1 - c))
CHIP = pairs(lambda p, y, z, x, c: (p, y, z, 1 - x, c))
ONWARD = pairs(lambda p, y, z, x, c: (1, y, z, 1 - x, c) if p == 0 else None)
BACK = pairs(lambda p, y, z, x, c: (0, y, z, 1 - x, c) if p == 1 else None)
Y_UP = pairs(lambda p, y, z, x, c: (p, y + 1, z, x, c))
Y_DOWN = pairs(lambda p, y, z, x, c: (p, y - 1, z, x, c))
Z_UP = pairs(lambda p, y, z, x, c: (p, y, z + 1, x, c))
Z_DOWN = pairs(lambda p, y, z, x, c: (p, y, z - 1, x, c))
Y_ONE = pairs(lambda p, y, z, x, c: (p, y ^ 1, z, x, c))
Y_TWO = pairs(lambda p, y, z, x, c: (p, y ^ 2, z, x, c))
Z_ONE = pairs(lambda p, y, z, x, c: (p, y, z ^ 1, x, c))
Z_TWO = pairs(lambda p, y, z, x, c: (p, y, z ^ 2, x, c))


def send(value, moves):
    return lax.ppermute(value, AXES, moves)


def rows(value, start, size):
    return lax.dynamic_slice_in_dim(value, start, size, 0)


def part(value, index):
    return lax.dynamic_index_in_dim(value, index % 4, 0, keepdims=False)


def dot(left, right):
    return jnp.dot(left, right, preferred_element_type=jnp.float32)


def dot_t(left, right):
    return lax.dot_general(
        left, right, (((1,), (1,)), ((), ())), preferred_element_type=jnp.float32
    )


def t_dot(left, right):
    return lax.dot_general(
        left, right, (((0,), (0,)), ((), ())), preferred_element_type=jnp.float32
    )


def low(value):
    return value.astype(jnp.bfloat16)


def wide(value):
    return value.astype(jnp.float32)


def standardize(values):
    centered = values - jnp.mean(values, -1, keepdims=True)
    variance = jnp.mean(centered * centered, -1, keepdims=True)
    inverse = lax.rsqrt(variance + 1e-05)
    return centered * inverse, inverse


def standardize_back(grad, hat, inverse):
    return inverse * (
        grad
        - jnp.mean(grad, -1, keepdims=True)
        - hat * jnp.mean(grad * hat, -1, keepdims=True)
    )


def in_order(first, second, swap):
    return jnp.where(
        swap, jnp.concatenate([second, first], 0), jnp.concatenate([first, second], 0)
    )


def chip_sum(value, core):
    half = value.shape[0] // 2
    return rows(value, core * half, half) + send(rows(value, (1 - core) * half, half), CORE)


def whole_rows(half, core):
    return in_order(half, send(half, CORE), core == 1)


def tensor_sum(value, core):
    half = chip_sum(value, core)
    return whole_rows(half + send(half, CHIP), core)


def quarter_sum(value, core, place):
    half = chip_sum(value, core)
    size = half.shape[0] // 2
    return rows(half, place * size, size) + send(rows(half, (1 - place) * size, size), CHIP)


def scatter_ring(value, me, up, down):
    far = part(value, me + 2)
    cut = far.shape[0] // 2
    from_down, from_up = send(far[:cut], up), send(far[cut:], down)
    above, below = part(value, me + 1), part(value, me + 3)
    above = jnp.concatenate([above[:cut] + from_down, above[cut:]], 0)
    below = jnp.concatenate([below[:cut], below[cut:] + from_up], 0)
    return part(value, me) + send(above, up) + send(below, down)


def gather_ring(value, up, down):
    below, above = send(value, up), send(value, down)
    cut = value.shape[0] // 2
    far = jnp.concatenate([send(below[:cut], up), send(above[cut:], down)], 0)
    return jnp.stack([value, above, far, below])


def ring_sum(value, first, second):
    shape = value.shape
    here, up, down = first
    there, up2, down2 = second
    total = value.reshape(4, 4, shape[0] // 16, shape[1])
    total = scatter_ring(total, here, up, down)
    total = scatter_ring(total, there, up2, down2)
    total = gather_ring(total, up2, down2)
    total = gather_ring(total, up, down)
    return jnp.roll(total, (here, there), (0, 1)).reshape(shape)


def body(
    inputs,
    memories,
    compressed,
    documents,
    cotangent,
    compressed_cotangent,
    query_weight,
    key_weight,
    value_weight,
    output_weight,
    output_bias,
    inner_weight,
    inner_bias,
    outer_weight,
    outer_bias,
    conv_weight,
    conv_bias,
    attn_gain,
    attn_shift,
    ffn_gain,
    ffn_shift,
):
    section = lax.axis_index("pipe")
    group = lax.axis_index("dp")
    member = lax.axis_index("tensor")
    core, chip = member % 2, member // 2
    y_axis = (group // 4, Y_UP, Y_DOWN)
    z_axis = (group % 4, Z_UP, Z_DOWN)
    context = documents.shape[1]
    width = inputs.shape[1]
    local = query_weight.shape[2]
    heads = local // HEAD_DIM
    held = context - SEG
    quarter = SEG // 4
    scale = HEAD_DIM ** (-0.5)
    query_w, key_w, value_w, output_w = (
        query_weight[0],
        key_weight[0],
        value_weight[0],
        output_weight[0],
    )
    inner_w, outer_w = inner_weight[0], outer_weight[0]
    output_b, inner_b, outer_b = wide(output_bias[0]), wide(inner_bias[0]), wide(outer_bias[0])
    gain_a, shift_a = wide(attn_gain[0]), wide(attn_shift[0])
    gain_f, shift_f = wide(ffn_gain[0]), wide(ffn_shift[0])
    first = section == 0

    memory, older = memories[0, 0], compressed[0, 0]
    squeeze_rows = memory.reshape(COMP, RATE * width)
    squeeze_cot = compressed_cotangent[0, 0]
    conv_g = t_dot(squeeze_rows, squeeze_cot).reshape(RATE, width, local)
    conv_g = lax.psum(conv_g, "dp")
    conv_bg = jnp.sum(wide(squeeze_cot), 0)
    squeezed = dot(squeeze_rows, conv_weight[0].reshape(RATE * width, local)) + wide(conv_bias[0])
    kept_old = lax.dynamic_slice_in_dim(older[COMP:], member * local, local, 1)
    new_compressed = jnp.concatenate([kept_old, low(squeezed)], 0)

    memory_hat, _ = standardize(wide(jnp.concatenate([older, memory], 0)))
    memory_low = low(memory_hat * gain_a + shift_a)
    memory_keys = low(dot(memory_low, key_w))
    memory_values = low(dot(memory_low, value_w))
    positions = jnp.arange(context, dtype=jnp.int32)
    allowed = (positions[None, :] <= positions[held:, None]) & (
        documents[0, held:, None] == documents[0, None, :]
    )

    def head(value, index):
        return value[:, index * HEAD_DIM : (index + 1) * HEAD_DIM]

    def attend(layer_input):
        hat, inverse = standardize(layer_input)
        normed = low(hat * gain_a + shift_a)
        queries = low(dot(normed, query_w))
        keys = jnp.concatenate([memory_keys, low(dot(normed, key_w))], 0)
        values = jnp.concatenate([memory_values, low(dot(normed, value_w))], 0)
        mixed, probs = [], []
        for index in range(heads):
            scores = dot_t(head(queries, index), head(keys, index)) * scale
            scores = jnp.where(allowed, scores, -1e30)
            exps = jnp.exp(scores - jnp.max(scores, -1, keepdims=True))
            probs.append(exps / jnp.sum(exps, -1, keepdims=True))
            mixed.append(low(dot(low(probs[-1]), head(values, index))))
        mixed = jnp.concatenate(mixed, 1)
        attended = tensor_sum(dot(mixed, output_w), core) + output_b
        hidden = layer_input + attended
        return hidden, (hat, inverse, normed, queries, keys, values, probs, mixed)

    def feed(hidden):
        hat, inverse = standardize(hidden)
        normed = low(hat * gain_f + shift_f)
        pre = dot(normed, inner_w) + inner_b
        acts = low(jax.nn.gelu(pre))
        return dot(acts, outer_w), (hat, inverse, normed, pre, acts)

    def feed_back(grad_out, kept):
        hat, inverse, normed, pre, acts = kept
        branch_grad = low(grad_out)
        unused, pull = jax.vjp(jax.nn.gelu, pre)
        pre_grad = low(pull(dot_t(branch_grad, outer_w))[0])
        normed_part = dot_t(pre_grad, inner_w)
        normed_grad = tensor_sum(normed_part, core)
        hidden_grad = grad_out + standardize_back(normed_grad * gain_f, hat, inverse)
        return hidden_grad, (branch_grad, pre_grad, normed_part)

    def attend_back(hidden_grad, kept):
        hat, inverse, normed, queries, keys, values, probs, mixed = kept
        attend_grad = low(hidden_grad)
        mixed_grad = low(dot_t(attend_grad, output_w))
        query_rows, key_rows, value_rows = [], [], []
        for index in range(heads):
            probs_grad = dot_t(head(mixed_grad, index), head(values, index))
            inner = jnp.sum(probs[index] * probs_grad, -1, keepdims=True)
            score_grad = low(probs[index] * (probs_grad - inner))
            query_rows.append(low(dot(score_grad, head(keys, index)) * scale))
            key_rows.append(low(t_dot(score_grad, head(queries, index)) * scale))
            value_rows.append(low(t_dot(low(probs[index]), head(mixed_grad, index))))
        query_rows = jnp.concatenate(query_rows, 1)
        key_rows = jnp.concatenate(key_rows, 1)
        value_rows = jnp.concatenate(value_rows, 1)
        normed_part = (
            dot_t(query_rows, query_w)
            + dot_t(key_rows[held:], key_w)
            + dot_t(value_rows[held:], value_w)
        )
        return normed_part, (attend_grad, query_rows, key_rows, value_rows)

    def pass_on(total, moves, receives, place):
        piece = jnp.where(receives, send(total, moves), total)
        half = in_order(piece, send(piece, CHIP), place == 1)
        return whole_rows(half, core)

    seg_inputs, seg_cot = wide(inputs), wide(cotangent)

    place = jnp.where(first, chip, 1 - chip)
    hidden, kept_a = attend(seg_inputs)
    branch, kept_f = feed(hidden)
    total = quarter_sum(branch, core, place) + outer_b
    total = total + rows(hidden, core * 2 * quarter + place * quarter, quarter)
    forward = pass_on(total, ONWARD, section == 1, place)

    layer_input = jnp.where(first, seg_inputs, forward)
    hidden, kept_a = attend(layer_input)
    branch, kept_f = feed(hidden)
    last_out = hidden + tensor_sum(branch, core) + outer_b
    layer_out = jnp.where(first, forward, last_out)

    hat_a, inverse_a = kept_a[0], kept_a[1]
    place = jnp.where(first, 1 - chip, chip)
    hidden_grad, kept_b = feed_back(seg_cot, kept_f)
    normed_part, kept_c = attend_back(hidden_grad, kept_a)
    total = quarter_sum(normed_part, core, place) * gain_a
    spot = core * 2 * quarter + place * quarter
    total = standardize_back(total, rows(hat_a, spot, quarter), rows(inverse_a, spot, quarter))
    total = total + rows(hidden_grad, spot, quarter)
    backward = pass_on(total, BACK, first, place)

    grad_out = jnp.where(first, backward, seg_cot)
    hidden_grad, (branch_grad, pre_grad, normed_f_part) = feed_back(grad_out, kept_f)
    hat_f, inverse_f, normed_f, pre, acts = kept_f
    outer_g = t_dot(acts, branch_grad)
    inner_g = t_dot(normed_f, pre_grad)
    normed_part, kept_c = attend_back(hidden_grad, kept_a)
    attend_grad, query_rows, key_rows, value_rows = kept_c
    total = hidden_grad + standardize_back(tensor_sum(normed_part, core) * gain_a, hat_a, inverse_a)
    input_grads = jnp.where(first, total, backward)

    normed, mixed = kept_a[2], kept_a[7]
    all_normed = jnp.concatenate([memory_low, normed], 0)
    query_g = t_dot(normed, query_rows)
    key_g = t_dot(all_normed, key_rows)
    value_g = t_dot(all_normed, value_rows)
    output_g = t_dot(mixed, attend_grad)
    memory_part = dot_t(key_rows[:held], key_w) + dot_t(value_rows[:held], value_w)

    small = jnp.stack(
        [
            jnp.sum(memory_part * memory_hat, 0) + jnp.sum(normed_part * hat_a, 0),
            jnp.sum(memory_part, 0) + jnp.sum(normed_part, 0),
            jnp.sum(normed_f_part * hat_f, 0),
            jnp.sum(normed_f_part, 0),
        ]
    )
    small = small + send(small, CORE)
    small = small + send(small, CHIP)
    own = jnp.stack(
        [
            jnp.sum(wide(attend_grad), 0),
            jnp.sum(wide(branch_grad), 0),
            jnp.sum(wide(pre_grad), 0),
            jnp.pad(conv_bg, (0, width - local)),
        ]
    )
    small = jnp.concatenate([small, own], 0)
    for moves in (Y_ONE, Y_TWO, Z_ONE, Z_TWO):
        small = small + send(small, moves)

    outer_g = ring_sum(outer_g, y_axis, z_axis)
    inner_g = ring_sum(inner_g, z_axis, y_axis)
    left = jnp.concatenate([query_g, key_g], 1)
    left = ring_sum(left, y_axis, z_axis)
    query_g, key_g = left[:, :local], left[:, local:]
    right = jnp.concatenate([value_g.reshape(local, width), output_g], 0)
    right = ring_sum(right, z_axis, y_axis)
    value_g, output_g = right[:local].reshape(width, local), right[local:]
    return (
        layer_out[None],
        new_compressed[None, None],
        input_grads[None],
        query_g[None],
        key_g[None],
        value_g[None],
        output_g[None],
        small[4][None],
        inner_g[None],
        small[6][None],
        outer_g[None],
        small[5][None],
        conv_g[None],
        small[7, :local][None],
        small[0][None],
        small[1][None],
        small[2][None],
        small[3][None],
    )


def solution(mesh):
    return jax.shard_map(
        body,
        mesh=mesh,
        in_specs=(
            P("dp", None),
            P("pipe", "dp", None, None),
            P("pipe", "dp", None, None),
            P("dp", None),
            P("dp", None),
            P("pipe", "dp", None, "tensor"),
            P("pipe", None, "tensor"),
            P("pipe", None, "tensor"),
            P("pipe", None, "tensor"),
            P("pipe", "tensor", None),
            P("pipe", None),
            P("pipe", None, "tensor"),
            P("pipe", "tensor"),
            P("pipe", "tensor", None),
            P("pipe", None),
            P("pipe", None, None, "tensor"),
            P("pipe", "tensor"),
            P("pipe", None),
            P("pipe", None),
            P("pipe", None),
            P("pipe", None),
        ),
        out_specs=(
            P("pipe", "dp", None),
            P("pipe", "dp", None, "tensor"),
            P("pipe", "dp", None),
            P("pipe", None, "tensor"),
            P("pipe", None, "tensor"),
            P("pipe", None, "tensor"),
            P("pipe", "tensor", None),
            P("pipe", None),
            P("pipe", None, "tensor"),
            P("pipe", "tensor"),
            P("pipe", "tensor", None),
            P("pipe", None),
            P("pipe", None, None, "tensor"),
            P("pipe", "tensor"),
            P("pipe", None),
            P("pipe", None),
            P("pipe", None),
            P("pipe", None),
        ),
        check_vma=False,
    )
```

```python
import jax
import jax.numpy as jnp
from jax import lax
from jax.experimental import pallas as pl
from jax.experimental.pallas import tpu as pltpu
from jax.sharding import PartitionSpec as P

HEAD_DIM = 128
SEG = 512
RATE = 2
COMP = 256
CHUNK = 256
HALF = 128
QUARTER = 64
TILE = 256
BLOCK = 256
SUB = 64
HEADS = 2
SCALE = HEAD_DIM ** (-0.5)
LIMIT = 10 * 2**20
AXES = ("pipe", "dp", "tensor")


def pairs(move):
    found = []
    for p in range(2):
        for y in range(4):
            for z in range(4):
                for x in range(2):
                    for c in range(2):
                        there = move(p, y, z, x, c)
                        if there is None:
                            continue
                        q, v, w, u, d = there
                        source = ((p * 4 + y) * 4 + z) * 4 + x * 2 + c
                        target = ((q * 4 + v % 4) * 4 + w % 4) * 4 + u * 2 + d
                        found.append((source, target))
    return found


CORE = pairs(lambda p, y, z, x, c: (p, y, z, x, 1 - c))
CHIP = pairs(lambda p, y, z, x, c: (p, y, z, 1 - x, c))
CORE_FIRST = pairs(lambda p, y, z, x, c: (p, y, z, x, 1 - c) if p == 0 else None)
CHIP_FIRST = pairs(lambda p, y, z, x, c: (p, y, z, 1 - x, c) if p == 0 else None)
CORE_LAST = pairs(lambda p, y, z, x, c: (p, y, z, x, 1 - c) if p == 1 else None)
CHIP_LAST = pairs(lambda p, y, z, x, c: (p, y, z, 1 - x, c) if p == 1 else None)
ONWARD = pairs(lambda p, y, z, x, c: (1, y, z, 1 - x, c) if p == 0 else None)
BACK = pairs(lambda p, y, z, x, c: (0, y, z, 1 - x, c) if p == 1 else None)
Y_ONE = pairs(lambda p, y, z, x, c: (p, y ^ 1, z, x, c))
Y_TWO = pairs(lambda p, y, z, x, c: (p, y ^ 2, z, x, c))
Z_ONE = pairs(lambda p, y, z, x, c: (p, y, z ^ 1, x, c))
Z_TWO = pairs(lambda p, y, z, x, c: (p, y, z ^ 2, x, c))
UP = pairs(lambda p, y, z, x, c: (p, y + 1 - c, z + c, x, c))
DOWN = pairs(lambda p, y, z, x, c: (p, y + 3 * (1 - c), z + 3 * c, x, c))
UP2 = pairs(lambda p, y, z, x, c: (p, y + c, z + 1 - c, x, c))
DOWN2 = pairs(lambda p, y, z, x, c: (p, y + 3 * c, z + 3 * (1 - c), x, c))


def low(value):
    return value.astype(jnp.bfloat16)


def wide(value):
    return value.astype(jnp.float32)


def send(value, moves):
    return lax.ppermute(value, AXES, moves)


def after(value, anchor):
    return lax.optimization_barrier((value, anchor))[0]


def dot(left, right):
    return jnp.dot(left, right, preferred_element_type=jnp.float32)


def dot_t(left, right):
    return lax.dot_general(
        left, right, (((1,), (1,)), ((), ())), preferred_element_type=jnp.float32
    )


def t_dot(left, right):
    return lax.dot_general(
        left, right, (((0,), (0,)), ((), ())), preferred_element_type=jnp.float32
    )


def standardize(values):
    centered = values - jnp.mean(values, -1, keepdims=True)
    variance = jnp.mean(centered * centered, -1, keepdims=True)
    inverse = lax.rsqrt(variance + 1e-05)
    return centered * inverse, inverse


def standardize_back(grad, hat, inverse):
    return inverse * (
        grad
        - jnp.mean(grad, -1, keepdims=True)
        - hat * jnp.mean(grad * hat, -1, keepdims=True)
    )


def gelu_and_slope(value):
    square = value * value
    curve = jnp.tanh(0.7978845608028654 * value * (1.0 + 0.044715 * square))
    up = 0.5 + 0.5 * curve
    slope = up + (0.5 * value) * (1.0 - curve * curve) * (
        0.7978845608028654 + (3 * 0.044715 * 0.7978845608028654) * square
    )
    return value * up, slope


F32, BF16 = jnp.float32, jnp.bfloat16
WHOLE = pl.BlockSpec(memory_space=pltpu.VMEM)
SCALAR = pl.BlockSpec(memory_space=pltpu.SMEM)
ANYWHERE = pl.BlockSpec(memory_space=pl.ANY)
OUTSIDE = pl.BlockSpec(memory_space=pltpu.HBM)
CORE_AT, ON_AT, BACK_AT, FIRST_AT, RING_AT, RING2_AT, MEMBER_AT = range(7)


class Order:
    def __init__(self, flags):
        self.flags = flags

    def then(self, anchor):
        self.flags = after(self.flags, anchor)

    def call(self, kernel, outs, args, flops=1, scratch=(), specs=None, out_specs=None, aliases=None):
        args = [self.flags, *args]
        results = pl.pallas_call(
            kernel,
            out_shape=[jax.ShapeDtypeStruct(shape, dtype) for shape, dtype in outs],
            in_specs=[SCALAR] + (specs or [WHOLE] * (len(args) - 1)),
            out_specs=out_specs or [WHOLE] * len(outs),
            scratch_shapes=list(scratch),
            input_output_aliases=aliases or {},
            compiler_params=pltpu.CompilerParams(vmem_limit_bytes=LIMIT),
            cost_estimate=pl.CostEstimate(flops=1, bytes_accessed=1, transcendentals=0),
        )(*args)
        self.then(results[0])
        return results


def at_rows(index, size):
    return pl.ds(pl.multiple_of(index * size, size), size)


def put_pieces(out_ref, pieces, core, place, start=0):
    spots = (
        core * 2 + place,
        core * 2 + 1 - place,
        (1 - core) * 2 + place,
        (1 - core) * 2 + 1 - place,
    )
    for piece, spot in zip(pieces, spots):
        out_ref[at_rows(spot + start // QUARTER, QUARTER), :] = piece[...]


def halves_of(width):
    return [((HALF, width), F32)] + [((QUARTER, width), F32)] * 2


def split_halves(value_ref, own_ref, send_refs, core):
    own_ref[...] = value_ref[at_rows(core, HALF), :]
    for i, ref in enumerate(send_refs):
        ref[...] = value_ref[at_rows(2 * (1 - core) + i, QUARTER), :]


def put_halves(out_ref, own, others, core):
    out_ref[at_rows(core, HALF), :] = own[...]
    for i, ref in enumerate(others):
        out_ref[at_rows(2 * (1 - core) + i, QUARTER), :] = ref[...]


def chunk_rows(index):
    return slice(index * CHUNK, (index + 1) * CHUNK)


def row_documents(docs, start):
    row = lax.broadcasted_iota(jnp.int32, (CHUNK, CHUNK), 0)
    col = lax.broadcasted_iota(jnp.int32, (CHUNK, CHUNK), 1)
    own = wide(docs[:, start : start + CHUNK])
    return jnp.sum(jnp.where(row == col, own, 0.0), -1, keepdims=True)


def masked(scores, docs_q, docs_k, causal):
    allowed = docs_q == docs_k
    if causal:
        q_pos = lax.broadcasted_iota(jnp.int32, scores.shape, 0)
        k_pos = lax.broadcasted_iota(jnp.int32, scores.shape, 1)
        allowed = allowed & (k_pos <= q_pos)
    return jnp.where(allowed, scores * SCALE, -1e30)


def prepare_memory(order, older, memory, gain, shift, key_w, value_w):
    held, width = older.shape[0] + memory.shape[0], older.shape[1]
    local = key_w.shape[1]
    pieces = range(0, held, CHUNK)

    def kernel(flag, older_ref, memory_ref, *refs):
        outside, (normed, k, v), refs = refs[:4], refs[4:7], refs[7:]
        gain_ref, shift_ref, wk, wv, rows_ref, sems = refs
        copies = [
            pltpu.make_async_copy(source, target, sems.at[i])
            for i, (source, target) in enumerate(zip(outside, (gain_ref, shift_ref, wk, wv)))
        ]
        for start in pieces:
            source = older_ref if start < older.shape[0] else memory_ref
            at = start % older.shape[0]
            copies.append(
                pltpu.make_async_copy(
                    source.at[at : at + CHUNK, :],
                    rows_ref.at[start : start + CHUNK, :],
                    sems.at[len(copies)],
                )
            )
        for copy in copies:
            copy.start()
        copies[0].wait()
        copies[1].wait()
        gain_row, shift_row = wide(gain_ref[...]), wide(shift_ref[...])
        for i, start in enumerate(pieces):
            copies[4 + i].wait()
            at = slice(start, start + CHUNK)
            hat, _ = standardize(wide(rows_ref[at, :]))
            normed[at, :] = low(hat * gain_row + shift_row)
            if i == 0:
                copies[2].wait()
                copies[3].wait()
            k[at, :] = low(dot(normed[at, :], wk[...]))
            v[at, :] = low(dot(normed[at, :], wv[...]))

    outs = [((held, width), BF16), ((held, local), BF16), ((held, local), BF16)]
    args = [older, memory, gain, shift, key_w, value_w]
    scratch = [pltpu.VMEM(a.shape, BF16) for a in args[2:]]
    scratch += [pltpu.VMEM((held, width), BF16), pltpu.SemaphoreType.DMA((4 + len(pieces),))]
    return order.call(kernel, outs, args, 1, scratch, specs=[OUTSIDE] * len(args))


def attend_chunk(order, inputs, pieces, past, docs, index, weights, gain, shift, output_w, keep):
    given, held = len(pieces), [k.shape[0] for k, _ in past]
    starts = [sum(held[:i]) for i in range(len(held) + 1)]

    def kernel(*refs):
        flag, x_in = refs[0], refs[1]
        piece_refs, rest = refs[2 : 2 + given], refs[2 + given :]
        gain_ref, shift_ref, wq, wk, wv, docs_ref, wo = rest[:7]
        past_refs, rest = rest[7 : 7 + 2 * len(held)], rest[7 + 2 * len(held) :]
        if keep:
            x, k, v, own, *others, hat, inverse, normed, q, lse, mixed, acc = rest
        else:
            x, k, v, own, *others, normed, q, mixed, acc = rest
        if given:
            put_pieces(x, piece_refs, flag[CORE_AT], flag[ON_AT])
            x[...] = jnp.where(flag[FIRST_AT] == 1, wide(x_in[chunk_rows(index), :]), x[...])
        else:
            x[...] = wide(x_in[chunk_rows(index), :])
        hat_value, inverse_value = standardize(x[...])
        normed[...] = low(hat_value * wide(gain_ref[...]) + wide(shift_ref[...]))
        if keep:
            hat[...], inverse[...] = hat_value, inverse_value
        q[...] = low(dot(normed[...], wq[...]))
        k[...] = low(dot(normed[...], wk[...]))
        v[...] = low(dot(normed[...], wv[...]))
        parts = [(past_refs[2 * i], past_refs[2 * i + 1]) for i in range(len(held))] + [(k, v)]
        sizes = held + [CHUNK]
        docs_q = row_documents(docs_ref, starts[-1])
        for h in range(HEADS):
            cols = slice(h * HEAD_DIM, (h + 1) * HEAD_DIM)
            scores = [
                masked(
                    dot_t(q[:, cols], key[:, cols]),
                    docs_q,
                    wide(docs_ref[:, start : start + size]),
                    key is k,
                )
                for (key, _), start, size in zip(parts, starts, sizes)
            ]
            top = scores[0].max(-1, keepdims=True)
            for score in scores[1:]:
                top = jnp.maximum(top, score.max(-1, keepdims=True))
            total, out = 0.0, 0.0
            for score, (_, value) in zip(scores, parts):
                exps = jnp.exp(score - top)
                total = total + exps.sum(-1, keepdims=True)
                out = out + dot(low(exps), value[:, cols])
            if keep:
                lse[:, h : h + 1] = top + jnp.log(total)
            mixed[:, cols] = low(out / total)
        acc[...] = dot(mixed[...], wo[...])
        split_halves(acc, own, others, flag[CORE_AT])

    width, local = inputs.shape[1], weights[0].shape[1]
    size = starts[-1] + CHUNK
    outs = [((CHUNK, width), F32), ((CHUNK, local), BF16), ((CHUNK, local), BF16)]
    outs += halves_of(width)
    kept = [
        ((CHUNK, width), F32),
        ((CHUNK, 1), F32),
        ((CHUNK, width), BF16),
        ((CHUNK, local), BF16),
        ((CHUNK, HEADS), F32),
        ((CHUNK, local), BF16),
    ]
    if keep:
        outs, scratch = outs + kept, []
    else:
        scratch = [pltpu.VMEM(*kept[i]) for i in (2, 3, 5)]
    args = [inputs, *pieces, gain, shift, *weights, docs, output_w]
    args += [item for pair in past for item in pair]
    return order.call(kernel, outs, args, 1, scratch + [pltpu.VMEM((CHUNK, width), F32)])


def feed_chunk(order, layer_input, parts, output_b, gain, shift, inner_w, inner_b, outer_w):
    ending = outer_w is not None
    units = inner_w.shape[1]

    def kernel(flag, x, half, twin0, twin1, bo, gain_ref, shift_ref, wi, bi, *rest):
        if ending:
            wf, hidden, own, *others, acc = rest
        else:
            hidden, hat_ref, inverse_ref, normed_ref, acts_ref, slope_ref = rest
        put_halves(hidden, half, (twin0, twin1), flag[CORE_AT])
        hidden[...] = x[...] + (hidden[...] + wide(bo[...]))
        hat, inverse = standardize(hidden[...])
        normed = low(hat * wide(gain_ref[...]) + wide(shift_ref[...]))
        if not ending:
            hat_ref[...], inverse_ref[...], normed_ref[...] = hat, inverse, normed
        for start in range(0, units, TILE):
            tile = slice(start, start + TILE)
            acts, slope = gelu_and_slope(dot(normed, wi[:, tile]) + wide(bi[:, tile]))
            if ending:
                term = dot(low(acts), wf[tile, :])
                acc[...] = term if start == 0 else acc[...] + term
            else:
                acts_ref[:, tile] = low(acts)
                slope_ref[:, tile] = slope
        if ending:
            split_halves(acc, own, others, flag[CORE_AT])

    width = layer_input.shape[1]
    outs = [((CHUNK, width), F32)]
    if ending:
        outs += halves_of(width)
    else:
        outs += [
            ((CHUNK, width), F32),
            ((CHUNK, 1), F32),
            ((CHUNK, width), BF16),
            ((CHUNK, units), BF16),
            ((CHUNK, units), F32),
        ]
    args = [layer_input, *parts, output_b, gain, shift, inner_w, inner_b]
    args += [outer_w] if ending else []
    scratch = [pltpu.VMEM((CHUNK, width), F32)] if ending else []
    return order.call(kernel, outs, args, 1, scratch)


def feed_back_chunk(order, cotangent, index, pieces, kept, outer_w, inner_w, final):
    hat, slope = kept
    given, units = len(pieces), outer_w.shape[0]

    def kernel(*refs):
        flag, cot = refs[0], refs[1]
        piece_refs, rest = refs[2 : 2 + given], refs[2 + given :]
        slope_ref, wf, wi = rest[:3]
        if final:
            hat_ref, grad_out, own, *others, branch, pre_grad, sums, acc = rest[3:]
        else:
            grad_out, own, *others, acc = rest[3:]
        own_cot = wide(cot[chunk_rows(index), :])
        if given:
            put_pieces(grad_out, piece_refs, flag[CORE_AT], flag[BACK_AT])
            grad_out[...] = jnp.where(flag[FIRST_AT] == 1, grad_out[...], own_cot)
        else:
            grad_out[...] = own_cot
        branch_grad = low(grad_out[...])
        for start in range(0, units, TILE):
            tile = slice(start, start + TILE)
            grad = low(slope_ref[:, tile] * dot_t(branch_grad, wf[tile, :]))
            if final:
                pre_grad[:, tile] = grad
                sums[3:4, tile] = jnp.sum(wide(grad), 0, keepdims=True)
            term = dot_t(grad, wi[:, tile])
            acc[...] = term if start == 0 else acc[...] + term
        split_halves(acc, own, others, flag[CORE_AT])
        if final:
            branch[...] = branch_grad
            sums[0:1, :] = jnp.sum(acc[...] * hat_ref[...], 0, keepdims=True)
            sums[1:2, :] = jnp.sum(acc[...], 0, keepdims=True)
            sums[2:3, :] = jnp.sum(wide(branch_grad), 0, keepdims=True)

    width = cotangent.shape[1]
    outs = [((CHUNK, width), F32)] + halves_of(width)
    args = [cotangent, *pieces, slope, outer_w, inner_w]
    if final:
        outs += [((CHUNK, width), BF16), ((CHUNK, units), BF16), ((4, width), F32)]
        args += [hat]
    flops = 4 * CHUNK * width * units
    return order.call(kernel, outs, args, flops, [pltpu.VMEM((CHUNK, width), F32)])


def attend_back_chunk(
    order, grad_out, parts, kept_f, kept_a, past, docs, weights, gain_f, later, final
):
    hat_f, inverse_f = kept_f
    hat, queries, keys, values, lse = kept_a
    held = [k.shape[0] for k, _ in past]
    starts = [sum(held[:i]) for i in range(len(held) + 1)]
    sizes = held + [CHUNK]
    last = len(held) > 1
    width, local = hat.shape[1], queries.shape[1]
    size = starts[-1] + CHUNK

    def kernel(*refs):
        refs = list(refs)

        def take(count):
            taken = refs[:count]
            del refs[:count]
            return taken

        flag, g_out, half, twin0, twin1, hf, invf, gf, wo, wq, wk, wv, docs_ref = take(13)
        q, k, v, lse_ref = take(4)
        past_refs = take(2 * len(held))
        later_refs = take(len(later))
        hat_ref = take(1)[0] if final else None
        hidden_grad, own, *others = take(4)
        passed = take(2) if last else []
        kept = take(7) if final else []
        acc, key_acc, value_acc = take(3)
        core = flag[CORE_AT]
        put_halves(acc, half, (twin0, twin1), core)
        grad = standardize_back(acc[...] * wide(gf[...]), hf[...], invf[...])
        hidden_grad[...] = g_out[...] + grad
        attend_grad = low(hidden_grad[...])
        mixed_grad = low(dot_t(attend_grad, wo[...]))
        parts = [(past_refs[2 * i], past_refs[2 * i + 1]) for i in range(len(held))] + [(k, v)]
        query_rows = []
        docs_q = row_documents(docs_ref, starts[-1])
        for h in range(HEADS):
            cols = slice(h * HEAD_DIM, (h + 1) * HEAD_DIM)
            grad = mixed_grad[:, cols]
            probs, probs_grads, inner = [], [], 0.0
            for (key, value), start, length in zip(parts, starts, sizes):
                score = masked(
                    dot_t(q[:, cols], key[:, cols]),
                    docs_q,
                    wide(docs_ref[:, start : start + length]),
                    key is k,
                )
                probs.append(jnp.exp(score - lse_ref[:, h : h + 1]))
                probs_grads.append(dot_t(grad, value[:, cols]))
                inner = inner + jnp.sum(probs[-1] * probs_grads[-1], -1, keepdims=True)
            query_row = 0.0
            for i, (key, value) in enumerate(parts):
                score_grad = low(probs[i] * (probs_grads[i] - inner))
                query_row = query_row + dot(score_grad, key[:, cols])
                if i == 0 and not final:
                    continue
                key_sum = t_dot(score_grad, q[:, cols])
                value_sum = t_dot(low(probs[i]), grad)
                key_acc[starts[i] : starts[i] + sizes[i], cols] = key_sum
                value_acc[starts[i] : starts[i] + sizes[i], cols] = value_sum
            query_rows.append(low(query_row * SCALE))
        query_rows = jnp.concatenate(query_rows, 1)
        key_own, value_own = key_acc[starts[-1] : size, :], value_acc[starts[-1] : size, :]
        if last:
            passed[0][...] = key_acc[starts[1] : starts[2], :]
            passed[1][...] = value_acc[starts[1] : starts[2], :]
        else:
            key_own, value_own = key_own + later_refs[0][...], value_own + later_refs[1][...]
        key_rows, value_rows = low(key_own * SCALE), low(value_own)
        acc[...] = dot_t(query_rows, wq[...]) + dot_t(key_rows, wk[...])
        acc[...] = acc[...] + dot_t(value_rows, wv[...])
        split_halves(acc, own, others, core)
        if final:
            kept[0][...], kept[1][...] = query_rows, key_rows
            kept[2][...], kept[3][...] = value_rows, attend_grad
            memory_key, memory_value = key_acc[: held[0], :], value_acc[: held[0], :]
            if last:
                kept[4][...], kept[5][...] = memory_key, memory_value
            else:
                kept[4][...] = low((memory_key + later_refs[2][...]) * SCALE)
                kept[5][...] = low(memory_value + later_refs[3][...])
            sums = kept[6]
            sums[0:1, :] = jnp.sum(acc[...] * hat_ref[...], 0, keepdims=True)
            sums[1:2, :] = jnp.sum(acc[...], 0, keepdims=True)
            sums[2:3, :] = jnp.sum(wide(attend_grad), 0, keepdims=True)
            sums[3:4, :] = jnp.zeros_like(sums[3:4, :])

    outs = [((CHUNK, width), F32)] + halves_of(width)
    if last:
        outs += [((CHUNK, local), F32)] * 2
    if final:
        outs += [((CHUNK, local), BF16)] * 3 + [((CHUNK, width), BF16)]
        outs += [((held[0], local), F32 if last else BF16)] * 2 + [((4, width), F32)]
    args = [grad_out, *parts, hat_f, inverse_f, gain_f, *weights, docs]
    args += [queries, keys, values, lse] + [item for pair in past for item in pair] + list(later)
    args += [hat] if final else []
    scratch = [
        pltpu.VMEM((CHUNK, width), F32),
        pltpu.VMEM((size, local), F32),
        pltpu.VMEM((size, local), F32),
    ]
    flops = 2 * CHUNK * local * (4 * width + 5 * size)
    return order.call(kernel, outs, args, flops, scratch)


def add(order, *terms):
    def kernel(flag, *refs):
        total = refs[0][...]
        for ref in refs[1:-1]:
            total = total + ref[...]
        refs[-1][...] = total

    return order.call(kernel, [(terms[0].shape, F32)], terms)[0]


def add_pieces(order, own, pieces):
    def kernel(flag, a, b0, b1, out):
        out[:QUARTER, :] = a[:QUARTER, :] + b0[...]
        out[QUARTER:, :] = a[QUARTER:, :] + b1[...]

    return order.call(kernel, [(own.shape, F32)], [own, *pieces])[0]


def add_into_pieces(order, own, arrived):
    def kernel(flag, a, b, out, first, second):
        out[...] = a[...] + b[...]
        first[...], second[...] = out[:QUARTER, :], out[QUARTER:, :]

    return order.call(kernel, halves_of(own.shape[1]), [own, arrived])


def halve(order, own, arrived, place_at):
    def kernel(flag, a, b0, b1, mine, other):
        place = flag[place_at]
        mine[...] = a[at_rows(place, QUARTER), :] + jnp.where(place == 0, b0[...], b1[...])
        other[...] = a[at_rows(1 - place, QUARTER), :] + jnp.where(place == 0, b1[...], b0[...])

    return order.call(kernel, [((QUARTER, own.shape[1]), F32)] * 2, [own, *arrived])


def finish_forward(order, mine, arrived, hidden, outer_b):
    def kernel(flag, a, b, h, bias, out):
        at = at_rows(flag[CORE_AT] * 2 + flag[ON_AT], QUARTER)
        out[...] = a[...] + b[...] + h[at, :] + wide(bias[...])

    return order.call(kernel, [(mine.shape, F32)], [mine, arrived, hidden, outer_b])[0]


def finish_backward(order, mine, arrived, hat, inverse, hidden_grad, gain):
    def kernel(flag, a, b, hat_ref, inverse_ref, h, gain_ref, out):
        at = at_rows(flag[CORE_AT] * 2 + flag[BACK_AT], QUARTER)
        grad = (a[...] + b[...]) * wide(gain_ref[...])
        out[...] = h[at, :] + standardize_back(grad, hat_ref[at, :], inverse_ref[at, :])

    args = [mine, arrived, hat, inverse, hidden_grad, gain]
    return order.call(kernel, [(mine.shape, F32)], args)[0]


def pick(order, arrived, own, receiver):
    def kernel(flag, a, b, out):
        out[...] = jnp.where(flag[FIRST_AT] == receiver, a[...], b[...])

    return order.call(kernel, [(own.shape, F32)], [arrived, own])[0]


def squeeze(order, memory, older, weight, bias):
    local = weight.shape[-1]

    def kernel(flag, memory_ref, older_ref, w, b, out):
        row = lax.broadcasted_iota(jnp.int32, (COMP, memory.shape[0]), 0)
        col = lax.broadcasted_iota(jnp.int32, (COMP, memory.shape[0]), 1)
        total = wide(b[...])
        for r in range(RATE):
            chosen = low(wide((col == row * RATE + r).astype(jnp.int32)))
            total = total + dot(low(dot(chosen, memory_ref[...])), w[r])
        out[:COMP, :] = older_ref[COMP:, at_rows(flag[MEMBER_AT], local)]
        out[COMP:, :] = low(total)

    return order.call(kernel, [((2 * COMP, local), BF16)], [memory, older, weight, bias])[0]


def memory_sums(order, older, memory, keys_grad, values_grad, key_w, value_w):
    def kernel(flag, older_ref, memory_ref, kg, vg, wk, wv, out):
        out[...] = jnp.zeros_like(out)
        for i, source in enumerate((older_ref, memory_ref)):
            for start in range(0, source.shape[0], CHUNK):
                hat, _ = standardize(wide(source[start : start + CHUNK, :]))
                at = slice(i * source.shape[0] + start, i * source.shape[0] + start + CHUNK)
                grad = dot_t(kg[at, :], wk[...]) + dot_t(vg[at, :], wv[...])
                out[0:1, :] = out[0:1, :] + jnp.sum(grad * hat, 0, keepdims=True)
                out[1:2, :] = out[1:2, :] + jnp.sum(grad, 0, keepdims=True)

    width, local = key_w.shape
    args = [older, memory, keys_grad, values_grad, key_w, value_w]
    flops = 4 * (older.shape[0] + memory.shape[0]) * width * local
    return order.call(kernel, [((2, width), F32)], args, flops)[0]


def block_at(index):
    return at_rows(index % 4, BLOCK)


def sub_at(index):
    return at_rows(index % 4, SUB)


def ring_sum(order, operands, make, columns, outs, place, extra=None):
    more = 0 if extra is None else extra.shape[0]
    extras = [] if extra is None else [extra]

    def rows_of(count, added=0):
        return ((count + added, columns), F32)

    blocks = [pltpu.VMEM((2, BLOCK, columns), F32)]

    def both(upward, up_moves, downward, down_moves):
        upward, downward = after((upward, downward), order.flags)
        return send(upward, up_moves), send(downward, down_moves)

    def far_kernel(flag, *refs):
        for q in range(2):
            refs[-2 + q][:BLOCK, :] = make(refs, q, flag[RING_AT] + 2)
            if more:
                refs[-2 + q][BLOCK:, :] = refs[-3][...]

    far = order.call(far_kernel, [rows_of(BLOCK, more)] * 2, operands + extras)
    yield
    below, above = both(far[0], UP, far[1], DOWN)
    yield

    def next_kernel(flag, *refs):
        below_ref, above_ref, up_ref, down_ref = refs[-4:]
        here = flag[RING_AT]
        up_ref[:BLOCK, :] = make(refs, 0, here + 1) + below_ref[:BLOCK, :]
        up_ref[BLOCK : 2 * BLOCK, :] = make(refs, 1, here + 1)
        down_ref[:BLOCK, :] = make(refs, 0, here + 3)
        down_ref[BLOCK : 2 * BLOCK, :] = make(refs, 1, here + 3) + above_ref[:BLOCK, :]
        if more:
            up_ref[2 * BLOCK :, :] = below_ref[BLOCK:, :]
            down_ref[2 * BLOCK :, :] = refs[-5][...] + below_ref[BLOCK:, :] + above_ref[BLOCK:, :]

    up, down = order.call(
        next_kernel, [rows_of(2 * BLOCK, more)] * 2, [*operands, *extras, below, above]
    )
    extras = [down] if more else []
    yield
    below, above = both(up, UP, down, DOWN)
    yield

    def own_kernel(flag, *refs):
        below_ref, above_ref, far_p, far_q, up_ref, down_ref, own_ref, acc = refs[-8:]
        if more:
            partial = refs[-9][2 * BLOCK :, :] + below_ref[2 * BLOCK :, :]
            far_p[SUB:, :], far_q[SUB:, :] = partial, partial
            up_ref[2 * SUB :, :], down_ref[2 * SUB :, :] = partial, partial
        here, there = flag[RING_AT], flag[RING2_AT]
        for q in range(2):
            at = slice(q * BLOCK, (q + 1) * BLOCK)
            acc[q] = make(refs, q, here) + below_ref[at, :] + above_ref[at, :]
            half = slice(q * SUB, (q + 1) * SUB)
            (far_p, far_q)[q][:SUB, :] = acc[q, sub_at(there + 2), :]
            up_ref[half, :] = acc[q, sub_at(there + 1), :]
            down_ref[half, :] = acc[q, sub_at(there + 3), :]
            own_ref[half, :] = acc[q, sub_at(there), :]

    far_p, far_q, up, down, own = order.call(
        own_kernel,
        [rows_of(SUB, more)] * 2 + [rows_of(2 * SUB, more)] * 2 + [rows_of(2 * SUB)],
        [*operands, *extras, below, above],
        scratch=blocks,
    )
    yield
    below, above = both(far_p, UP2, far_q, DOWN2)
    yield

    def next_small(flag, up_in, down_in, below_ref, above_ref, up_ref, down_ref):
        p, q, rest = slice(0, SUB), slice(SUB, 2 * SUB), slice(2 * SUB, None)
        up_ref[p, :], up_ref[q, :] = up_in[p, :] + below_ref[:SUB, :], up_in[q, :]
        down_ref[p, :], down_ref[q, :] = down_in[p, :], down_in[q, :] + above_ref[:SUB, :]
        if more:
            up_ref[rest, :] = below_ref[SUB:, :]
            down_ref[rest, :] = down_in[rest, :] + below_ref[SUB:, :] + above_ref[SUB:, :]

    up, down = order.call(
        next_small, [rows_of(2 * SUB, more)] * 2, [up, down, below, above]
    )
    yield
    below, above = both(up, UP2, down, DOWN2)
    yield

    def own_small(flag, own_ref, below_ref, above_ref, down_ref, out, *rest):
        out[...] = own_ref[...] + below_ref[: 2 * SUB, :] + above_ref[: 2 * SUB, :]
        if more:
            rest[0][...] = down_ref[2 * SUB :, :] + below_ref[2 * SUB :, :]

    outs_small = [rows_of(2 * SUB)] + ([rows_of(more)] if more else [])
    own, *extras = order.call(own_small, outs_small, [own, below, above, down])
    yield extras
    below, above = both(own, UP2, own, DOWN2)
    yield

    def pass_small(flag, below_ref, above_ref, up_ref, down_ref):
        up_ref[...], down_ref[...] = below_ref[:SUB, :], above_ref[SUB:, :]

    up, down = order.call(pass_small, [rows_of(SUB)] * 2, [below, above])
    yield
    far_p, far_q = both(up, UP2, down, DOWN2)
    yield

    def join(flag, own_ref, below_ref, above_ref, far_p_ref, far_q_ref, out, acc):
        there = flag[RING2_AT]
        for q, far_ref in enumerate((far_p_ref, far_q_ref)):
            half = slice(q * SUB, (q + 1) * SUB)
            acc[q, sub_at(there), :] = own_ref[half, :]
            acc[q, sub_at(there + 3), :] = below_ref[half, :]
            acc[q, sub_at(there + 1), :] = above_ref[half, :]
            acc[q, sub_at(there + 2), :] = far_ref[...]
            out[q * BLOCK : (q + 1) * BLOCK, :] = acc[q]

    total = order.call(
        join, [rows_of(2 * BLOCK)], [own, below, above, far_p, far_q], 1, blocks
    )[0]
    yield
    below, above = both(total, UP, total, DOWN)
    yield

    def pass_kernel(flag, below_ref, above_ref, up_ref, down_ref):
        up_ref[...], down_ref[...] = below_ref[:BLOCK, :], above_ref[BLOCK:, :]

    up, down = order.call(pass_kernel, [rows_of(BLOCK)] * 2, [below, above])
    yield
    far_p, far_q = both(up, UP, down, DOWN)
    yield

    copies = len(place(0, 0)) + len(place(1, 0))

    def run(moves, sems):
        started = [pltpu.make_async_copy(a, b, sems.at[i]) for i, (a, b) in enumerate(moves)]
        for copy in started:
            copy.start()
        for copy in started:
            copy.wait()

    def moves_of(piece, start, q, index, out_refs):
        return [
            (piece.at[start : start + BLOCK, cols], out_refs[out].at[to])
            for cols, out, to in place(q, index)
        ]

    def first_writes(flag, own_ref, below_ref, above_ref, *rest):
        out_refs, sems = rest[:-1], rest[-1]
        here = flag[RING_AT]
        moves = []
        for piece, index in ((own_ref, here), (below_ref, here + 3), (above_ref, here + 1)):
            for q in range(2):
                moves += moves_of(piece, q * BLOCK, q, index, out_refs)
        run(moves, sems)

    outs = [(shape, F32) for shape in outs]
    results = order.call(
        first_writes,
        outs,
        [total, below, above],
        1,
        [pltpu.SemaphoreType.DMA((3 * copies,))],
        out_specs=[ANYWHERE] * len(outs),
    )
    yield

    def last_writes(flag, far_p_ref, far_q_ref, *rest):
        out_refs, sems = rest[len(outs) : -1], rest[-1]
        index = flag[RING_AT] + 2
        moves = moves_of(far_p_ref, 0, 0, index, out_refs)
        moves += moves_of(far_q_ref, 0, 1, index, out_refs)
        run(moves, sems)

    results = order.call(
        last_writes,
        outs,
        [far_p, far_q, *results],
        1,
        [pltpu.SemaphoreType.DMA((copies,))],
        specs=[WHOLE] * 2 + [ANYWHERE] * len(outs),
        out_specs=[ANYWHERE] * len(outs),
        aliases={3 + i: i for i in range(len(outs))},
    )
    return [*results, *extras]


class Task:
    def __init__(self, steps):
        self.steps, self.result, self.ended, self.extra = steps, None, False, None

    def step(self, count=1):
        for _ in range(count):
            if not self.ended:
                try:
                    told = next(self.steps)
                    self.extra = told[0] if told else self.extra
                except StopIteration as end:
                    self.result, self.ended = end.value, True
        return self.result

    def finish(self):
        while not self.ended:
            self.step()
        return self.result


def body(
    inputs,
    memories,
    compressed,
    documents,
    cotangent,
    compressed_cotangent,
    query_weight,
    key_weight,
    value_weight,
    output_weight,
    output_bias,
    inner_weight,
    inner_bias,
    outer_weight,
    outer_bias,
    conv_weight,
    conv_bias,
    attn_gain,
    attn_shift,
    ffn_gain,
    ffn_shift,
):
    section = lax.axis_index("pipe")
    group = lax.axis_index("dp")
    member = lax.axis_index("tensor")
    core, chip = member % 2, member // 2
    on_place = jnp.where(section == 0, chip, 1 - chip)
    y, z = group // 4, group % 4
    ring, ring2 = jnp.where(core == 0, y, z), jnp.where(core == 0, z, y)
    order = Order(
        jnp.stack([core, on_place, 1 - on_place, 1 - section, ring, ring2, member]).astype(jnp.int32)
    )
    width = inputs.shape[1]
    local = query_weight.shape[2]
    held = documents.shape[1] - SEG
    chunks = range(SEG // CHUNK)
    qkv_w = (query_weight[0], key_weight[0], value_weight[0])
    key_w, value_w, output_w = key_weight[0], value_weight[0], output_weight[0]
    inner_w, outer_w = inner_weight[0], outer_weight[0]
    norm_a, norm_f = (attn_gain, attn_shift), (ffn_gain, ffn_shift)
    memory, older = memories[0, 0], compressed[0, 0]
    squeeze_cot = compressed_cotangent[0, 0]

    memory_low, *past_memory = prepare_memory(order, older, memory, *norm_a, key_w, value_w)

    def make_conv(refs, q, index):
        memory_ref, cot = refs[:2]
        row = lax.broadcasted_iota(jnp.int32, (SEG, COMP), 0)
        col = lax.broadcasted_iota(jnp.int32, (SEG, COMP), 1)
        chosen = low(wide((row == col * RATE + q).astype(jnp.int32)))
        return t_dot(memory_ref[:, block_at(index)], low(dot(chosen, cot[...])))

    def place_conv(q, index):
        return [(slice(None), 0, (q, block_at(index)))]

    conv = Task(
        ring_sum(order, [memory, squeeze_cot], make_conv, local, [(RATE, width, local)], place_conv)
    )

    weights_a = (qkv_w, *norm_a, output_w)
    weights_f = (output_bias, *norm_f, inner_w, inner_bias)

    def twins(pieces, moves):
        return [send(piece, moves) for piece in pieces]

    def to_chip(own, pieces, moves):
        total = add_pieces(order, own, pieces)
        return total, send(total, moves)

    def to_core(value, arrived, moves):
        total, *pieces = add_into_pieces(order, value, arrived)
        return [total, *twins(pieces, moves)]

    def spread(piece):
        beyond = send(piece, CHIP)
        return [piece, beyond, send(piece, CORE), send(beyond, CORE)]

    attended, past = [], [past_memory]
    for i in chunks:
        made = attend_chunk(order, inputs, [], past, documents, i, *weights_a, False)
        past = past + [(made[1], made[2])]
        attended.append((made[0], made[3], twins(made[4:], CORE_FIRST)))

    def feed(i, parts):
        hidden, own, *others = feed_chunk(order, attended[i][0], parts, *weights_f, outer_w)
        return hidden, own, twins(others, CORE_FIRST)

    def split(own, arrived):
        mine, other = halve(order, own, arrived, ON_AT)
        return mine, send(other, CHIP_FIRST)

    def finish(hidden, mine, arrived):
        total = finish_forward(order, mine, arrived, hidden, outer_bias)
        return send(total, ONWARD), total

    half0 = to_chip(*attended[0][1:], CHIP_FIRST)
    half1 = to_chip(*attended[1][1:], CHIP_FIRST)
    conv.step(4)
    half0 = to_core(*half0, CORE_FIRST)
    hidden0, *half0 = feed(0, half0)
    quarter0 = split(*half0)
    half1 = to_core(*half1, CORE_FIRST)
    conv.step(2)
    total0 = finish(hidden0, *quarter0)
    hidden1, *half1 = feed(1, half1)
    quarter1 = split(*half1)
    conv.step(2)
    total1 = finish(hidden1, *quarter1)

    forward, kept_a, kept_f, pasts = [], [], [], [[past_memory]]

    def attend(i):
        made = attend_chunk(order, inputs, forward[i], pasts[i], documents, i, *weights_a, True)
        kept_a.append(made)
        pasts.append(pasts[i] + [(made[1], made[2])])
        return made[3], twins(made[4:6], CORE)

    def feed_last(i, parts):
        kept_f.append(feed_chunk(order, kept_a[i][0], parts, *weights_f, None))

    def feed_back(i, pieces, final, core_moves):
        made = feed_back_chunk(
            order, cotangent, i, pieces, (kept_f[i][1], kept_f[i][5]), outer_w, inner_w, final
        )
        return made, (made[1], twins(made[2:4], core_moves))

    def attend_back(i, grad_out, parts, later, final):
        x, k, v, _, _, _, hat, inverse, normed, q, lse, mixed = kept_a[i]
        return attend_back_chunk(
            order,
            grad_out,
            parts,
            kept_f[i][1:3],
            (hat, q, k, v, lse),
            pasts[i],
            documents,
            (output_w, *qkv_w),
            ffn_gain,
            later,
            final,
        )

    forward.append(spread(pick(order, *total0, 0)))
    conv.step(2)
    half0 = attend(0)
    forward.append(spread(pick(order, *total1, 0)))
    half0 = to_chip(*half0, CHIP)
    half1 = attend(1)
    half1 = to_chip(*half1, CHIP)
    conv.step(4)
    half0 = to_core(*half0, CORE)
    feed_last(0, half0)
    made0, half0 = feed_back(0, [], False, CORE_LAST)
    half0 = to_chip(*half0, CHIP_LAST)
    half1 = to_core(*half1, CORE)
    feed_last(1, half1)
    made1, half1 = feed_back(1, [], False, CORE_LAST)
    half1 = to_chip(*half1, CHIP_LAST)
    conv.step(2)
    half0 = to_core(*half0, CORE_LAST)
    half1 = to_core(*half1, CORE_LAST)

    def split_back(own, others):
        mine, other = halve(order, own, others, BACK_AT)
        return mine, send(other, CHIP_LAST)

    def finish_back(i, made, mine, arrived):
        total = finish_backward(
            order, mine, arrived, kept_a[i][6], kept_a[i][7], made[0], attn_gain
        )
        return send(total, BACK), total

    back1 = attend_back(1, made1[0], half1, [], False)
    half1 = back1[1], twins(back1[2:4], CORE_LAST)
    back0 = attend_back(0, made0[0], half0, back1[4:6], False)
    half0 = back0[1], twins(back0[2:4], CORE_LAST)
    quarter1 = split_back(*half1)
    quarter0 = split_back(*half0)
    conv.step()
    total1 = finish_back(1, back1, *quarter1)
    total0 = finish_back(0, back0, *quarter0)
    conv.finish()
    backward = [None, None]
    backward[1] = spread(pick(order, *total1, 1))

    made1, half1 = feed_back(1, backward[1], True, CORE)
    backward[0] = spread(pick(order, *total0, 1))
    half1 = to_chip(*half1, CHIP)
    made0, half0 = feed_back(0, backward[0], True, CORE)

    def make_feed(refs, q, index):
        result = 0.0
        for i in chunks:
            acts, branch, normed, pre = refs[4 * i : 4 * i + 4]
            left, right = (normed, pre) if q else (acts, branch)
            result = result + t_dot(left[:, block_at(index)], right[...])
        return result

    def place_feed(q, index):
        return [(slice(None), q, (block_at(index),))]

    operands = []
    for i, made in enumerate((made0, made1)):
        operands += [kept_f[i][4], made[4], kept_f[i][3], made[5]]
    feeding = Task(
        ring_sum(
            order, operands, make_feed, width, [(width, width)] * 2, place_feed
        )
    )
    feeding.step()
    half0 = to_chip(*half0, CHIP)
    feeding.step()
    half1 = to_core(*half1, CORE)
    back1 = attend_back(1, made1[0], half1, [], True)
    feeding.step(2)
    half0 = to_core(*half0, CORE)
    back0 = attend_back(0, made0[0], half0, [*back1[4:6], *back1[10:12]], True)
    grads = [back0[4:], back1[6:]]
    memory_grads = grads[0][4:6]

    def make_attend(refs, q, index):
        at = block_at(index)
        memory_ref, memory_grad = refs[0], refs[1 + q]
        one, two = 0.0, t_dot(memory_ref[:, at], memory_grad[...])
        for i in chunks:
            normed, mixed, dq, dk, dv, attend_grad = refs[3 + 6 * i : 9 + 6 * i]
            if q:
                two = two + t_dot(normed[:, at], dv[...])
                one = one + t_dot(mixed[...], attend_grad[:, at])
            else:
                two = two + t_dot(normed[:, at], dk[...])
                one = one + t_dot(normed[:, at], dq[...])
        return jnp.concatenate([one, two], 1)

    def place_attend(q, index):
        at, one, two = block_at(index), slice(0, local), slice(local, 2 * local)
        if q:
            return [(one, 3, (slice(None), at)), (two, 2, (at,))]
        return [(one, 0, (at,)), (two, 1, (at,))]

    operands = [memory_low, *memory_grads]
    for i in chunks:
        operands += [kept_a[i][8], kept_a[i][11], *grads[i][:4]]
    sums_m = memory_sums(order, older, memory, *memory_grads, key_w, value_w)

    def pack(flag, a0, a1, m, f0, f1, cot, out):
        for i in range(2):
            at = slice(i * width // 2, (i + 1) * width // 2)
            start = 8 * i
            out[start : start + 2, :] = a0[0:2, at] + a1[0:2, at] + m[:, at]
            out[start + 2 : start + 4, :] = f0[0:2, at] + f1[0:2, at]
            out[start + 4 : start + 5, :] = a0[2:3, at] + a1[2:3, at]
            out[start + 5 : start + 7, :] = f0[2:4, at] + f1[2:4, at]
            out[start + 7 : start + 8, :] = jnp.zeros_like(out[start + 7 : start + 8, :])
        out[7:8, :local] = jnp.sum(wide(cot[...]), 0, keepdims=True)

    args = [grads[0][6], grads[1][6], sums_m, made0[6], made1[6], squeeze_cot]
    small = order.call(pack, [((16, width // 2), F32)], args)[0]
    attending = Task(
        ring_sum(
            order,
            operands,
            make_attend,
            2 * local,
            [(width, local)] * 3 + [(local, width)],
            place_attend,
            small,
        )
    )

    def small_sums(value):
        total = add(order, value, send(value, CORE))
        yield
        total = add(order, total, send(total, CHIP))
        yield

        def unpack(flag, shared, own, out):
            for i in range(2):
                at = slice(i * width // 2, (i + 1) * width // 2)
                out[0:4, at] = shared[8 * i : 8 * i + 4, :]
                out[4:8, at] = own[8 * i + 4 : 8 * i + 8, :]

        return order.call(unpack, [((8, width), F32)], [total, value])[0]

    def sum_rows(own, other):
        half = add(order, own, send(other, CORE))
        arrived = send(half, CHIP)
        yield
        half = add(order, half, arrived)
        arrived = send(half, CORE)
        yield
        return half, arrived

    def put_chunk(out, i, core, half, twin):
        for at, source in ((core, half), (1 - core, twin)):
            out[at_rows(2 * i + at, HALF), :] = source[i * HALF : (i + 1) * HALF, :]

    def layer_output():
        def kernel(flag, *refs):
            wf, own, other, acc = refs[-4:]
            for i in chunks:
                acc[...] = dot(refs[i][...], wf[...])
                at = slice(i * HALF, (i + 1) * HALF)
                own[at, :] = acc[at_rows(flag[CORE_AT], HALF), :]
                other[at, :] = acc[at_rows(1 - flag[CORE_AT], HALF), :]

        args = [kept[4] for kept in kept_f] + [outer_w]
        outs = [((SEG // 2, width), F32)] * 2
        own, other = order.call(kernel, outs, args, scratch=[pltpu.VMEM((CHUNK, width), F32)])
        yield
        half, twin = yield from sum_rows(own, other)

        def kernel(flag, half_ref, twin_ref, bias, *refs):
            out, acc = refs[-2:]
            for i in chunks:
                hidden, pieces = refs[5 * i], refs[5 * i + 1 : 5 * i + 5]
                put_chunk(out, i, flag[CORE_AT], half_ref, twin_ref)
                put_pieces(acc, pieces, flag[CORE_AT], flag[ON_AT])
                at = chunk_rows(i)
                own_out = out[at, :] + hidden[...] + wide(bias[...])
                out[at, :] = jnp.where(flag[FIRST_AT] == 1, acc[...], own_out)

        args = [half, twin, outer_bias]
        for i in chunks:
            args += [kept_f[i][0], *forward[i]]
        return order.call(
            kernel, [((SEG, width), F32)], args, scratch=[pltpu.VMEM((CHUNK, width), F32)]
        )[0]

    def input_gradient():
        def kernel(flag, a0, b0, c0, a1, b1, c1, own, other):
            own[:HALF, :], own[HALF:, :] = a0[...], a1[...]
            for i, ref in enumerate((b0, c0, b1, c1)):
                other[i * QUARTER : (i + 1) * QUARTER, :] = ref[...]

        outs = [((SEG // 2, width), F32)] * 2
        own, other = order.call(kernel, outs, [*back0[1:4], *back1[1:4]])
        yield
        half, twin = yield from sum_rows(own, other)

        def kernel(flag, half_ref, twin_ref, gain, *refs):
            out, acc = refs[-2:]
            for i in chunks:
                hat, inverse, hidden_grad, *pieces = refs[7 * i : 7 * i + 7]
                put_chunk(out, i, flag[CORE_AT], half_ref, twin_ref)
                put_pieces(acc, pieces, flag[CORE_AT], flag[BACK_AT])
                at = chunk_rows(i)
                grad = standardize_back(out[at, :] * wide(gain[...]), hat[...], inverse[...])
                out[at, :] = jnp.where(flag[FIRST_AT] == 1, hidden_grad[...] + grad, acc[...])

        args = [half, twin, attn_gain]
        for i, back in enumerate((back0, back1)):
            args += [kept_a[i][6], kept_a[i][7], back[0], *backward[i]]
        return order.call(
            kernel, [((SEG, width), F32)], args, scratch=[pltpu.VMEM((CHUNK, width), F32)]
        )[0]

    outward, inward = Task(layer_output()), Task(input_gradient())
    attending.step(2)
    outward.step()
    new_compressed = squeeze(order, memory, older, conv_weight[0], conv_bias)
    attending.step(2)
    outward.step()
    feeding.step(2)
    feeding.step(2)
    attending.step(2)
    feeding.step(2)
    attending.step(2)
    outward.step()
    feeding.step(2)
    attending.step(2)
    outward.finish()
    feeding.step(2)
    attending.step(2)
    inward.step(2)
    attending.step(2)
    inward.step()
    feeding.step(2)
    inward.step()
    attending.step(2)
    small = Task(small_sums(attending.extra))
    small.step()
    inward.finish()
    small.step()
    attending.step()
    small.finish()
    feeding.step()
    outer_g, inner_g = feeding.finish()
    query_g, key_g, value_g, output_g, _ = attending.finish()
    total = small.result
    return (
        outward.result[None],
        new_compressed[None, None],
        inward.result[None],
        query_g[None],
        key_g[None],
        value_g[None],
        output_g[None],
        total[4][None],
        inner_g[None],
        total[6][None],
        outer_g[None],
        total[5][None],
        conv.result[0][None],
        total[7, :local][None],
        total[0][None],
        total[1][None],
        total[2][None],
        total[3][None],
    )


def solution(mesh):
    return jax.shard_map(
        body,
        mesh=mesh,
        in_specs=(
            P("dp", None),
            P("pipe", "dp", None, None),
            P("pipe", "dp", None, None),
            P("dp", None),
            P("dp", None),
            P("pipe", "dp", None, "tensor"),
            P("pipe", None, "tensor"),
            P("pipe", None, "tensor"),
            P("pipe", None, "tensor"),
            P("pipe", "tensor", None),
            P("pipe", None),
            P("pipe", None, "tensor"),
            P("pipe", "tensor"),
            P("pipe", "tensor", None),
            P("pipe", None),
            P("pipe", None, None, "tensor"),
            P("pipe", "tensor"),
            P("pipe", None),
            P("pipe", None),
            P("pipe", None),
            P("pipe", None),
        ),
        out_specs=(
            P("pipe", "dp", None),
            P("pipe", "dp", None, "tensor"),
            P("pipe", "dp", None),
            P("pipe", None, "tensor"),
            P("pipe", None, "tensor"),
            P("pipe", None, "tensor"),
            P("pipe", "tensor", None),
            P("pipe", None),
            P("pipe", None, "tensor"),
            P("pipe", "tensor"),
            P("pipe", "tensor", None),
            P("pipe", None),
            P("pipe", None, None, "tensor"),
            P("pipe", "tensor"),
            P("pipe", None),
            P("pipe", None),
            P("pipe", None),
            P("pipe", None),
        ),
        check_vma=False,
    )
```

```python
import jax
import jax.numpy as jnp
from jax import lax
from jax.experimental import pallas as pl
from jax.experimental.pallas import tpu as pltpu
from jax.sharding import PartitionSpec as P

HEAD_DIM = 128
SEG = 512
RATE = 2
COMP = 256
CHUNK = 256
HALF = 128
QUARTER = 64
TILE = 256
BLOCK = 256
SUB = 64
HEADS = 2
SCALE = HEAD_DIM ** (-0.5)
LIMIT = 16 * 2**20
AXES = ("pipe", "dp", "tensor")


def pairs(move):
    found = []
    for p in range(2):
        for y in range(4):
            for z in range(4):
                for x in range(2):
                    for c in range(2):
                        there = move(p, y, z, x, c)
                        if there is None:
                            continue
                        q, v, w, u, d = there
                        source = ((p * 4 + y) * 4 + z) * 4 + x * 2 + c
                        target = ((q * 4 + v % 4) * 4 + w % 4) * 4 + u * 2 + d
                        found.append((source, target))
    return found


CORE = pairs(lambda p, y, z, x, c: (p, y, z, x, 1 - c))
CHIP = pairs(lambda p, y, z, x, c: (p, y, z, 1 - x, c))
ONWARD = pairs(lambda p, y, z, x, c: (1, y, z, 1 - x, c) if p == 0 else None)
BACK = pairs(lambda p, y, z, x, c: (0, y, z, 1 - x, c) if p == 1 else None)
UP = pairs(lambda p, y, z, x, c: (p, y + 1 - c, z + c, x, c))
DOWN = pairs(lambda p, y, z, x, c: (p, y + 3 * (1 - c), z + 3 * c, x, c))
UP2 = pairs(lambda p, y, z, x, c: (p, y + c, z + 1 - c, x, c))
DOWN2 = pairs(lambda p, y, z, x, c: (p, y + 3 * c, z + 3 * (1 - c), x, c))
ONE = pairs(lambda p, y, z, x, c: (p, y ^ (1 - c), z ^ c, x, c))
TWO = pairs(lambda p, y, z, x, c: (p, y ^ (2 * (1 - c)), z ^ (2 * c), x, c))
ONE2 = pairs(lambda p, y, z, x, c: (p, y ^ c, z ^ (1 - c), x, c))
TWO2 = pairs(lambda p, y, z, x, c: (p, y ^ (2 * c), z ^ (2 * (1 - c)), x, c))


def low(value):
    return value.astype(jnp.bfloat16)


def wide(value):
    return value.astype(jnp.float32)


def send(value, moves):
    return lax.ppermute(value, AXES, moves)


def after(value, anchor):
    return lax.optimization_barrier((value, anchor))[0]


def dot(left, right):
    return jnp.dot(left, right, preferred_element_type=jnp.float32)


def dot_t(left, right):
    return lax.dot_general(
        left, right, (((1,), (1,)), ((), ())), preferred_element_type=jnp.float32
    )


def t_dot(left, right):
    return lax.dot_general(
        left, right, (((0,), (0,)), ((), ())), preferred_element_type=jnp.float32
    )


def standardize(values):
    centered = values - jnp.mean(values, -1, keepdims=True)
    variance = jnp.mean(centered * centered, -1, keepdims=True)
    inverse = lax.rsqrt(variance + 1e-05)
    return centered * inverse, inverse


def standardize_back(grad, hat, inverse):
    return inverse * (
        grad
        - jnp.mean(grad, -1, keepdims=True)
        - hat * jnp.mean(grad * hat, -1, keepdims=True)
    )


def gelu_and_slope(value):
    square = value * value
    curve = jnp.tanh(0.7978845608028654 * value * (1.0 + 0.044715 * square))
    up = 0.5 + 0.5 * curve
    slope = up + (0.5 * value) * (1.0 - curve * curve) * (
        0.7978845608028654 + (3 * 0.044715 * 0.7978845608028654) * square
    )
    return value * up, slope


F32, BF16 = jnp.float32, jnp.bfloat16
WHOLE = pl.BlockSpec(memory_space=pltpu.VMEM)
SCALAR = pl.BlockSpec(memory_space=pltpu.SMEM)
ANYWHERE = pl.BlockSpec(memory_space=pl.ANY)
OUTSIDE = pl.BlockSpec(memory_space=pltpu.HBM)
CORE_AT, ON_AT, BACK_AT, FIRST_AT, RING_AT, RING2_AT, MEMBER_AT = range(7)


class Order:
    def __init__(self, flags):
        self.flags = flags

    def then(self, anchor):
        self.flags = after(self.flags, anchor)

    def call(
        self, kernel, outs, args, scratch=(), specs=None, out_specs=None, aliases=None, limit=LIMIT, only=None
    ):
        args = [self.flags, *args]
        whole = kernel
        if only is not None:

            def kernel(flag, *refs):
                @pl.when(flag[FIRST_AT] == only)
                def _():
                    whole(flag, *refs)

        results = pl.pallas_call(
            kernel,
            out_shape=[jax.ShapeDtypeStruct(shape, dtype) for shape, dtype in outs],
            in_specs=[SCALAR] + (specs or [WHOLE] * (len(args) - 1)),
            out_specs=out_specs or [WHOLE] * len(outs),
            scratch_shapes=list(scratch),
            input_output_aliases=aliases or {},
            compiler_params=pltpu.CompilerParams(vmem_limit_bytes=limit),
            cost_estimate=pl.CostEstimate(flops=1, bytes_accessed=1, transcendentals=0),
        )(*args)
        self.then(tuple(results))
        return results


def at_rows(index, size):
    return pl.ds(pl.multiple_of(index * size, size), size)


def chunk_at(index, core):
    return pl.ds(pl.multiple_of(index * CHUNK + core * HALF, HALF), HALF)


def put_pieces(out_ref, pieces, place):
    out_ref[at_rows(place, QUARTER), :] = pieces[0][...]
    out_ref[at_rows(1 - place, QUARTER), :] = pieces[1][...]


def split_rows(value_ref, mine_ref, other_ref, place):
    mine_ref[...] = value_ref[at_rows(place, QUARTER), :]
    other_ref[...] = value_ref[at_rows(1 - place, QUARTER), :]


def own_documents(docs, start, core):
    row = lax.broadcasted_iota(jnp.int32, (HALF, HALF), 0)
    col = lax.broadcasted_iota(jnp.int32, (HALF, HALF), 1)
    own = wide(docs[:, pl.ds(pl.multiple_of(start + core * HALF, HALF), HALF)])
    return jnp.sum(jnp.where(row == col, own, 0.0), -1, keepdims=True)


def masked(scores, docs_q, docs_k, core):
    allowed = docs_q == docs_k
    if core is not None:
        q_pos = lax.broadcasted_iota(jnp.int32, scores.shape, 0) + core * HALF
        k_pos = lax.broadcasted_iota(jnp.int32, scores.shape, 1)
        allowed = allowed & (k_pos <= q_pos)
    return jnp.where(allowed, scores * SCALE, -1e30)


def widen(order, parts, limit=LIMIT):
    def kernel(flag, *refs):
        start = 0
        for ref in refs[:-1]:
            refs[-1][:, start : start + ref.shape[1]] = wide(ref[...])
            start += ref.shape[1]

    shape = (parts[0].shape[0], sum(part.shape[1] for part in parts))
    return order.call(kernel, [(shape, F32)], parts, limit=limit)[0]


def widen_with_row(order, value, row):
    def kernel(flag, a, b, out):
        rows = a.shape[0]
        out[:rows, :] = wide(a[...])
        out[rows:, :] = jnp.broadcast_to(wide(b[...]), (8, b.shape[1]))

    shape = (value.shape[0] + 8, value.shape[1])
    return order.call(kernel, [(shape, F32)], [value, row])[0]


def prepare_memory(order, older, memory, gain, shift, key_w, value_w):
    held, width = older.shape[0] + memory.shape[0], older.shape[1]
    local = key_w.shape[1]

    def kernel(flag, older_ref, memory_ref, gain_ref, shift_ref, wk, wv, normed, k, v):
        gain_row, shift_row = wide(gain_ref[...]), wide(shift_ref[...])
        for i, source in enumerate((older_ref, memory_ref)):
            for start in range(0, source.shape[0], CHUNK):
                hat, _ = standardize(wide(source[start : start + CHUNK, :]))
                at = slice(i * source.shape[0] + start, i * source.shape[0] + start + CHUNK)
                normed[at, :] = low(hat * gain_row + shift_row)
                k[at, :] = low(dot(normed[at, :], wk[...]))
                v[at, :] = low(dot(normed[at, :], wv[...]))

    outs = [((held, width), BF16), ((held, local), BF16), ((held, local), BF16)]
    return order.call(kernel, outs, [older, memory, gain, shift, key_w, value_w])


def gather_projections(order, memory_low, memory_k, memory_v, own, twin_qkv, twin_o):
    width, local = own[0].shape
    held = memory_low.shape[0]

    def kernel(flag, normed, k, v, wq, wk, wv, wo, other, other_o, q_out, k_out, v_out, o_out, ks, vs):
        for i, (ref, out) in enumerate(((wq, q_out), (wk, k_out), (wv, v_out))):
            out[:, :local] = ref[...]
            out[:, local:] = low(other[:, i * local : (i + 1) * local])
        o_out[:local, :], o_out[local:, :] = wo[...], low(other_o[...])
        ks[:, :local], vs[:, :local] = k[...], v[...]
        for start in range(0, held, CHUNK):
            at = slice(start, start + CHUNK)
            ks[at, local:] = low(dot(normed[at, :], k_out[:, local:]))
            vs[at, local:] = low(dot(normed[at, :], v_out[:, local:]))

    outs = [((width, 2 * local), BF16)] * 3 + [((2 * local, width), BF16)]
    outs += [((held, 2 * local), BF16)] * 2
    return order.call(kernel, outs, [memory_low, memory_k, memory_v, *own, twin_qkv, twin_o])


def gather_feed(order, inner_w, inner_b, outer_w, twin_inner, twin_outer):
    width, units = inner_w.shape

    def kernel(flag, wi, bi, wf, other_i, other_f, i_out, b_out, f_out):
        i_out[:, :units], i_out[:, units:] = wi[...], low(other_i[:width, :])
        b_out[:, :units], b_out[:, units:] = wide(bi[...]), other_i[width : width + 1, :]
        f_out[:units, :], f_out[units:, :] = wf[...], low(other_f[...])

    outs = [((width, 2 * units), BF16), ((1, 2 * units), F32), ((2 * units, width), BF16)]
    return order.call(kernel, outs, [inner_w, inner_b, outer_w, twin_inner, twin_outer])


def project(order, inputs, pieces, index, weights, gain, shift, keep):
    given = len(pieces)
    width, columns = weights[0].shape

    def kernel(*refs):
        flag, x_in = refs[0], refs[1]
        piece_refs, rest = refs[2 : 2 + given], refs[2 + given :]
        gain_ref, shift_ref, wq, wk, wv, x, q, kv, *rest = rest
        own = wide(x_in[chunk_at(index, flag[CORE_AT]), :])
        if given:
            put_pieces(x, piece_refs, flag[ON_AT])
            x[...] = jnp.where(flag[FIRST_AT] == 1, own, x[...])
        else:
            x[...] = own
        hat, inverse = standardize(x[...])
        normed = low(hat * wide(gain_ref[...]) + wide(shift_ref[...]))
        if keep:
            rest[0][...], rest[1][...], rest[2][...] = hat, inverse, normed
        q[...] = low(dot(normed, wq[...]))
        kv[:, :columns] = wide(low(dot(normed, wk[...])))
        kv[:, columns:] = wide(low(dot(normed, wv[...])))

    outs = [((HALF, width), F32), ((HALF, columns), BF16), ((HALF, 2 * columns), F32)]
    if keep:
        outs += [((HALF, width), F32), ((HALF, 1), F32), ((HALF, width), BF16)]
    return order.call(kernel, outs, [inputs, *pieces, gain, shift, *weights])


def swap_halves(value):
    half = value.shape[1] // 2
    return jnp.concatenate([value[:, half:], value[:, :half]], 1)


def spans(past):
    sizes = [k.shape[0] for k, _ in past] + [CHUNK]
    return [sum(sizes[:i]) for i in range(len(sizes))], sizes


def attention(q, parts, starts, sizes, docs_ref, core, lse=None):
    docs_q = own_documents(docs_ref, starts[-1], core)
    mixed = []
    for h in range(q.shape[1] // HEAD_DIM):
        cols = slice(h * HEAD_DIM, (h + 1) * HEAD_DIM)
        scores = [
            masked(
                dot_t(q[:, cols], key[:, cols]),
                docs_q,
                wide(docs_ref[:, start : start + size]),
                core if i == len(parts) - 1 else None,
            )
            for i, ((key, _), start, size) in enumerate(zip(parts, starts, sizes))
        ]
        top = scores[0].max(-1, keepdims=True)
        for score in scores[1:]:
            top = jnp.maximum(top, score.max(-1, keepdims=True))
        total, value_sum = 0.0, 0.0
        for score, (_, value) in zip(scores, parts):
            exps = jnp.exp(score - top)
            total = total + exps.sum(-1, keepdims=True)
            value_sum = value_sum + dot(low(exps), value[:, cols])
        mixed.append(low(value_sum / total))
        if lse is not None:
            lse[:, h : h + 1] = top + jnp.log(total)
    return jnp.concatenate(mixed, 1)


def attend_inputs(order, inputs, index, weights, gain, shift, past, docs, output_w):
    starts, sizes = spans(past)
    width, columns = weights[0].shape

    def kernel(flag, x_in, gain_ref, shift_ref, wq, wk, wv, docs_ref, wo, *rest):
        past_refs, rest = rest[: 2 * len(past)], rest[2 * len(past) :]
        x, k, v, out, normed = rest
        core = flag[CORE_AT]
        x[...] = wide(x_in[chunk_at(index, core), :])
        hat, _ = standardize(wide(x_in[index * CHUNK : (index + 1) * CHUNK, :]))
        normed[...] = low(hat * wide(gain_ref[...]) + wide(shift_ref[...]))
        k[...] = low(dot(normed[...], wk[...]))
        v[...] = low(dot(normed[...], wv[...]))
        q = low(dot(normed[at_rows(core, HALF), :], wq[...]))
        parts = [(past_refs[2 * i], past_refs[2 * i + 1]) for i in range(len(past))] + [(k, v)]
        out[...] = dot(attention(q, parts, starts, sizes, docs_ref, core), wo[...])

    outs = [((HALF, width), F32)] + [((CHUNK, columns), BF16)] * 2 + [((HALF, width), F32)]
    args = [inputs, gain, shift, *weights, docs, output_w] + [item for pair in past for item in pair]
    return order.call(kernel, outs, args, [pltpu.VMEM((CHUNK, width), BF16)], only=1)


def attend_chunk(order, queries, kv, kv_twin, past, docs, output_w):
    starts, sizes = spans(past)
    columns, width = output_w.shape

    def kernel(flag, q, own, other, docs_ref, wo, *rest):
        past_refs, rest = rest[: 2 * len(past)], rest[2 * len(past) :]
        k, v, out, lse, mixed = rest
        core = flag[CORE_AT]
        k[at_rows(core, HALF), :] = low(own[:, :columns])
        v[at_rows(core, HALF), :] = low(own[:, columns:])
        k[at_rows(1 - core, HALF), :] = low(swap_halves(other[:, :columns]))
        v[at_rows(1 - core, HALF), :] = low(swap_halves(other[:, columns:]))
        parts = [(past_refs[2 * i], past_refs[2 * i + 1]) for i in range(len(past))] + [(k, v)]
        mixed[...] = attention(q, parts, starts, sizes, docs_ref, core, lse)
        out[...] = dot(mixed[...], wo[...])

    outs = [((CHUNK, columns), BF16)] * 2 + [((HALF, width), F32)]
    outs += [((HALF, columns // HEAD_DIM), F32), ((HALF, columns), BF16)]
    args = [queries, kv, kv_twin, docs, output_w] + [item for pair in past for item in pair]
    return order.call(kernel, outs, args)


def feed_chunk(order, layer_input, part, arrived, output_b, gain, shift, inner_w, inner_b, outer_w):
    ending = outer_w is not None
    width, units = inner_w.shape

    def kernel(flag, x, a, b, bo, gain_ref, shift_ref, wi, bi, *rest):
        if ending:
            wf, hidden, mine, other, acc = rest
        else:
            hidden, hat_ref, inverse_ref, normed_ref, acts_ref, slope_ref = rest
        hidden[...] = x[...] + (a[...] + b[...] + wide(bo[...]))
        hat, inverse = standardize(hidden[...])
        normed = low(hat * wide(gain_ref[...]) + wide(shift_ref[...]))
        if not ending:
            hat_ref[...], inverse_ref[...], normed_ref[...] = hat, inverse, normed
        for start in range(0, units, TILE):
            tile = slice(start, start + TILE)
            acts, slope = gelu_and_slope(dot(normed, wi[:, tile]) + bi[:, tile])
            if ending:
                term = dot(low(acts), wf[tile, :])
                acc[...] = term if start == 0 else acc[...] + term
            else:
                acts_ref[:, tile] = low(acts)
                slope_ref[:, tile] = slope
        if ending:
            split_rows(acc, mine, other, flag[ON_AT])

    outs = [((HALF, width), F32)]
    if ending:
        outs += [((QUARTER, width), F32)] * 2
    else:
        outs += [
            ((HALF, width), F32),
            ((HALF, 1), F32),
            ((HALF, width), BF16),
            ((HALF, units), BF16),
            ((HALF, units), F32),
        ]
    args = [layer_input, part, arrived, output_b, gain, shift, inner_w, inner_b]
    args += [outer_w] if ending else []
    scratch = [pltpu.VMEM((HALF, width), F32)] if ending else []
    return order.call(kernel, outs, args, scratch, only=1 if ending else None)


def feed_back_chunk(order, cotangent, index, pieces, kept, outer_w, inner_w, final):
    hat, slope = kept
    given = len(pieces)
    units, width = outer_w.shape
    own_units = units // 2

    def kernel(*refs):
        flag, cot = refs[0], refs[1]
        piece_refs, rest = refs[2 : 2 + given], refs[2 + given :]
        slope_ref, wf, wi, *rest = rest
        if final:
            hat_ref, grad_out, out, branch, pre_grad, sums, passed = rest
        else:
            grad_out, out = rest
        own_cot = wide(cot[chunk_at(index, flag[CORE_AT]), :])
        if given:
            put_pieces(grad_out, piece_refs, flag[BACK_AT])
            grad_out[...] = jnp.where(flag[FIRST_AT] == 1, grad_out[...], own_cot)
        else:
            grad_out[...] = own_cot
        branch_grad = low(grad_out[...])
        for start in range(0, units, TILE):
            tile = slice(start, start + TILE)
            grad = low(slope_ref[:, tile] * dot_t(branch_grad, wf[tile, :]))
            if final and start < own_units:
                pre_grad[:, tile] = grad
            elif final:
                passed[HALF:, start - own_units : start - own_units + TILE] = wide(grad)
            term = dot_t(grad, wi[:, tile])
            out[...] = term if start == 0 else out[...] + term
        if final:
            branch[...] = branch_grad
            passed[:HALF, :] = wide(branch_grad)
            sums[0:1, :] = jnp.sum(out[...] * hat_ref[...], 0, keepdims=True)
            sums[1:2, :] = jnp.sum(out[...], 0, keepdims=True)
            sums[2:3, :] = jnp.sum(wide(branch_grad), 0, keepdims=True)
            sums[3:4, :] = jnp.zeros_like(sums[3:4, :])

    outs = [((HALF, width), F32)] * 2
    args = [cotangent, *pieces, slope, outer_w, inner_w]
    if final:
        outs += [((HALF, width), BF16), ((HALF, own_units), BF16), ((4, width), F32)]
        outs += [((CHUNK, width), F32)]
        args += [hat]
    return order.call(kernel, outs, args, only=None if final else 0)


def attend_back_chunk(
    order, grad_out, part, arrived, kept_f, queries, kv, lse, past, docs, output_w, gain_f, later, final
):
    hat_f, inverse_f = kept_f
    starts, sizes = spans(past)
    last = len(past) > 1
    columns, width = output_w.shape
    heads, local = columns // HEAD_DIM, columns // 2
    held, size = sizes[0], starts[-1] + CHUNK
    first_key = 0 if final else held

    def kernel(*refs):
        refs = list(refs)

        def take(count):
            taken = refs[:count]
            del refs[:count]
            return taken

        flag, g_out, a, b, hf, invf, gf, wo, docs_ref, q, k, v, lse_ref = take(13)
        past_refs = take(2 * len(past))
        later_refs = take(len(later))
        hidden_grad, query_rows, own, other = take(4)
        passed = take(1) if last else []
        kept = take(3) if final else []
        (sums,) = take(1)
        core = flag[CORE_AT]
        grad = standardize_back((a[...] + b[...]) * wide(gf[...]), hf[...], invf[...])
        hidden_grad[...] = g_out[...] + grad
        attend_grad = low(hidden_grad[...])
        mixed_grad = low(dot_t(attend_grad, wo[...]))
        parts = [(past_refs[2 * i], past_refs[2 * i + 1]) for i in range(len(past))] + [(k, v)]
        docs_q = own_documents(docs_ref, starts[-1], core)
        for h in range(heads):
            cols = slice(h * HEAD_DIM, (h + 1) * HEAD_DIM)
            value_cols = slice(columns + h * HEAD_DIM, columns + (h + 1) * HEAD_DIM)
            grad = mixed_grad[:, cols]
            probs, probs_grads, inner = [], [], 0.0
            for (key, value), start, length in zip(parts, starts, sizes):
                score = masked(
                    dot_t(q[:, cols], key[:, cols]),
                    docs_q,
                    wide(docs_ref[:, start : start + length]),
                    core if key is k else None,
                )
                probs.append(jnp.exp(score - lse_ref[:, h : h + 1]))
                probs_grads.append(dot_t(grad, value[:, cols]))
                inner = inner + jnp.sum(probs[-1] * probs_grads[-1], -1, keepdims=True)
            query_row = 0.0
            for i, (key, value) in enumerate(parts):
                score_grad = low(probs[i] * (probs_grads[i] - inner))
                query_row = query_row + dot(score_grad, key[:, cols])
                if i == 0 and not final:
                    continue
                at = slice(starts[i] - first_key, starts[i] - first_key + sizes[i])
                sums[at, cols] = t_dot(score_grad, q[:, cols])
                sums[at, value_cols] = t_dot(low(probs[i]), grad)
            query_rows[:, cols] = low(query_row * SCALE)
        chunk = slice(starts[-1] - first_key, size - first_key)
        if last:
            passed[0][...] = sums[starts[1] - first_key : starts[2] - first_key, :]
        else:
            sums[chunk, :] = sums[chunk, :] + later_refs[0][...]
        base = (starts[-1] - first_key) // HALF
        own[...] = sums[at_rows(base + core, HALF), :]
        other[...] = sums[at_rows(base + 1 - core, HALF), :]
        if final:
            kept[0][...] = attend_grad
            for i in range(2):
                for j in range(2):
                    cols = slice(j * columns + i * local, j * columns + (i + 1) * local)
                    total = sums[:held, cols]
                    out_cols = slice(j * local, (j + 1) * local)
                    if not last:
                        total = total + later_refs[1 + i][:, out_cols]
                    kept[1 + i][:, out_cols] = total

    outs = [((HALF, width), F32), ((HALF, columns), BF16)] + [((HALF, 2 * columns), F32)] * 2
    if last:
        outs += [((CHUNK, 2 * columns), F32)]
    if final:
        outs += [((HALF, width), BF16)] + [((held, columns), F32)] * 2
    args = [grad_out, part, arrived, hat_f, inverse_f, gain_f, output_w, docs, queries, *kv, lse]
    args += [item for pair in past for item in pair] + list(later)
    scratch = [pltpu.VMEM((size - first_key, 2 * columns), F32)]
    return order.call(kernel, outs, args, scratch, only=None if final else 0)


def project_back(order, query_rows, own, arrived, weights, hat, final):
    width, columns = weights[0].shape

    def kernel(flag, dq, a, b, wq, wk, wv, *rest):
        key_rows = low((a[:, :columns] + swap_halves(b[:, :columns])) * SCALE)
        value_rows = low(a[:, columns:] + swap_halves(b[:, columns:]))
        out = rest[1] if final else rest[-1]
        out[...] = dot_t(dq[...], wq[...]) + dot_t(key_rows, wk[...])
        out[...] = out[...] + dot_t(value_rows, wv[...])
        if final:
            hat_ref, _, keys_out, values_out, sums = rest
            keys_out[...], values_out[...] = key_rows, value_rows
            sums[0:1, :] = jnp.sum(out[...] * hat_ref[...], 0, keepdims=True)
            sums[1:2, :] = jnp.sum(out[...], 0, keepdims=True)
        else:
            split_rows(out, rest[0], rest[1], flag[BACK_AT])

    args = [query_rows, own, arrived, *weights]
    if final:
        outs = [((HALF, width), F32)] + [((HALF, columns), BF16)] * 2 + [((2, width), F32)]
        return order.call(kernel, outs, args + [hat])
    outs = [((QUARTER, width), F32)] * 2
    return order.call(kernel, outs, args, [pltpu.VMEM((HALF, width), F32)], only=0)


def add(order, *terms):
    def kernel(flag, *refs):
        total = refs[0][...]
        for ref in refs[1:-1]:
            total = total + ref[...]
        refs[-1][...] = total

    return order.call(kernel, [(terms[0].shape, F32)], terms)[0]


def finish_forward(order, mine, arrived, hidden, outer_b):
    def kernel(flag, a, b, h, bias, out):
        out[...] = a[...] + b[...] + h[at_rows(flag[ON_AT], QUARTER), :] + wide(bias[...])

    return order.call(kernel, [(mine.shape, F32)], [mine, arrived, hidden, outer_b])[0]


def finish_backward(order, mine, arrived, hat, inverse, hidden_grad, gain):
    def kernel(flag, a, b, hat_ref, inverse_ref, h, gain_ref, out):
        at = at_rows(flag[BACK_AT], QUARTER)
        grad = (a[...] + b[...]) * wide(gain_ref[...])
        out[...] = h[at, :] + standardize_back(grad, hat_ref[at, :], inverse_ref[at, :])

    args = [mine, arrived, hat, inverse, hidden_grad, gain]
    return order.call(kernel, [(mine.shape, F32)], args)[0]


def pick(order, arrived, own, receiver):
    def kernel(flag, a, b, out):
        out[...] = jnp.where(flag[FIRST_AT] == receiver, a[...], b[...])

    return order.call(kernel, [(own.shape, F32)], [arrived, own])[0]


def squeeze(order, memory, older, weight, bias):
    local = weight.shape[-1]

    def kernel(flag, memory_ref, older_ref, w, b, out):
        row = lax.broadcasted_iota(jnp.int32, (COMP, memory.shape[0]), 0)
        col = lax.broadcasted_iota(jnp.int32, (COMP, memory.shape[0]), 1)
        total = wide(b[...])
        for r in range(RATE):
            chosen = low(wide((col == row * RATE + r).astype(jnp.int32)))
            total = total + dot(low(dot(chosen, memory_ref[...])), w[r])
        out[:COMP, :] = older_ref[COMP:, at_rows(flag[MEMBER_AT], local)]
        out[COMP:, :] = low(total)

    return order.call(kernel, [((2 * COMP, local), BF16)], [memory, older, weight, bias])[0]


def memory_sums(order, older, memory, keys_grad, values_grad, key_w, value_w):
    def kernel(flag, older_ref, memory_ref, kg, vg, wk, wv, out):
        out[...] = jnp.zeros_like(out)
        for i, source in enumerate((older_ref, memory_ref)):
            for start in range(0, source.shape[0], CHUNK):
                hat, _ = standardize(wide(source[start : start + CHUNK, :]))
                at = slice(i * source.shape[0] + start, i * source.shape[0] + start + CHUNK)
                grad = dot_t(kg[at, :], wk[...]) + dot_t(vg[at, :], wv[...])
                out[0:1, :] = out[0:1, :] + jnp.sum(grad * hat, 0, keepdims=True)
                out[1:2, :] = out[1:2, :] + jnp.sum(grad, 0, keepdims=True)

    width, local = key_w.shape
    args = [older, memory, keys_grad, values_grad, key_w, value_w]
    return order.call(kernel, [((2, width), F32)], args)[0]


def block_at(index):
    return at_rows(index % 4, BLOCK)


def sub_at(index):
    return at_rows(index % 4, SUB)


def ring_sum(order, operands, make, columns, outs, place, extra=None):
    more = 0 if extra is None else extra.shape[0]
    extras = [] if extra is None else [extra]

    def rows_of(count, added=0):
        return ((count + added, columns), F32)

    blocks = [pltpu.VMEM((2, BLOCK, columns), F32)]

    def both(upward, up_moves, downward, down_moves):
        upward, downward = after((upward, downward), order.flags)
        return send(upward, up_moves), send(downward, down_moves)

    def far_kernel(flag, *refs):
        for q in range(2):
            refs[-2 + q][:BLOCK, :] = make(refs, q, flag[RING_AT] + 2)
            if more:
                refs[-2 + q][BLOCK:, :] = refs[-3][...]

    far = order.call(far_kernel, [rows_of(BLOCK, more)] * 2, operands + extras)
    yield
    below, above = both(far[0], UP, far[1], DOWN)
    yield

    def next_kernel(flag, *refs):
        below_ref, above_ref, up_ref, down_ref = refs[-4:]
        here = flag[RING_AT]
        up_ref[:BLOCK, :] = make(refs, 0, here + 1) + below_ref[:BLOCK, :]
        up_ref[BLOCK : 2 * BLOCK, :] = make(refs, 1, here + 1)
        down_ref[:BLOCK, :] = make(refs, 0, here + 3)
        down_ref[BLOCK : 2 * BLOCK, :] = make(refs, 1, here + 3) + above_ref[:BLOCK, :]
        if more:
            up_ref[2 * BLOCK :, :] = below_ref[BLOCK:, :]
            down_ref[2 * BLOCK :, :] = refs[-5][...] + below_ref[BLOCK:, :] + above_ref[BLOCK:, :]

    up, down = order.call(
        next_kernel, [rows_of(2 * BLOCK, more)] * 2, [*operands, *extras, below, above]
    )
    extras = [down] if more else []
    yield
    below, above = both(up, UP, down, DOWN)
    yield

    def own_kernel(flag, *refs):
        below_ref, above_ref, far_p, far_q, up_ref, down_ref, own_ref, acc = refs[-8:]
        if more:
            partial = refs[-9][2 * BLOCK :, :] + below_ref[2 * BLOCK :, :]
            far_p[SUB:, :], far_q[SUB:, :] = partial, partial
            up_ref[2 * SUB :, :], down_ref[2 * SUB :, :] = partial, partial
        here, there = flag[RING_AT], flag[RING2_AT]
        for q in range(2):
            at = slice(q * BLOCK, (q + 1) * BLOCK)
            acc[q] = make(refs, q, here) + below_ref[at, :] + above_ref[at, :]
            half = slice(q * SUB, (q + 1) * SUB)
            (far_p, far_q)[q][:SUB, :] = acc[q, sub_at(there + 2), :]
            up_ref[half, :] = acc[q, sub_at(there + 1), :]
            down_ref[half, :] = acc[q, sub_at(there + 3), :]
            own_ref[half, :] = acc[q, sub_at(there), :]

    far_p, far_q, up, down, own = order.call(
        own_kernel,
        [rows_of(SUB, more)] * 2 + [rows_of(2 * SUB, more)] * 2 + [rows_of(2 * SUB)],
        [*operands, *extras, below, above],
        scratch=blocks,
    )
    yield
    below, above = both(far_p, UP2, far_q, DOWN2)
    yield

    def next_small(flag, up_in, down_in, below_ref, above_ref, up_ref, down_ref):
        p, q, rest = slice(0, SUB), slice(SUB, 2 * SUB), slice(2 * SUB, None)
        up_ref[p, :], up_ref[q, :] = up_in[p, :] + below_ref[:SUB, :], up_in[q, :]
        down_ref[p, :], down_ref[q, :] = down_in[p, :], down_in[q, :] + above_ref[:SUB, :]
        if more:
            up_ref[rest, :] = below_ref[SUB:, :]
            down_ref[rest, :] = down_in[rest, :] + below_ref[SUB:, :] + above_ref[SUB:, :]

    up, down = order.call(
        next_small, [rows_of(2 * SUB, more)] * 2, [up, down, below, above]
    )
    yield
    below, above = both(up, UP2, down, DOWN2)
    yield

    def own_small(flag, own_ref, below_ref, above_ref, down_ref, out, *rest):
        out[...] = own_ref[...] + below_ref[: 2 * SUB, :] + above_ref[: 2 * SUB, :]
        if more:
            rest[0][...] = down_ref[2 * SUB :, :] + below_ref[2 * SUB :, :]

    outs_small = [rows_of(2 * SUB)] + ([rows_of(more)] if more else [])
    own, *extras = order.call(own_small, outs_small, [own, below, above, down])
    yield extras
    below, above = both(own, UP2, own, DOWN2)
    yield

    def pass_small(flag, below_ref, above_ref, up_ref, down_ref):
        up_ref[...], down_ref[...] = below_ref[:SUB, :], above_ref[SUB:, :]

    up, down = order.call(pass_small, [rows_of(SUB)] * 2, [below, above])
    yield
    far_p, far_q = both(up, UP2, down, DOWN2)
    yield

    def join(flag, own_ref, below_ref, above_ref, far_p_ref, far_q_ref, out, acc):
        there = flag[RING2_AT]
        for q, far_ref in enumerate((far_p_ref, far_q_ref)):
            half = slice(q * SUB, (q + 1) * SUB)
            acc[q, sub_at(there), :] = own_ref[half, :]
            acc[q, sub_at(there + 3), :] = below_ref[half, :]
            acc[q, sub_at(there + 1), :] = above_ref[half, :]
            acc[q, sub_at(there + 2), :] = far_ref[...]
            out[q * BLOCK : (q + 1) * BLOCK, :] = acc[q]

    total = order.call(
        join, [rows_of(2 * BLOCK)], [own, below, above, far_p, far_q], blocks
    )[0]
    yield
    below, above = both(total, UP, total, DOWN)
    yield

    def pass_kernel(flag, below_ref, above_ref, up_ref, down_ref):
        up_ref[...], down_ref[...] = below_ref[:BLOCK, :], above_ref[BLOCK:, :]

    up, down = order.call(pass_kernel, [rows_of(BLOCK)] * 2, [below, above])
    yield
    far_p, far_q = both(up, UP, down, DOWN)
    yield

    copies = len(place(0, 0)) + len(place(1, 0))

    def run(moves, sems):
        started = [pltpu.make_async_copy(a, b, sems.at[i]) for i, (a, b) in enumerate(moves)]
        for copy in started:
            copy.start()
        for copy in started:
            copy.wait()

    def moves_of(piece, start, q, index, out_refs):
        return [
            (piece.at[start : start + BLOCK, cols], out_refs[out].at[to])
            for cols, out, to in place(q, index)
        ]

    def first_writes(flag, own_ref, below_ref, above_ref, *rest):
        out_refs, sems = rest[:-1], rest[-1]
        here = flag[RING_AT]
        moves = []
        for piece, index in ((own_ref, here), (below_ref, here + 3), (above_ref, here + 1)):
            for q in range(2):
                moves += moves_of(piece, q * BLOCK, q, index, out_refs)
        run(moves, sems)

    outs = [(shape, F32) for shape in outs]
    results = order.call(
        first_writes,
        outs,
        [total, below, above],
        [pltpu.SemaphoreType.DMA((3 * copies,))],
        out_specs=[ANYWHERE] * len(outs),
    )
    yield

    def last_writes(flag, far_p_ref, far_q_ref, *rest):
        out_refs, sems = rest[len(outs) : -1], rest[-1]
        index = flag[RING_AT] + 2
        moves = moves_of(far_p_ref, 0, 0, index, out_refs)
        moves += moves_of(far_q_ref, 0, 1, index, out_refs)
        run(moves, sems)

    results = order.call(
        last_writes,
        outs,
        [far_p, far_q, *results],
        [pltpu.SemaphoreType.DMA((copies,))],
        specs=[WHOLE] * 2 + [ANYWHERE] * len(outs),
        out_specs=[ANYWHERE] * len(outs),
        aliases={3 + i: i for i in range(len(outs))},
    )
    return [*results, *extras]


class Task:
    def __init__(self, steps):
        self.steps, self.result, self.ended, self.extra = steps, None, False, None

    def step(self, count=1):
        for _ in range(count):
            if not self.ended:
                try:
                    told = next(self.steps)
                    self.extra = told[0] if told else self.extra
                except StopIteration as end:
                    self.result, self.ended = end.value, True
        return self.result

    def finish(self):
        while not self.ended:
            self.step()
        return self.result


def body(
    inputs,
    memories,
    compressed,
    documents,
    cotangent,
    compressed_cotangent,
    query_weight,
    key_weight,
    value_weight,
    output_weight,
    output_bias,
    inner_weight,
    inner_bias,
    outer_weight,
    outer_bias,
    conv_weight,
    conv_bias,
    attn_gain,
    attn_shift,
    ffn_gain,
    ffn_shift,
):
    section = lax.axis_index("pipe")
    group = lax.axis_index("dp")
    member = lax.axis_index("tensor")
    core, chip = member % 2, member // 2
    on_place = jnp.where(section == 0, chip, 1 - chip)
    y, z = group // 4, group % 4
    ring, ring2 = jnp.where(core == 0, y, z), jnp.where(core == 0, z, y)
    order = Order(
        jnp.stack([core, on_place, 1 - on_place, 1 - section, ring, ring2, member]).astype(jnp.int32)
    )
    width = inputs.shape[1]
    local = query_weight.shape[2]
    units = inner_weight.shape[2]
    held = documents.shape[1] - SEG
    chunks = range(SEG // CHUNK)
    both = CHUNK * len(chunks) // 2
    own_qkv = (query_weight[0], key_weight[0], value_weight[0])
    key_w, value_w = key_weight[0], value_weight[0]
    norm_a, norm_f = (attn_gain, attn_shift), (ffn_gain, ffn_shift)
    memory, older = memories[0, 0], compressed[0, 0]
    squeeze_cot = compressed_cotangent[0, 0]

    twin_qkv = send(widen(order, own_qkv), CORE)
    twin_o = send(widen(order, [output_weight[0]]), CORE)
    memory_low, memory_k, memory_v = prepare_memory(order, older, memory, *norm_a, key_w, value_w)
    *qkv_w, output_w, memory_k, memory_v = gather_projections(
        order, memory_low, memory_k, memory_v, (*own_qkv, output_weight[0]), twin_qkv, twin_o
    )
    past_memory = (memory_k, memory_v)

    twin_inner = send(widen_with_row(order, inner_weight[0], inner_bias), CORE)
    twin_outer = send(widen(order, [outer_weight[0]]), CORE)
    attended, past = [], [past_memory]
    for i in chunks:
        made = attend_inputs(order, inputs, i, qkv_w, *norm_a, past, documents, output_w)
        past = past + [tuple(made[1:3])]
        attended.append((made[0], made[3], send(made[3], CHIP)))
    inner_w, inner_b, outer_w = gather_feed(
        order, inner_weight[0], inner_bias, outer_weight[0], twin_inner, twin_outer
    )
    weights_f = (output_bias, *norm_f, inner_w, inner_b)
    hidden, mine, arrived, total, arriving = ([None, None] for _ in range(5))
    for i in chunks:
        hidden[i], mine[i], other = feed_chunk(
            order, *attended[i], *weights_f, outer_w
        )
        arrived[i] = send(other, CHIP)
    for i in chunks:
        total[i] = finish_forward(order, mine[i], arrived[i], hidden[i], outer_bias)
        arriving[i] = send(total[i], ONWARD)


    forward = []
    for i in chunks:
        piece = pick(order, arriving[i], total[i], 0)
        forward.append([piece, send(piece, CHIP)])
    kept_p, kept_a, pasts = [], [], [[past_memory]]
    for i in chunks:
        made = project(order, inputs, forward[i], i, qkv_w, *norm_a, True)
        kept_p.append((*made, send(made[2], CORE)))
    for i in chunks:
        x, q, kv = kept_p[i][:3]
        made = attend_chunk(order, q, kv, kept_p[i][-1], pasts[i], documents, output_w)
        pasts.append(pasts[i] + [tuple(made[:2])])
        kept_a.append((*made, send(made[2], CHIP)))
    kept_f, fed = [], []
    for i in chunks:
        kept_f.append(
            feed_chunk(order, kept_p[i][0], kept_a[i][2], kept_a[i][-1], *weights_f, None)
        )
        grad_out, out = feed_back_chunk(
            order, cotangent, i, [], (kept_f[i][1], kept_f[i][5]), outer_w, inner_w, False
        )
        fed.append((grad_out, out, send(out, CHIP)))

    def pack_rows(flag, *refs):
        out = refs[-1]
        for i, ref in enumerate(refs[:-1]):
            out[i * HALF : (i + 1) * HALF, :] = wide(ref[:, -width:])

    def attend_back(i, grad_out, out, arrived, later, final, core_moves):
        made = attend_back_chunk(
            order,
            grad_out,
            out,
            arrived,
            kept_f[i][1:3],
            kept_p[i][1],
            kept_a[i][:2],
            kept_a[i][3],
            pasts[i],
            documents,
            output_w,
            ffn_gain,
            later,
            final,
        )
        return made, send(made[3], core_moves)

    back, arrived, mine, total, backward = ([None, None] for _ in range(5))

    def begin_back(i, later):
        back[i], arrived[i] = attend_back(i, *fed[i], later, False, CORE)

    def middle_back(i):
        mine[i], other = project_back(
            order, back[i][1], back[i][2], arrived[i], qkv_w, None, False
        )
        arrived[i] = send(other, CHIP)

    def end_back(i):
        total[i] = finish_backward(
            order, mine[i], arrived[i], kept_p[i][3], kept_p[i][4], back[i][0], attn_gain
        )
        arriving[i] = send(total[i], BACK)

    def receive_back(i):
        piece = pick(order, arriving[i], total[i], 1)
        backward[i] = [piece, send(piece, CHIP)]

    begin_back(1, [])
    begin_back(0, [back[1][4]])
    middle_back(1)
    middle_back(0)
    args = [kept_f[i][4] for i in chunks] + [kept_f[i][3] for i in chunks]
    args += [kept_p[i][5] for i in chunks]
    twin_rows = send(order.call(pack_rows, [((len(args) * HALF, width), F32)], args)[0], CORE)


    end_back(1)
    end_back(0)
    receive_back(1)
    receive_back(0)

    def unpack_rows(flag, *refs):
        parts, arrived_ref, outs = refs[:6], refs[6], refs[7:]
        for i, out in enumerate(outs):
            out[:HALF, :] = parts[2 * i][:, :width]
            out[HALF : 2 * HALF, :] = parts[2 * i + 1][:, :width]
            out[2 * HALF :, :] = low(arrived_ref[2 * i * HALF : 2 * (i + 1) * HALF, :])

    acts_all, normed_f_all, normed_all = order.call(
        unpack_rows, [((SEG, width), BF16)] * 3, [*args, twin_rows]
    )
    made = [None, None]
    for i in reversed(chunks):
        made[i] = feed_back_chunk(
            order, cotangent, i, backward[i], (kept_f[i][1], kept_f[i][5]), outer_w, inner_w, True
        )
        arrived[i] = send(made[i][5], CORE)
        fed[i] = (made[i][0], made[i][1], send(made[i][1], CHIP))

    def unpack_feed(flag, b0, b1, p0, p1, a0, a1, branch, pre, sums):
        for i, (ref, out) in enumerate(((b0, branch), (b1, branch), (p0, pre), (p1, pre))):
            start = i % 2 * HALF
            out[start : start + HALF, :] = ref[...]
        for i, ref in enumerate((a0, a1)):
            at = slice((2 + i) * HALF, (3 + i) * HALF)
            branch[at, :], pre[at, :] = low(ref[:HALF, :]), low(ref[HALF:, :])
        sums[...] = jnp.sum(wide(pre[...]), 0, keepdims=True)

    branch_all, pre_all, pre_sum = order.call(
        unpack_feed,
        [((SEG, width), BF16), ((SEG, units), BF16), ((1, units), F32)],
        [made[0][2], made[1][2], made[0][3], made[1][3], *arrived],
    )

    def make_feed(refs, q, index):
        acts, branch, normed, pre = refs[:4]
        left, right = (normed, pre) if q else (acts, branch)
        return t_dot(left[:, block_at(index)], right[...])

    def place_feed(q, index):
        return [(slice(None), q, (block_at(index),))]

    feeding = Task(
        ring_sum(
            order,
            [acts_all, branch_all, normed_f_all, pre_all],
            make_feed,
            width,
            [(width, width)] * 2,
            place_feed,
        )
    )
    feeding.step(4)
    projected, later = [None, None], []
    for i in reversed(chunks):
        back[i], arrived[i] = attend_back(i, *fed[i], later, True, CORE)
        later = [back[i][4], *back[i][6:8]] if i else []
    kept = [back[0][4:], back[1][5:]]
    twin_memory = send(kept[0][2], CORE)
    def assemble(own):
        arrived = send(own, CORE)
        yield

        def kernel(flag, a, b, out):
            for i in chunks:
                at = slice(i * HALF, (i + 1) * HALF)
                out[chunk_at(i, flag[CORE_AT]), :] = a[at, :]
                out[chunk_at(i, 1 - flag[CORE_AT]), :] = b[at, :]

        return order.call(kernel, [((SEG, width), F32)], [own, arrived])[0]

    def layer_output():
        def kernel(flag, a0, a1, wf, out):
            for i, ref in enumerate((a0, a1)):
                out[i * HALF : (i + 1) * HALF, :] = dot(ref[...], wf[...])

        args = [kept_f[i][4] for i in chunks] + [outer_w]
        out = order.call(kernel, [((both, width), F32)], args)[0]
        yield
        arrived = send(after(out, order.flags), CHIP)
        yield

        def kernel(flag, a, b, bias, *refs):
            out, acc = refs[-2:]
            for i in chunks:
                hidden_ref, *pieces = refs[3 * i : 3 * i + 3]
                put_pieces(acc, pieces, flag[ON_AT])
                at = slice(i * HALF, (i + 1) * HALF)
                total = hidden_ref[...] + (a[at, :] + b[at, :] + wide(bias[...]))
                out[at, :] = jnp.where(flag[FIRST_AT] == 1, acc[...], total)

        args = [out, arrived, outer_bias]
        for i in chunks:
            args += [kept_f[i][0], *forward[i]]
        scratch = [pltpu.VMEM((HALF, width), F32)]
        own = order.call(kernel, [((both, width), F32)], args, scratch)[0]
        return (yield from assemble(own))

    def pack_attend(flag, *refs):
        *heads, attend_grad, out = refs
        for j, ref in enumerate(heads):
            out[:HALF, j * local : (j + 1) * local] = wide(ref[:, local:])
        out[HALF:, :] = wide(attend_grad[...])

    heads, twin_heads = [None, None], [None, None]
    for i in reversed(chunks):
        projected[i] = project_back(
            order, back[i][1], back[i][2], arrived[i], qkv_w, kept_p[i][3], True
        )
        heads[i] = [back[i][1], projected[i][1], projected[i][2], kept_a[i][4], kept[i][0]]
        packed = order.call(pack_attend, [((CHUNK, width), F32)], heads[i])[0]
        twin_heads[i] = send(packed, CORE)
    outward = Task(layer_output())
    outward.step()
    new_compressed = squeeze(order, memory, older, conv_weight[0], conv_bias)
    feeding.step(2)

    def unpack_attend(flag, *refs):
        *outs, attend_out = refs[12:]
        for i in chunks:
            *parts, attend_grad, arrived_ref = refs[6 * i : 6 * i + 6]
            own, twin = i * HALF, (2 + i) * HALF
            for j, (ref, out) in enumerate(zip(parts, outs)):
                out[own : own + HALF, :] = ref[:, :local]
                out[twin : twin + HALF, :] = low(arrived_ref[:HALF, j * local : (j + 1) * local])
            attend_out[own : own + HALF, :] = attend_grad[...]
            attend_out[twin : twin + HALF, :] = low(arrived_ref[HALF:, :])

    def unpack_memory(flag, mine_ref, memory_ref, keys_out, values_out):
        keys_out[...] = low((mine_ref[:, :local] + memory_ref[:, :local]) * SCALE)
        values_out[...] = low(mine_ref[:, local:] + memory_ref[:, local:])

    *heads_all, attend_all = order.call(
        unpack_attend,
        [((SEG, local), BF16)] * 4 + [((SEG, width), BF16)],
        [item for i in chunks for item in (*heads[i], twin_heads[i])],
    )
    feeding.step(2)
    memory_kg, memory_vg = order.call(
        unpack_memory, [((held, local), BF16)] * 2, [kept[0][1], twin_memory]
    )
    sums_m = memory_sums(order, older, memory, memory_kg, memory_vg, key_w, value_w)

    def pack_sums(flag, a0, a1, m, f0, f1, g0, g1, pre, cot, out):
        out[...] = jnp.zeros_like(out)
        for i in range(2):
            at = slice(i * width // 2, (i + 1) * width // 2)
            start, to = 8 * i, slice(0, width // 2)
            out[start : start + 2, to] = a0[:, at] + a1[:, at] + m[:, at]
            out[start + 2 : start + 4, to] = f0[0:2, at] + f1[0:2, at]
            attend_sum = jnp.sum(wide(g0[:, at]) + wide(g1[:, at]), 0, keepdims=True)
            out[start + 4 : start + 5, to] = attend_sum
            out[start + 5 : start + 6, to] = f0[2:3, at] + f1[2:3, at]
            out[start + 6 : start + 7, to] = pre[:, at]
        out[7:8, :local] = jnp.sum(wide(cot[...]), 0, keepdims=True)

    args = [projected[0][3], projected[1][3], sums_m, made[0][4], made[1][4]]
    args += [kept[0][0], kept[1][0], pre_sum, squeeze_cot]
    small = order.call(pack_sums, [((16, 3 * local), F32)], args)[0]

    def make_attend(refs, q, index):
        at = block_at(index)
        memory_ref, normed = refs[0], refs[1]
        dq, dk, dv, mixed, attend_grad, memory_keys, memory_values, segment, cot = refs[2:11]
        row = lax.broadcasted_iota(jnp.int32, (SEG, COMP), 0)
        col = lax.broadcasted_iota(jnp.int32, (SEG, COMP), 1)
        chosen = low(wide((row == col * RATE + q).astype(jnp.int32)))
        three = t_dot(segment[:, at], low(dot(chosen, cot[...])))
        if q:
            one = t_dot(mixed[...], attend_grad[:, at])
            two = t_dot(memory_ref[:, at], memory_values[...]) + t_dot(normed[:, at], dv[...])
        else:
            one = t_dot(normed[:, at], dq[...])
            two = t_dot(memory_ref[:, at], memory_keys[...]) + t_dot(normed[:, at], dk[...])
        return jnp.concatenate([one, two, three], 1)

    def place_attend(q, index):
        at = block_at(index)
        one, two, three = (slice(i * local, (i + 1) * local) for i in range(3))
        if q:
            return [(one, 3, (slice(None), at)), (two, 2, (at,)), (three, 4, (q, at))]
        return [(one, 0, (at,)), (two, 1, (at,)), (three, 4, (q, at))]

    attending = Task(
        ring_sum(
            order,
            [
                memory_low,
                normed_all,
                *heads_all,
                attend_all,
                memory_kg,
                memory_vg,
                memory,
                squeeze_cot,
            ],
            make_attend,
            3 * local,
            [(width, local)] * 3 + [(local, width), (RATE, width, local)],
            place_attend,
            small,
        )
    )

    def small_sums(value):
        pair = add(order, value, send(value, CORE))
        yield
        total = add(order, pair, send(pair, CHIP))
        yield

        def unpack(flag, all_ref, pair_ref, own_ref, out):
            for i in range(2):
                at = slice(i * width // 2, (i + 1) * width // 2)
                start, held_at = 8 * i, slice(0, width // 2)
                out[0:4, at] = all_ref[start : start + 4, held_at]
                out[4:6, at] = pair_ref[start + 4 : start + 6, held_at]
                out[6:8, at] = own_ref[start + 6 : start + 8, held_at]

        return order.call(unpack, [((8, width), F32)], [total, pair, value])[0]

    def input_gradient():
        def kernel(flag, a0, a1, out):
            out[:HALF, :], out[HALF:, :] = a0[...], a1[...]

        args = [projected[i][0] for i in chunks]
        out = order.call(kernel, [((both, width), F32)], args)[0]
        yield
        arrived = send(after(out, order.flags), CHIP)
        yield

        def kernel(flag, a, b, gain, *refs):
            out, acc = refs[-2:]
            for i in chunks:
                hat, inverse, hidden_grad, *pieces = refs[5 * i : 5 * i + 5]
                put_pieces(acc, pieces, flag[BACK_AT])
                at = slice(i * HALF, (i + 1) * HALF)
                grad = (a[at, :] + b[at, :]) * wide(gain[...])
                grad = hidden_grad[...] + standardize_back(grad, hat[...], inverse[...])
                out[at, :] = jnp.where(flag[FIRST_AT] == 1, grad, acc[...])

        args = [out, arrived, attn_gain]
        for i in chunks:
            args += [kept_p[i][3], kept_p[i][4], back[i][0], *backward[i]]
        scratch = [pltpu.VMEM((HALF, width), F32)]
        own = order.call(kernel, [((both, width), F32)], args, scratch)[0]
        return (yield from assemble(own))

    inward = Task(input_gradient())
    attending.step(2)
    feeding.step(2)
    outward.step()
    feeding.step(2)
    attending.step(2)
    feeding.step(2)
    attending.step(2)
    outward.step()
    attending.step(2)
    attending.step(2)
    outward.finish()
    inward.step(2)
    attending.step(2)
    attending.step(2)
    feeding.step(2)
    inward.step()
    small = Task(small_sums(attending.extra))
    inward.finish()
    small.step(2)
    attending.step(2)
    small.finish()
    feeding.step()
    feeding.finish()
    attending.step()
    outer_g, inner_g = feeding.finish()
    query_g, key_g, value_g, output_g, conv_g, _ = attending.finish()
    total = small.result
    return (
        outward.result[None],
        new_compressed[None, None],
        inward.result[None],
        query_g[None],
        key_g[None],
        value_g[None],
        output_g[None],
        total[4][None],
        inner_g[None],
        total[6][None],
        outer_g[None],
        total[5][None],
        conv_g[None],
        total[7, :local][None],
        total[0][None],
        total[1][None],
        total[2][None],
        total[3][None],
    )


def solution(mesh):
    return jax.shard_map(
        body,
        mesh=mesh,
        in_specs=(
            P("dp", None),
            P("pipe", "dp", None, None),
            P("pipe", "dp", None, None),
            P("dp", None),
            P("dp", None),
            P("pipe", "dp", None, "tensor"),
            P("pipe", None, "tensor"),
            P("pipe", None, "tensor"),
            P("pipe", None, "tensor"),
            P("pipe", "tensor", None),
            P("pipe", None),
            P("pipe", None, "tensor"),
            P("pipe", "tensor"),
            P("pipe", "tensor", None),
            P("pipe", None),
            P("pipe", None, None, "tensor"),
            P("pipe", "tensor"),
            P("pipe", None),
            P("pipe", None),
            P("pipe", None),
            P("pipe", None),
        ),
        out_specs=(
            P("pipe", "dp", None),
            P("pipe", "dp", None, "tensor"),
            P("pipe", "dp", None),
            P("pipe", None, "tensor"),
            P("pipe", None, "tensor"),
            P("pipe", None, "tensor"),
            P("pipe", "tensor", None),
            P("pipe", None),
            P("pipe", None, "tensor"),
            P("pipe", "tensor"),
            P("pipe", "tensor", None),
            P("pipe", None),
            P("pipe", None, None, "tensor"),
            P("pipe", "tensor"),
            P("pipe", None),
            P("pipe", None),
            P("pipe", None),
            P("pipe", None),
        ),
        check_vma=False,
    )
```

```python
import jax
import jax.numpy as jnp
from jax import lax
from jax.experimental import pallas as pl
from jax.experimental.pallas import tpu as pltpu
from jax.sharding import PartitionSpec as P

HEAD_DIM = 128
SEG = 512
RATE = 2
COMP = 256
CHUNK = 256
HALF = 128
QUARTER = 64
TILE = 256
BLOCK = 256
SUB = 64
HEADS = 2
SCALE = HEAD_DIM ** (-0.5)
LIMIT = 10 * 2**20
AXES = ("pipe", "dp", "tensor")


def pairs(move):
    found = []
    for p in range(2):
        for y in range(4):
            for z in range(4):
                for x in range(2):
                    for c in range(2):
                        there = move(p, y, z, x, c)
                        if there is None:
                            continue
                        q, v, w, u, d = there
                        source = ((p * 4 + y) * 4 + z) * 4 + x * 2 + c
                        target = ((q * 4 + v % 4) * 4 + w % 4) * 4 + u * 2 + d
                        found.append((source, target))
    return found


CORE = pairs(lambda p, y, z, x, c: (p, y, z, x, 1 - c))
CHIP = pairs(lambda p, y, z, x, c: (p, y, z, 1 - x, c))
ONWARD = pairs(lambda p, y, z, x, c: (1, y, z, 1 - x, c) if p == 0 else None)
BACK = pairs(lambda p, y, z, x, c: (0, y, z, 1 - x, c) if p == 1 else None)
UP = pairs(lambda p, y, z, x, c: (p, y + 1 - c, z + c, x, c))
DOWN = pairs(lambda p, y, z, x, c: (p, y + 3 * (1 - c), z + 3 * c, x, c))
UP2 = pairs(lambda p, y, z, x, c: (p, y + c, z + 1 - c, x, c))
DOWN2 = pairs(lambda p, y, z, x, c: (p, y + 3 * c, z + 3 * (1 - c), x, c))
ONE = pairs(lambda p, y, z, x, c: (p, y ^ (1 - c), z ^ c, x, c))
TWO = pairs(lambda p, y, z, x, c: (p, y ^ (2 * (1 - c)), z ^ (2 * c), x, c))
ONE2 = pairs(lambda p, y, z, x, c: (p, y ^ c, z ^ (1 - c), x, c))
TWO2 = pairs(lambda p, y, z, x, c: (p, y ^ (2 * c), z ^ (2 * (1 - c)), x, c))


def low(value):
    return value.astype(jnp.bfloat16)


def wide(value):
    return value.astype(jnp.float32)


def send(value, moves):
    return lax.ppermute(value, AXES, moves)


def after(value, anchor):
    return lax.optimization_barrier((value, anchor))[0]


def dot(left, right):
    return jnp.dot(left, right, preferred_element_type=jnp.float32)


def dot_t(left, right):
    return lax.dot_general(
        left, right, (((1,), (1,)), ((), ())), preferred_element_type=jnp.float32
    )


def t_dot(left, right):
    return lax.dot_general(
        left, right, (((0,), (0,)), ((), ())), preferred_element_type=jnp.float32
    )


def standardize(values):
    centered = values - jnp.mean(values, -1, keepdims=True)
    variance = jnp.mean(centered * centered, -1, keepdims=True)
    inverse = lax.rsqrt(variance + 1e-05)
    return centered * inverse, inverse


def standardize_back(grad, hat, inverse):
    return inverse * (
        grad
        - jnp.mean(grad, -1, keepdims=True)
        - hat * jnp.mean(grad * hat, -1, keepdims=True)
    )


def gelu_and_slope(value):
    square = value * value
    curve = jnp.tanh(0.7978845608028654 * value * (1.0 + 0.044715 * square))
    up = 0.5 + 0.5 * curve
    slope = up + (0.5 * value) * (1.0 - curve * curve) * (
        0.7978845608028654 + (3 * 0.044715 * 0.7978845608028654) * square
    )
    return value * up, slope


F32, BF16 = jnp.float32, jnp.bfloat16
WHOLE = pl.BlockSpec(memory_space=pltpu.VMEM)
SCALAR = pl.BlockSpec(memory_space=pltpu.SMEM)
ANYWHERE = pl.BlockSpec(memory_space=pl.ANY)
OUTSIDE = pl.BlockSpec(memory_space=pltpu.HBM)
CORE_AT, ON_AT, BACK_AT, FIRST_AT, RING_AT, RING2_AT, MEMBER_AT = range(7)


class Order:
    def __init__(self, flags):
        self.flags = flags

    def then(self, anchor):
        self.flags = after(self.flags, anchor)

    def call(
        self, kernel, outs, args, scratch=(), specs=None, out_specs=None, aliases=None, limit=LIMIT, only=None
    ):
        args = [self.flags, *args]
        whole = kernel
        if only is not None:

            def kernel(flag, *refs):
                @pl.when(flag[FIRST_AT] == only)
                def _():
                    whole(flag, *refs)

        results = pl.pallas_call(
            kernel,
            out_shape=[jax.ShapeDtypeStruct(shape, dtype) for shape, dtype in outs],
            in_specs=[SCALAR] + (specs or [WHOLE] * (len(args) - 1)),
            out_specs=out_specs or [WHOLE] * len(outs),
            scratch_shapes=list(scratch),
            input_output_aliases=aliases or {},
            compiler_params=pltpu.CompilerParams(vmem_limit_bytes=limit),
            cost_estimate=pl.CostEstimate(flops=1, bytes_accessed=1, transcendentals=0),
        )(*args)
        self.then(tuple(results))
        return results


def at_rows(index, size):
    return pl.ds(pl.multiple_of(index * size, size), size)


def chunk_at(index, core):
    return pl.ds(pl.multiple_of(index * CHUNK + core * HALF, HALF), HALF)


def put_pieces(out_ref, pieces, place):
    out_ref[at_rows(place, QUARTER), :] = pieces[0][...]
    out_ref[at_rows(1 - place, QUARTER), :] = pieces[1][...]


def split_rows(value_ref, mine_ref, other_ref, place):
    mine_ref[...] = value_ref[at_rows(place, QUARTER), :]
    other_ref[...] = value_ref[at_rows(1 - place, QUARTER), :]


def own_documents(docs, start, core):
    row = lax.broadcasted_iota(jnp.int32, (HALF, HALF), 0)
    col = lax.broadcasted_iota(jnp.int32, (HALF, HALF), 1)
    own = wide(docs[:, pl.ds(pl.multiple_of(start + core * HALF, HALF), HALF)])
    return jnp.sum(jnp.where(row == col, own, 0.0), -1, keepdims=True)


def masked(scores, docs_q, docs_k, core):
    allowed = docs_q == docs_k
    if core is not None:
        q_pos = lax.broadcasted_iota(jnp.int32, scores.shape, 0) + core * HALF
        k_pos = lax.broadcasted_iota(jnp.int32, scores.shape, 1)
        allowed = allowed & (k_pos <= q_pos)
    return jnp.where(allowed, scores * SCALE, -1e30)


def widen(order, parts, limit=LIMIT):
    def kernel(flag, *refs):
        start = 0
        for ref in refs[:-1]:
            refs[-1][:, start : start + ref.shape[1]] = wide(ref[...])
            start += ref.shape[1]

    shape = (parts[0].shape[0], sum(part.shape[1] for part in parts))
    return order.call(kernel, [(shape, F32)], parts, limit=limit)[0]


def widen_with_row(order, value, row):
    def kernel(flag, a, b, out):
        rows = a.shape[0]
        out[:rows, :] = wide(a[...])
        out[rows:, :] = jnp.broadcast_to(wide(b[...]), (8, b.shape[1]))

    shape = (value.shape[0] + 8, value.shape[1])
    return order.call(kernel, [(shape, F32)], [value, row])[0]


def prepare_memory(order, older, memory, gain, shift, key_w, value_w):
    held, width = older.shape[0] + memory.shape[0], older.shape[1]
    local = key_w.shape[1]

    def kernel(flag, older_ref, memory_ref, gain_ref, shift_ref, wk, wv, normed, k, v):
        gain_row, shift_row = wide(gain_ref[...]), wide(shift_ref[...])
        for i, source in enumerate((older_ref, memory_ref)):
            for start in range(0, source.shape[0], CHUNK):
                hat, _ = standardize(wide(source[start : start + CHUNK, :]))
                at = slice(i * source.shape[0] + start, i * source.shape[0] + start + CHUNK)
                normed[at, :] = low(hat * gain_row + shift_row)
                k[at, :] = low(dot(normed[at, :], wk[...]))
                v[at, :] = low(dot(normed[at, :], wv[...]))

    outs = [((held, width), BF16), ((held, local), BF16), ((held, local), BF16)]
    return order.call(kernel, outs, [older, memory, gain, shift, key_w, value_w])


def gather_projections(order, memory_low, memory_k, memory_v, own, twin_qkv, twin_o):
    width, local = own[0].shape
    held = memory_low.shape[0]

    def kernel(flag, normed, k, v, wq, wk, wv, wo, other, other_o, q_out, k_out, v_out, o_out, ks, vs):
        for i, (ref, out) in enumerate(((wq, q_out), (wk, k_out), (wv, v_out))):
            out[:, :local] = ref[...]
            out[:, local:] = low(other[:, i * local : (i + 1) * local])
        o_out[:local, :], o_out[local:, :] = wo[...], low(other_o[...])
        ks[:, :local], vs[:, :local] = k[...], v[...]
        for start in range(0, held, CHUNK):
            at = slice(start, start + CHUNK)
            ks[at, local:] = low(dot(normed[at, :], k_out[:, local:]))
            vs[at, local:] = low(dot(normed[at, :], v_out[:, local:]))

    outs = [((width, 2 * local), BF16)] * 3 + [((2 * local, width), BF16)]
    outs += [((held, 2 * local), BF16)] * 2
    return order.call(kernel, outs, [memory_low, memory_k, memory_v, *own, twin_qkv, twin_o])


def gather_feed(order, inner_w, inner_b, outer_w, twin_inner, twin_outer):
    width, units = inner_w.shape

    def kernel(flag, wi, bi, wf, other_i, other_f, i_out, b_out, f_out):
        i_out[:, :units], i_out[:, units:] = wi[...], low(other_i[:width, :])
        b_out[:, :units], b_out[:, units:] = wide(bi[...]), other_i[width : width + 1, :]
        f_out[:units, :], f_out[units:, :] = wf[...], low(other_f[...])

    outs = [((width, 2 * units), BF16), ((1, 2 * units), F32), ((2 * units, width), BF16)]
    return order.call(kernel, outs, [inner_w, inner_b, outer_w, twin_inner, twin_outer])


def project(order, inputs, pieces, index, weights, gain, shift, keep):
    given = len(pieces)
    width, columns = weights[0].shape

    def kernel(*refs):
        flag, x_in = refs[0], refs[1]
        piece_refs, rest = refs[2 : 2 + given], refs[2 + given :]
        gain_ref, shift_ref, wq, wk, wv, x, q, kv, *rest = rest
        own = wide(x_in[chunk_at(index, flag[CORE_AT]), :])
        if given:
            put_pieces(x, piece_refs, flag[ON_AT])
            x[...] = jnp.where(flag[FIRST_AT] == 1, own, x[...])
        else:
            x[...] = own
        hat, inverse = standardize(x[...])
        normed = low(hat * wide(gain_ref[...]) + wide(shift_ref[...]))
        if keep:
            rest[0][...], rest[1][...], rest[2][...] = hat, inverse, normed
        q[...] = low(dot(normed, wq[...]))
        kv[:, :columns] = wide(low(dot(normed, wk[...])))
        kv[:, columns:] = wide(low(dot(normed, wv[...])))

    outs = [((HALF, width), F32), ((HALF, columns), BF16), ((HALF, 2 * columns), F32)]
    if keep:
        outs += [((HALF, width), F32), ((HALF, 1), F32), ((HALF, width), BF16)]
    return order.call(kernel, outs, [inputs, *pieces, gain, shift, *weights])


def swap_halves(value):
    half = value.shape[1] // 2
    return jnp.concatenate([value[:, half:], value[:, :half]], 1)


def spans(past):
    sizes = [k.shape[0] for k, _ in past] + [CHUNK]
    return [sum(sizes[:i]) for i in range(len(sizes))], sizes


def attention(q, parts, starts, sizes, docs_ref, core, lse=None):
    docs_q = own_documents(docs_ref, starts[-1], core)
    mixed = []
    for h in range(q.shape[1] // HEAD_DIM):
        cols = slice(h * HEAD_DIM, (h + 1) * HEAD_DIM)
        scores = [
            masked(
                dot_t(q[:, cols], key[:, cols]),
                docs_q,
                wide(docs_ref[:, start : start + size]),
                core if i == len(parts) - 1 else None,
            )
            for i, ((key, _), start, size) in enumerate(zip(parts, starts, sizes))
        ]
        top = scores[0].max(-1, keepdims=True)
        for score in scores[1:]:
            top = jnp.maximum(top, score.max(-1, keepdims=True))
        total, value_sum = 0.0, 0.0
        for score, (_, value) in zip(scores, parts):
            exps = jnp.exp(score - top)
            total = total + exps.sum(-1, keepdims=True)
            value_sum = value_sum + dot(low(exps), value[:, cols])
        mixed.append(low(value_sum / total))
        if lse is not None:
            lse[:, h : h + 1] = top + jnp.log(total)
    return jnp.concatenate(mixed, 1)


def attend_inputs(order, inputs, index, weights, gain, shift, past, docs, output_w):
    starts, sizes = spans(past)
    width, columns = weights[0].shape

    def kernel(flag, x_in, gain_ref, shift_ref, wq, wk, wv, docs_ref, wo, *rest):
        past_refs, rest = rest[: 2 * len(past)], rest[2 * len(past) :]
        x, k, v, out, normed = rest
        core = flag[CORE_AT]
        x[...] = wide(x_in[chunk_at(index, core), :])
        hat, _ = standardize(wide(x_in[index * CHUNK : (index + 1) * CHUNK, :]))
        normed[...] = low(hat * wide(gain_ref[...]) + wide(shift_ref[...]))
        k[...] = low(dot(normed[...], wk[...]))
        v[...] = low(dot(normed[...], wv[...]))
        q = low(dot(normed[at_rows(core, HALF), :], wq[...]))
        parts = [(past_refs[2 * i], past_refs[2 * i + 1]) for i in range(len(past))] + [(k, v)]
        out[...] = dot(attention(q, parts, starts, sizes, docs_ref, core), wo[...])

    outs = [((HALF, width), F32)] + [((CHUNK, columns), BF16)] * 2 + [((HALF, width), F32)]
    args = [inputs, gain, shift, *weights, docs, output_w] + [item for pair in past for item in pair]
    return order.call(kernel, outs, args, [pltpu.VMEM((CHUNK, width), BF16)], only=1)


def attend_chunk(order, queries, kv, kv_twin, past, docs, output_w):
    starts, sizes = spans(past)
    columns, width = output_w.shape

    def kernel(flag, q, own, other, docs_ref, wo, *rest):
        past_refs, rest = rest[: 2 * len(past)], rest[2 * len(past) :]
        k, v, out, lse, mixed = rest
        core = flag[CORE_AT]
        k[at_rows(core, HALF), :] = low(own[:, :columns])
        v[at_rows(core, HALF), :] = low(own[:, columns:])
        k[at_rows(1 - core, HALF), :] = low(swap_halves(other[:, :columns]))
        v[at_rows(1 - core, HALF), :] = low(swap_halves(other[:, columns:]))
        parts = [(past_refs[2 * i], past_refs[2 * i + 1]) for i in range(len(past))] + [(k, v)]
        mixed[...] = attention(q, parts, starts, sizes, docs_ref, core, lse)
        out[...] = dot(mixed[...], wo[...])

    outs = [((CHUNK, columns), BF16)] * 2 + [((HALF, width), F32)]
    outs += [((HALF, columns // HEAD_DIM), F32), ((HALF, columns), BF16)]
    args = [queries, kv, kv_twin, docs, output_w] + [item for pair in past for item in pair]
    return order.call(kernel, outs, args)


def feed_chunk(order, layer_input, part, arrived, output_b, gain, shift, inner_w, inner_b, outer_w):
    ending = outer_w is not None
    width, units = inner_w.shape

    def kernel(flag, x, a, b, bo, gain_ref, shift_ref, wi, bi, *rest):
        if ending:
            wf, hidden, mine, other, acc = rest
        else:
            hidden, hat_ref, inverse_ref, normed_ref, acts_ref, slope_ref = rest
        hidden[...] = x[...] + (a[...] + b[...] + wide(bo[...]))
        hat, inverse = standardize(hidden[...])
        normed = low(hat * wide(gain_ref[...]) + wide(shift_ref[...]))
        if not ending:
            hat_ref[...], inverse_ref[...], normed_ref[...] = hat, inverse, normed
        for start in range(0, units, TILE):
            tile = slice(start, start + TILE)
            acts, slope = gelu_and_slope(dot(normed, wi[:, tile]) + bi[:, tile])
            if ending:
                term = dot(low(acts), wf[tile, :])
                acc[...] = term if start == 0 else acc[...] + term
            else:
                acts_ref[:, tile] = low(acts)
                slope_ref[:, tile] = slope
        if ending:
            split_rows(acc, mine, other, flag[ON_AT])

    outs = [((HALF, width), F32)]
    if ending:
        outs += [((QUARTER, width), F32)] * 2
    else:
        outs += [
            ((HALF, width), F32),
            ((HALF, 1), F32),
            ((HALF, width), BF16),
            ((HALF, units), BF16),
            ((HALF, units), F32),
        ]
    args = [layer_input, part, arrived, output_b, gain, shift, inner_w, inner_b]
    args += [outer_w] if ending else []
    scratch = [pltpu.VMEM((HALF, width), F32)] if ending else []
    return order.call(kernel, outs, args, scratch, only=1 if ending else None)


def feed_back_chunk(order, cotangent, index, pieces, kept, outer_w, inner_w, final):
    hat, slope = kept
    given = len(pieces)
    units, width = outer_w.shape
    own_units = units // 2

    def kernel(*refs):
        flag, cot = refs[0], refs[1]
        piece_refs, rest = refs[2 : 2 + given], refs[2 + given :]
        slope_ref, wf, wi, *rest = rest
        if final:
            hat_ref, grad_out, out, branch, pre_grad, sums, passed = rest
        else:
            grad_out, out = rest
        own_cot = wide(cot[chunk_at(index, flag[CORE_AT]), :])
        if given:
            put_pieces(grad_out, piece_refs, flag[BACK_AT])
            grad_out[...] = jnp.where(flag[FIRST_AT] == 1, grad_out[...], own_cot)
        else:
            grad_out[...] = own_cot
        branch_grad = low(grad_out[...])
        for start in range(0, units, TILE):
            tile = slice(start, start + TILE)
            grad = low(slope_ref[:, tile] * dot_t(branch_grad, wf[tile, :]))
            if final and start < own_units:
                pre_grad[:, tile] = grad
            elif final:
                passed[HALF:, start - own_units : start - own_units + TILE] = wide(grad)
            term = dot_t(grad, wi[:, tile])
            out[...] = term if start == 0 else out[...] + term
        if final:
            branch[...] = branch_grad
            passed[:HALF, :] = wide(branch_grad)
            sums[0:1, :] = jnp.sum(out[...] * hat_ref[...], 0, keepdims=True)
            sums[1:2, :] = jnp.sum(out[...], 0, keepdims=True)
            sums[2:3, :] = jnp.sum(wide(branch_grad), 0, keepdims=True)
            sums[3:4, :] = jnp.zeros_like(sums[3:4, :])

    outs = [((HALF, width), F32)] * 2
    args = [cotangent, *pieces, slope, outer_w, inner_w]
    if final:
        outs += [((HALF, width), BF16), ((HALF, own_units), BF16), ((4, width), F32)]
        outs += [((CHUNK, width), F32)]
        args += [hat]
    return order.call(kernel, outs, args, only=None if final else 0)


def attend_back_chunk(
    order, grad_out, part, arrived, kept_f, queries, kv, lse, past, docs, output_w, gain_f, later, final
):
    hat_f, inverse_f = kept_f
    starts, sizes = spans(past)
    last = len(past) > 1
    columns, width = output_w.shape
    heads, local = columns // HEAD_DIM, columns // 2
    held, size = sizes[0], starts[-1] + CHUNK
    first_key = 0 if final else held

    def kernel(*refs):
        refs = list(refs)

        def take(count):
            taken = refs[:count]
            del refs[:count]
            return taken

        flag, g_out, a, b, hf, invf, gf, wo, docs_ref, q, k, v, lse_ref = take(13)
        past_refs = take(2 * len(past))
        later_refs = take(len(later))
        hidden_grad, query_rows, own, other = take(4)
        passed = take(1) if last else []
        kept = take(3) if final else []
        (sums,) = take(1)
        core = flag[CORE_AT]
        grad = standardize_back((a[...] + b[...]) * wide(gf[...]), hf[...], invf[...])
        hidden_grad[...] = g_out[...] + grad
        attend_grad = low(hidden_grad[...])
        mixed_grad = low(dot_t(attend_grad, wo[...]))
        parts = [(past_refs[2 * i], past_refs[2 * i + 1]) for i in range(len(past))] + [(k, v)]
        docs_q = own_documents(docs_ref, starts[-1], core)
        for h in range(heads):
            cols = slice(h * HEAD_DIM, (h + 1) * HEAD_DIM)
            value_cols = slice(columns + h * HEAD_DIM, columns + (h + 1) * HEAD_DIM)
            grad = mixed_grad[:, cols]
            probs, probs_grads, inner = [], [], 0.0
            for (key, value), start, length in zip(parts, starts, sizes):
                score = masked(
                    dot_t(q[:, cols], key[:, cols]),
                    docs_q,
                    wide(docs_ref[:, start : start + length]),
                    core if key is k else None,
                )
                probs.append(jnp.exp(score - lse_ref[:, h : h + 1]))
                probs_grads.append(dot_t(grad, value[:, cols]))
                inner = inner + jnp.sum(probs[-1] * probs_grads[-1], -1, keepdims=True)
            query_row = 0.0
            for i, (key, value) in enumerate(parts):
                score_grad = low(probs[i] * (probs_grads[i] - inner))
                query_row = query_row + dot(score_grad, key[:, cols])
                if i == 0 and not final:
                    continue
                at = slice(starts[i] - first_key, starts[i] - first_key + sizes[i])
                sums[at, cols] = t_dot(score_grad, q[:, cols])
                sums[at, value_cols] = t_dot(low(probs[i]), grad)
            query_rows[:, cols] = low(query_row * SCALE)
        chunk = slice(starts[-1] - first_key, size - first_key)
        if last:
            passed[0][...] = sums[starts[1] - first_key : starts[2] - first_key, :]
        else:
            sums[chunk, :] = sums[chunk, :] + later_refs[0][...]
        base = (starts[-1] - first_key) // HALF
        own[...] = sums[at_rows(base + core, HALF), :]
        other[...] = sums[at_rows(base + 1 - core, HALF), :]
        if final:
            kept[0][...] = attend_grad
            for i in range(2):
                for j in range(2):
                    cols = slice(j * columns + i * local, j * columns + (i + 1) * local)
                    total = sums[:held, cols]
                    out_cols = slice(j * local, (j + 1) * local)
                    if not last:
                        total = total + later_refs[1 + i][:, out_cols]
                    kept[1 + i][:, out_cols] = total

    outs = [((HALF, width), F32), ((HALF, columns), BF16)] + [((HALF, 2 * columns), F32)] * 2
    if last:
        outs += [((CHUNK, 2 * columns), F32)]
    if final:
        outs += [((HALF, width), BF16)] + [((held, columns), F32)] * 2
    args = [grad_out, part, arrived, hat_f, inverse_f, gain_f, output_w, docs, queries, *kv, lse]
    args += [item for pair in past for item in pair] + list(later)
    scratch = [pltpu.VMEM((size - first_key, 2 * columns), F32)]
    return order.call(kernel, outs, args, scratch, only=None if final else 0)


def project_back(order, query_rows, own, arrived, weights, hat, final):
    width, columns = weights[0].shape

    def kernel(flag, dq, a, b, wq, wk, wv, *rest):
        key_rows = low((a[:, :columns] + swap_halves(b[:, :columns])) * SCALE)
        value_rows = low(a[:, columns:] + swap_halves(b[:, columns:]))
        out = rest[1] if final else rest[-1]
        out[...] = dot_t(dq[...], wq[...]) + dot_t(key_rows, wk[...])
        out[...] = out[...] + dot_t(value_rows, wv[...])
        if final:
            hat_ref, _, keys_out, values_out, sums = rest
            keys_out[...], values_out[...] = key_rows, value_rows
            sums[0:1, :] = jnp.sum(out[...] * hat_ref[...], 0, keepdims=True)
            sums[1:2, :] = jnp.sum(out[...], 0, keepdims=True)
        else:
            split_rows(out, rest[0], rest[1], flag[BACK_AT])

    args = [query_rows, own, arrived, *weights]
    if final:
        outs = [((HALF, width), F32)] + [((HALF, columns), BF16)] * 2 + [((2, width), F32)]
        return order.call(kernel, outs, args + [hat])
    outs = [((QUARTER, width), F32)] * 2
    return order.call(kernel, outs, args, [pltpu.VMEM((HALF, width), F32)], only=0)


def add(order, *terms):
    def kernel(flag, *refs):
        total = refs[0][...]
        for ref in refs[1:-1]:
            total = total + ref[...]
        refs[-1][...] = total

    return order.call(kernel, [(terms[0].shape, F32)], terms)[0]


def finish_forward(order, mine, arrived, hidden, outer_b):
    def kernel(flag, a, b, h, bias, out):
        out[...] = a[...] + b[...] + h[at_rows(flag[ON_AT], QUARTER), :] + wide(bias[...])

    return order.call(kernel, [(mine.shape, F32)], [mine, arrived, hidden, outer_b])[0]


def finish_backward(order, mine, arrived, hat, inverse, hidden_grad, gain):
    def kernel(flag, a, b, hat_ref, inverse_ref, h, gain_ref, out):
        at = at_rows(flag[BACK_AT], QUARTER)
        grad = (a[...] + b[...]) * wide(gain_ref[...])
        out[...] = h[at, :] + standardize_back(grad, hat_ref[at, :], inverse_ref[at, :])

    args = [mine, arrived, hat, inverse, hidden_grad, gain]
    return order.call(kernel, [(mine.shape, F32)], args)[0]


def pick(order, arrived, own, receiver):
    def kernel(flag, a, b, out):
        out[...] = jnp.where(flag[FIRST_AT] == receiver, a[...], b[...])

    return order.call(kernel, [(own.shape, F32)], [arrived, own])[0]


def squeeze(order, memory, older, weight, bias):
    local = weight.shape[-1]

    def kernel(flag, memory_ref, older_ref, w, b, out):
        row = lax.broadcasted_iota(jnp.int32, (COMP, memory.shape[0]), 0)
        col = lax.broadcasted_iota(jnp.int32, (COMP, memory.shape[0]), 1)
        total = wide(b[...])
        for r in range(RATE):
            chosen = low(wide((col == row * RATE + r).astype(jnp.int32)))
            total = total + dot(low(dot(chosen, memory_ref[...])), w[r])
        out[:COMP, :] = older_ref[COMP:, at_rows(flag[MEMBER_AT], local)]
        out[COMP:, :] = low(total)

    return order.call(kernel, [((2 * COMP, local), BF16)], [memory, older, weight, bias])[0]


def memory_sums(order, older, memory, keys_grad, values_grad, key_w, value_w):
    def kernel(flag, older_ref, memory_ref, kg, vg, wk, wv, out):
        out[...] = jnp.zeros_like(out)
        for i, source in enumerate((older_ref, memory_ref)):
            for start in range(0, source.shape[0], CHUNK):
                hat, _ = standardize(wide(source[start : start + CHUNK, :]))
                at = slice(i * source.shape[0] + start, i * source.shape[0] + start + CHUNK)
                grad = dot_t(kg[at, :], wk[...]) + dot_t(vg[at, :], wv[...])
                out[0:1, :] = out[0:1, :] + jnp.sum(grad * hat, 0, keepdims=True)
                out[1:2, :] = out[1:2, :] + jnp.sum(grad, 0, keepdims=True)

    width, local = key_w.shape
    args = [older, memory, keys_grad, values_grad, key_w, value_w]
    return order.call(kernel, [((2, width), F32)], args)[0]


def block_at(index):
    return at_rows(index % 4, BLOCK)


def sub_at(index):
    return at_rows(index % 4, SUB)


def ring_sum(order, operands, make, columns, outs, place, extra=None, more=0):
    def rows_of(count, added=0):
        return ((count + added, columns), F32)

    blocks = [pltpu.VMEM((2, BLOCK, columns), F32)]

    def both(upward, up_moves, downward, down_moves):
        upward, downward = after((upward, downward), order.flags)
        return send(upward, up_moves), send(downward, down_moves)

    def far_kernel(flag, *refs):
        for q in range(2):
            refs[-2 + q][...] = make(refs, q, flag[RING_AT] + 2)

    far = order.call(far_kernel, [rows_of(BLOCK)] * 2, operands)
    yield
    below, above = both(far[0], UP, far[1], DOWN)
    yield

    def next_kernel(flag, *refs):
        below_ref, above_ref, up_ref, down_ref = refs[-4:]
        here = flag[RING_AT]
        up_ref[:BLOCK, :] = make(refs, 0, here + 1) + below_ref[...]
        up_ref[BLOCK:, :] = make(refs, 1, here + 1)
        down_ref[:BLOCK, :] = make(refs, 0, here + 3)
        down_ref[BLOCK:, :] = make(refs, 1, here + 3) + above_ref[...]

    up, down = order.call(next_kernel, [rows_of(2 * BLOCK)] * 2, [*operands, below, above])
    yield
    below, above = both(up, UP, down, DOWN)
    yield

    def own_kernel(flag, *refs):
        below_ref, above_ref, far_p, far_q, up_ref, down_ref, own_ref, acc = refs[-8:]
        here, there = flag[RING_AT], flag[RING2_AT]
        for q in range(2):
            at = slice(q * BLOCK, (q + 1) * BLOCK)
            acc[q] = make(refs, q, here) + below_ref[at, :] + above_ref[at, :]
            half = slice(q * SUB, (q + 1) * SUB)
            (far_p, far_q)[q][...] = acc[q, sub_at(there + 2), :]
            up_ref[half, :] = acc[q, sub_at(there + 1), :]
            down_ref[half, :] = acc[q, sub_at(there + 3), :]
            own_ref[half, :] = acc[q, sub_at(there), :]

    far_p, far_q, up, down, own = order.call(
        own_kernel,
        [rows_of(SUB)] * 2 + [rows_of(2 * SUB)] * 3,
        [*operands, below, above],
        scratch=blocks,
    )
    yield
    below, above = both(far_p, UP2, far_q, DOWN2)
    yield

    def next_small(flag, up_in, down_in, below_ref, above_ref, up_ref, down_ref):
        up_ref[:SUB, :], up_ref[SUB:, :] = up_in[:SUB, :] + below_ref[...], up_in[SUB:, :]
        down_ref[:SUB, :], down_ref[SUB:, :] = down_in[:SUB, :], down_in[SUB:, :] + above_ref[...]

    up, down = order.call(next_small, [rows_of(2 * SUB)] * 2, [up, down, below, above])
    yield
    below, above = both(up, UP2, down, DOWN2)
    yield
    extras = [] if extra is None else [extra()]

    def own_small(flag, own_ref, below_ref, above_ref, *rest):
        out = rest[-1]
        out[: 2 * SUB, :] = own_ref[...] + below_ref[...] + above_ref[...]
        if more:
            out[2 * SUB :, :] = rest[0][...]

    own = order.call(own_small, [rows_of(2 * SUB, more)], [own, below, above, *extras])[0]
    yield
    below, above = both(own, UP2, own, DOWN2)
    yield

    def pass_on(count):
        def kernel(flag, own_ref, below_ref, above_ref, up_ref, down_ref):
            rest = slice(2 * count, None)
            up_ref[:count, :], down_ref[:count, :] = below_ref[:count, :], above_ref[count : 2 * count, :]
            if more:
                up_ref[count:, :] = below_ref[rest, :]
                down_ref[count:, :] = own_ref[rest, :] + below_ref[rest, :] + above_ref[rest, :]

        return kernel

    up, down = order.call(pass_on(SUB), [rows_of(SUB, more)] * 2, [own, below, above])
    yield
    far_p, far_q = both(up, UP2, down, DOWN2)
    yield

    def join(flag, own_ref, below_ref, above_ref, far_p_ref, far_q_ref, *rest):
        out, acc = rest[-2:]
        there = flag[RING2_AT]
        for q, far_ref in enumerate((far_p_ref, far_q_ref)):
            half = slice(q * SUB, (q + 1) * SUB)
            acc[q, sub_at(there), :] = own_ref[half, :]
            acc[q, sub_at(there + 3), :] = below_ref[half, :]
            acc[q, sub_at(there + 1), :] = above_ref[half, :]
            acc[q, sub_at(there + 2), :] = far_ref[:SUB, :]
            out[q * BLOCK : (q + 1) * BLOCK, :] = acc[q]
        if more:
            out[2 * BLOCK :, :] = rest[0][SUB:, :] + far_p_ref[SUB:, :]

    sums = [down] if more else []
    total = order.call(
        join, [rows_of(2 * BLOCK, more)], [own, below, above, far_p, far_q, *sums], blocks
    )[0]
    yield
    below, above = both(total, UP, total, DOWN)
    yield
    up, down = order.call(pass_on(BLOCK), [rows_of(BLOCK, more)] * 2, [total, below, above])
    yield
    far_p, far_q = both(up, UP, down, DOWN)
    yield

    copies = len(place(0, 0)) + len(place(1, 0))

    def run(moves, sems):
        started = [pltpu.make_async_copy(a, b, sems.at[i]) for i, (a, b) in enumerate(moves)]
        for copy in started:
            copy.start()
        for copy in started:
            copy.wait()

    def moves_of(piece, start, q, index, out_refs):
        return [
            (piece.at[start : start + BLOCK, cols], out_refs[out].at[to])
            for cols, out, to in place(q, index)
        ]

    def first_writes(flag, own_ref, below_ref, above_ref, *rest):
        out_refs, sems = rest[:-1], rest[-1]
        here = flag[RING_AT]
        moves = []
        for piece, index in ((own_ref, here), (below_ref, here + 3), (above_ref, here + 1)):
            for q in range(2):
                moves += moves_of(piece, q * BLOCK, q, index, out_refs)
        run(moves, sems)

    outs = [(shape, F32) for shape in outs]
    results = order.call(
        first_writes,
        outs,
        [total, below, above],
        [pltpu.SemaphoreType.DMA((3 * copies,))],
        out_specs=[ANYWHERE] * len(outs),
    )
    yield

    def last_writes(flag, far_p_ref, far_q_ref, *rest):
        out_refs, sems = rest[len(outs) : -1], rest[-1]
        index = flag[RING_AT] + 2
        moves = moves_of(far_p_ref, 0, 0, index, out_refs)
        moves += moves_of(far_q_ref, 0, 1, index, out_refs)
        run(moves, sems)

    results = order.call(
        last_writes,
        outs,
        [far_p, far_q, *results],
        [pltpu.SemaphoreType.DMA((copies,))],
        specs=[WHOLE] * 2 + [ANYWHERE] * len(outs),
        out_specs=[ANYWHERE] * len(outs),
        aliases={3 + i: i for i in range(len(outs))},
    )
    if not more:
        return results

    def last_sum(flag, down_ref, far_ref, out):
        out[...] = down_ref[BLOCK:, :] + far_ref[BLOCK:, :]

    return [*results, order.call(last_sum, [rows_of(more)], [down, far_p])[0]]


class Task:
    def __init__(self, steps):
        self.steps, self.result, self.ended = steps, None, False

    def step(self, count=1):
        for _ in range(count):
            if not self.ended:
                try:
                    next(self.steps)
                except StopIteration as end:
                    self.result, self.ended = end.value, True
        return self.result

    def finish(self):
        while not self.ended:
            self.step()
        return self.result


def body(
    inputs,
    memories,
    compressed,
    documents,
    cotangent,
    compressed_cotangent,
    query_weight,
    key_weight,
    value_weight,
    output_weight,
    output_bias,
    inner_weight,
    inner_bias,
    outer_weight,
    outer_bias,
    conv_weight,
    conv_bias,
    attn_gain,
    attn_shift,
    ffn_gain,
    ffn_shift,
):
    section = lax.axis_index("pipe")
    group = lax.axis_index("dp")
    member = lax.axis_index("tensor")
    core, chip = member % 2, member // 2
    on_place = jnp.where(section == 0, chip, 1 - chip)
    y, z = group // 4, group % 4
    ring, ring2 = jnp.where(core == 0, y, z), jnp.where(core == 0, z, y)
    order = Order(
        jnp.stack([core, on_place, 1 - on_place, 1 - section, ring, ring2, member]).astype(jnp.int32)
    )
    width = inputs.shape[1]
    local = query_weight.shape[2]
    units = inner_weight.shape[2]
    held = documents.shape[1] - SEG
    chunks = range(SEG // CHUNK)
    both = CHUNK * len(chunks) // 2
    own_qkv = (query_weight[0], key_weight[0], value_weight[0])
    key_w, value_w = key_weight[0], value_weight[0]
    norm_a, norm_f = (attn_gain, attn_shift), (ffn_gain, ffn_shift)
    memory, older = memories[0, 0], compressed[0, 0]
    squeeze_cot = compressed_cotangent[0, 0]

    twin_qkv = send(widen(order, own_qkv), CORE)
    twin_o = send(widen(order, [output_weight[0]]), CORE)
    memory_low, memory_k, memory_v = prepare_memory(order, older, memory, *norm_a, key_w, value_w)
    *qkv_w, output_w, memory_k, memory_v = gather_projections(
        order, memory_low, memory_k, memory_v, (*own_qkv, output_weight[0]), twin_qkv, twin_o
    )
    past_memory = (memory_k, memory_v)

    twin_inner = send(widen_with_row(order, inner_weight[0], inner_bias), CORE)
    twin_outer = send(widen(order, [outer_weight[0]]), CORE)
    attended, past = [], [past_memory]
    for i in chunks:
        made = attend_inputs(order, inputs, i, qkv_w, *norm_a, past, documents, output_w)
        past = past + [tuple(made[1:3])]
        attended.append((made[0], made[3], send(made[3], CHIP)))
    inner_w, inner_b, outer_w = gather_feed(
        order, inner_weight[0], inner_bias, outer_weight[0], twin_inner, twin_outer
    )
    weights_f = (output_bias, *norm_f, inner_w, inner_b)
    hidden, mine, arrived, total, arriving = ([None, None] for _ in range(5))
    for i in chunks:
        hidden[i], mine[i], other = feed_chunk(
            order, *attended[i], *weights_f, outer_w
        )
        arrived[i] = send(other, CHIP)
    for i in chunks:
        total[i] = finish_forward(order, mine[i], arrived[i], hidden[i], outer_bias)
        arriving[i] = send(total[i], ONWARD)


    forward = []
    for i in chunks:
        piece = pick(order, arriving[i], total[i], 0)
        forward.append([piece, send(piece, CHIP)])
    kept_p, kept_a, pasts = [], [], [[past_memory]]
    for i in chunks:
        made = project(order, inputs, forward[i], i, qkv_w, *norm_a, True)
        kept_p.append((*made, send(made[2], CORE)))
    for i in chunks:
        x, q, kv = kept_p[i][:3]
        made = attend_chunk(order, q, kv, kept_p[i][-1], pasts[i], documents, output_w)
        pasts.append(pasts[i] + [tuple(made[:2])])
        kept_a.append((*made, send(made[2], CHIP)))
    kept_f, fed = [], []
    for i in chunks:
        kept_f.append(
            feed_chunk(order, kept_p[i][0], kept_a[i][2], kept_a[i][-1], *weights_f, None)
        )
        grad_out, out = feed_back_chunk(
            order, cotangent, i, [], (kept_f[i][1], kept_f[i][5]), outer_w, inner_w, False
        )
        fed.append((grad_out, out, send(out, CHIP)))

    def pack_rows(flag, *refs):
        out = refs[-1]
        for i, ref in enumerate(refs[:-1]):
            out[i * HALF : (i + 1) * HALF, :] = wide(ref[:, -width:])

    def attend_back(i, grad_out, out, arrived, later, final, core_moves):
        made = attend_back_chunk(
            order,
            grad_out,
            out,
            arrived,
            kept_f[i][1:3],
            kept_p[i][1],
            kept_a[i][:2],
            kept_a[i][3],
            pasts[i],
            documents,
            output_w,
            ffn_gain,
            later,
            final,
        )
        return made, send(made[3], core_moves)

    back, arrived, mine, total, backward = ([None, None] for _ in range(5))

    def begin_back(i, later):
        back[i], arrived[i] = attend_back(i, *fed[i], later, False, CORE)

    def middle_back(i):
        mine[i], other = project_back(
            order, back[i][1], back[i][2], arrived[i], qkv_w, None, False
        )
        arrived[i] = send(other, CHIP)

    def end_back(i):
        total[i] = finish_backward(
            order, mine[i], arrived[i], kept_p[i][3], kept_p[i][4], back[i][0], attn_gain
        )
        arriving[i] = send(total[i], BACK)

    def receive_back(i):
        piece = pick(order, arriving[i], total[i], 1)
        backward[i] = [piece, send(piece, CHIP)]

    begin_back(1, [])
    begin_back(0, [back[1][4]])
    middle_back(1)
    middle_back(0)
    args = [kept_f[i][4] for i in chunks] + [kept_f[i][3] for i in chunks]
    args += [kept_p[i][5] for i in chunks]
    twin_rows = send(order.call(pack_rows, [((len(args) * HALF, width), F32)], args)[0], CORE)


    end_back(1)
    end_back(0)
    receive_back(1)
    receive_back(0)

    def unpack_rows(flag, *refs):
        parts, arrived_ref, outs = refs[:6], refs[6], refs[7:]
        for i, out in enumerate(outs):
            out[:HALF, :] = parts[2 * i][:, :width]
            out[HALF : 2 * HALF, :] = parts[2 * i + 1][:, :width]
            out[2 * HALF :, :] = low(arrived_ref[2 * i * HALF : 2 * (i + 1) * HALF, :])

    acts_all, normed_f_all, normed_all = order.call(
        unpack_rows, [((SEG, width), BF16)] * 3, [*args, twin_rows]
    )
    made = [None, None]
    for i in reversed(chunks):
        made[i] = feed_back_chunk(
            order, cotangent, i, backward[i], (kept_f[i][1], kept_f[i][5]), outer_w, inner_w, True
        )
        arrived[i] = send(made[i][5], CORE)
        fed[i] = (made[i][0], made[i][1], send(made[i][1], CHIP))

    def unpack_feed(flag, b0, b1, p0, p1, a0, a1, branch, pre, sums):
        for i, (ref, out) in enumerate(((b0, branch), (b1, branch), (p0, pre), (p1, pre))):
            start = i % 2 * HALF
            out[start : start + HALF, :] = ref[...]
        for i, ref in enumerate((a0, a1)):
            at = slice((2 + i) * HALF, (3 + i) * HALF)
            branch[at, :], pre[at, :] = low(ref[:HALF, :]), low(ref[HALF:, :])
        sums[...] = jnp.sum(wide(pre[...]), 0, keepdims=True)

    branch_all, pre_all, pre_sum = order.call(
        unpack_feed,
        [((SEG, width), BF16), ((SEG, units), BF16), ((1, units), F32)],
        [made[0][2], made[1][2], made[0][3], made[1][3], *arrived],
    )

    def make_feed(refs, q, index):
        acts, branch, normed, pre = refs[:4]
        left, right = (normed, pre) if q else (acts, branch)
        return t_dot(left[:, block_at(index)], right[...])

    def place_feed(q, index):
        return [(slice(None), q, (block_at(index),))]

    feeding = Task(
        ring_sum(
            order,
            [acts_all, branch_all, normed_f_all, pre_all],
            make_feed,
            width,
            [(width, width)] * 2,
            place_feed,
        )
    )
    def assemble(own):
        arrived = send(own, CORE)
        yield

        def kernel(flag, a, b, out):
            for i in chunks:
                at = slice(i * HALF, (i + 1) * HALF)
                out[chunk_at(i, flag[CORE_AT]), :] = a[at, :]
                out[chunk_at(i, 1 - flag[CORE_AT]), :] = b[at, :]

        return order.call(kernel, [((SEG, width), F32)], [own, arrived])[0]

    def layer_output():
        def kernel(flag, a0, a1, wf, out):
            for i, ref in enumerate((a0, a1)):
                out[i * HALF : (i + 1) * HALF, :] = dot(ref[...], wf[...])

        args = [kept_f[i][4] for i in chunks] + [outer_w]
        out = order.call(kernel, [((both, width), F32)], args)[0]
        yield
        arrived = send(after(out, order.flags), CHIP)
        yield

        def kernel(flag, a, b, bias, *refs):
            out, acc = refs[-2:]
            for i in chunks:
                hidden_ref, *pieces = refs[3 * i : 3 * i + 3]
                put_pieces(acc, pieces, flag[ON_AT])
                at = slice(i * HALF, (i + 1) * HALF)
                total = hidden_ref[...] + (a[at, :] + b[at, :] + wide(bias[...]))
                out[at, :] = jnp.where(flag[FIRST_AT] == 1, acc[...], total)

        args = [out, arrived, outer_bias]
        for i in chunks:
            args += [kept_f[i][0], *forward[i]]
        scratch = [pltpu.VMEM((HALF, width), F32)]
        own = order.call(kernel, [((both, width), F32)], args, scratch)[0]
        return (yield from assemble(own))

    def pack_attend(flag, *refs):
        *heads, attend_grad, out = refs
        for j, ref in enumerate(heads):
            out[:HALF, j * local : (j + 1) * local] = wide(ref[:, local:])
        out[HALF:, :] = wide(attend_grad[...])

    feeding.step(2)
    projected, heads, twin_heads = ([None, None] for _ in range(3))

    def begin_last(i, later):
        back[i], arrived[i] = attend_back(i, *fed[i], later, True, CORE)

    def end_last(i):
        projected[i] = project_back(
            order, back[i][1], back[i][2], arrived[i], qkv_w, kept_p[i][3], True
        )
        attend_grad = back[i][5 if i else 4]
        heads[i] = [back[i][1], projected[i][1], projected[i][2], kept_a[i][4], attend_grad]
        packed = order.call(pack_attend, [((CHUNK, width), F32)], heads[i])[0]
        twin_heads[i] = send(packed, CORE)

    begin_last(1, [])
    end_last(1)
    feeding.step(2)
    begin_last(0, [back[1][4], *back[1][6:8]])
    kept = [back[0][4:], back[1][5:]]
    twin_memory = send(kept[0][2], CORE)
    end_last(0)
    outward = Task(layer_output())
    outward.step()
    feeding.step(2)

    def unpack_attend(flag, *refs):
        *outs, attend_out = refs[12:]
        for i in chunks:
            *parts, attend_grad, arrived_ref = refs[6 * i : 6 * i + 6]
            own, twin = i * HALF, (2 + i) * HALF
            for j, (ref, out) in enumerate(zip(parts, outs)):
                out[own : own + HALF, :] = ref[:, :local]
                out[twin : twin + HALF, :] = low(arrived_ref[:HALF, j * local : (j + 1) * local])
            attend_out[own : own + HALF, :] = attend_grad[...]
            attend_out[twin : twin + HALF, :] = low(arrived_ref[HALF:, :])

    def unpack_memory(flag, mine_ref, memory_ref, keys_out, values_out):
        keys_out[...] = low((mine_ref[:, :local] + memory_ref[:, :local]) * SCALE)
        values_out[...] = low(mine_ref[:, local:] + memory_ref[:, local:])

    *heads_all, attend_all = order.call(
        unpack_attend,
        [((SEG, local), BF16)] * 4 + [((SEG, width), BF16)],
        [item for i in chunks for item in (*heads[i], twin_heads[i])],
    )
    memory_kg, memory_vg = order.call(
        unpack_memory, [((held, local), BF16)] * 2, [kept[0][1], twin_memory]
    )
    def small_sums():
        sums_m = memory_sums(order, older, memory, memory_kg, memory_vg, key_w, value_w)

        def pack(flag, a0, a1, m, f0, f1, g0, g1, pre, cot, out):
            out[0:2, :] = a0[...] + a1[...] + m[...]
            out[2:4, :] = f0[0:2, :] + f1[0:2, :]
            out[4:5, :] = jnp.sum(wide(g0[...]) + wide(g1[...]), 0, keepdims=True)
            out[5:6, :] = f0[2:3, :] + f1[2:3, :]
            out[6:7, :] = pre[...]
            out[7:8, :] = jnp.zeros_like(out[7:8, :])
            out[7:8, :local] = jnp.sum(wide(cot[...]), 0, keepdims=True)

        args = [projected[0][3], projected[1][3], sums_m, made[0][4], made[1][4]]
        args += [kept[0][0], kept[1][0], pre_sum, squeeze_cot]
        own = order.call(pack, [((8, width), F32)], args)[0]
        arrived = send(own, CORE)
        yield
        pair = add(order, own, arrived)
        arrived = send(pair, CHIP)
        yield

        def choose(flag, a, b, own_ref, out):
            out[...] = jnp.zeros_like(out)
            for i in range(2):
                at, to = slice(i * width // 2, (i + 1) * width // 2), slice(0, width // 2)
                out[8 * i : 8 * i + 4, to] = a[0:4, at] + b[0:4, at]
                out[8 * i + 4 : 8 * i + 6, to] = a[4:6, at]
                out[8 * i + 6 : 8 * i + 8, to] = own_ref[6:8, at]

        return order.call(choose, [((16, 3 * local), F32)], [pair, arrived, own])[0]

    sums = Task(small_sums())

    def make_attend(refs, q, index):
        at = block_at(index)
        memory_ref, normed = refs[0], refs[1]
        dq, dk, dv, mixed, attend_grad, memory_keys, memory_values, segment, cot = refs[2:11]
        row = lax.broadcasted_iota(jnp.int32, (SEG, COMP), 0)
        col = lax.broadcasted_iota(jnp.int32, (SEG, COMP), 1)
        chosen = low(wide((row == col * RATE + q).astype(jnp.int32)))
        three = t_dot(segment[:, at], low(dot(chosen, cot[...])))
        if q:
            one = t_dot(mixed[...], attend_grad[:, at])
            two = t_dot(memory_ref[:, at], memory_values[...]) + t_dot(normed[:, at], dv[...])
        else:
            one = t_dot(normed[:, at], dq[...])
            two = t_dot(memory_ref[:, at], memory_keys[...]) + t_dot(normed[:, at], dk[...])
        return jnp.concatenate([one, two, three], 1)

    def place_attend(q, index):
        at = block_at(index)
        one, two, three = (slice(i * local, (i + 1) * local) for i in range(3))
        if q:
            return [(one, 3, (slice(None), at)), (two, 2, (at,)), (three, 4, (q, at))]
        return [(one, 0, (at,)), (two, 1, (at,)), (three, 4, (q, at))]

    attending = Task(
        ring_sum(
            order,
            [
                memory_low,
                normed_all,
                *heads_all,
                attend_all,
                memory_kg,
                memory_vg,
                memory,
                squeeze_cot,
            ],
            make_attend,
            3 * local,
            [(width, local)] * 3 + [(local, width), (RATE, width, local)],
            place_attend,
            sums.finish,
            16,
        )
    )

    def input_gradient():
        def kernel(flag, a0, a1, out):
            out[:HALF, :], out[HALF:, :] = a0[...], a1[...]

        args = [projected[i][0] for i in chunks]
        out = order.call(kernel, [((both, width), F32)], args)[0]
        yield
        arrived = send(after(out, order.flags), CHIP)
        yield

        def kernel(flag, a, b, gain, *refs):
            out, acc = refs[-2:]
            for i in chunks:
                hat, inverse, hidden_grad, *pieces = refs[5 * i : 5 * i + 5]
                put_pieces(acc, pieces, flag[BACK_AT])
                at = slice(i * HALF, (i + 1) * HALF)
                grad = (a[at, :] + b[at, :]) * wide(gain[...])
                grad = hidden_grad[...] + standardize_back(grad, hat[...], inverse[...])
                out[at, :] = jnp.where(flag[FIRST_AT] == 1, grad, acc[...])

        args = [out, arrived, attn_gain]
        for i in chunks:
            args += [kept_p[i][3], kept_p[i][4], back[i][0], *backward[i]]
        scratch = [pltpu.VMEM((HALF, width), F32)]
        own = order.call(kernel, [((both, width), F32)], args, scratch)[0]
        return (yield from assemble(own))

    inward = Task(input_gradient())
    attending.step(2)
    feeding.step(4)
    attending.step(2)
    feeding.step(2)
    feeding.step(2)
    sums.step()
    attending.step(2)
    sums.step()
    attending.step(2)
    sums.finish()
    outward.step()
    attending.step(2)
    feeding.step(2)
    feeding.step()
    attending.step(2)
    attending.step(2)
    outer_g, inner_g = feeding.finish()
    outward.step()
    inward.step(2)
    new_compressed = squeeze(order, memory, older, conv_weight[0], conv_bias)
    outward.finish()
    attending.step(2)
    attending.step()
    query_g, key_g, value_g, output_g, conv_g, total = attending.finish()
    inward.finish()

    def unpack(flag, rows_ref, *outs):
        for r, out in enumerate(outs):
            size = min(out.shape[1], width // 2)
            out[:, :size] = rows_ref[r : r + 1, :size]
            if size < out.shape[1]:
                out[:, size:] = rows_ref[8 + r : 9 + r, :size]

    total = order.call(unpack, [((1, width), F32)] * 7 + [((1, local), F32)], [total])
    return (
        outward.result[None],
        new_compressed[None, None],
        inward.result[None],
        query_g[None],
        key_g[None],
        value_g[None],
        output_g[None],
        total[4],
        inner_g[None],
        total[6],
        outer_g[None],
        total[5],
        conv_g[None],
        total[7],
        total[0],
        total[1],
        total[2],
        total[3],
    )


def solution(mesh):
    return jax.shard_map(
        body,
        mesh=mesh,
        in_specs=(
            P("dp", None),
            P("pipe", "dp", None, None),
            P("pipe", "dp", None, None),
            P("dp", None),
            P("dp", None),
            P("pipe", "dp", None, "tensor"),
            P("pipe", None, "tensor"),
            P("pipe", None, "tensor"),
            P("pipe", None, "tensor"),
            P("pipe", "tensor", None),
            P("pipe", None),
            P("pipe", None, "tensor"),
            P("pipe", "tensor"),
            P("pipe", "tensor", None),
            P("pipe", None),
            P("pipe", None, None, "tensor"),
            P("pipe", "tensor"),
            P("pipe", None),
            P("pipe", None),
            P("pipe", None),
            P("pipe", None),
        ),
        out_specs=(
            P("pipe", "dp", None),
            P("pipe", "dp", None, "tensor"),
            P("pipe", "dp", None),
            P("pipe", None, "tensor"),
            P("pipe", None, "tensor"),
            P("pipe", None, "tensor"),
            P("pipe", "tensor", None),
            P("pipe", None),
            P("pipe", None, "tensor"),
            P("pipe", "tensor"),
            P("pipe", "tensor", None),
            P("pipe", None),
            P("pipe", None, None, "tensor"),
            P("pipe", "tensor"),
            P("pipe", None),
            P("pipe", None),
            P("pipe", None),
            P("pipe", None),
        ),
        check_vma=False,
    )
```

```python
import jax
import jax.numpy as jnp
from jax import lax
from jax.experimental import pallas as pl
from jax.experimental.pallas import tpu as pltpu
from jax.sharding import PartitionSpec as P

HEAD_DIM = 128
SEG = 512
RATE = 2
COMP = 256
CHUNK = 256
HALF = 128
QUARTER = 64
TILE = 256
BLOCK = 256
SUB = 64
HEADS = 2
SCALE = HEAD_DIM ** (-0.5)
LIMIT = 10 * 2**20
AXES = ("pipe", "dp", "tensor")


def pairs(move):
    found = []
    for p in range(2):
        for y in range(4):
            for z in range(4):
                for x in range(2):
                    for c in range(2):
                        there = move(p, y, z, x, c)
                        if there is None:
                            continue
                        q, v, w, u, d = there
                        source = ((p * 4 + y) * 4 + z) * 4 + x * 2 + c
                        target = ((q * 4 + v % 4) * 4 + w % 4) * 4 + u * 2 + d
                        found.append((source, target))
    return found


CORE = pairs(lambda p, y, z, x, c: (p, y, z, x, 1 - c))
CHIP = pairs(lambda p, y, z, x, c: (p, y, z, 1 - x, c))
ONWARD = pairs(lambda p, y, z, x, c: (1, y, z, 1 - x, c) if p == 0 else None)
BACK = pairs(lambda p, y, z, x, c: (0, y, z, 1 - x, c) if p == 1 else None)
UP = pairs(lambda p, y, z, x, c: (p, y + 1 - c, z + c, x, c))
DOWN = pairs(lambda p, y, z, x, c: (p, y + 3 * (1 - c), z + 3 * c, x, c))
UP2 = pairs(lambda p, y, z, x, c: (p, y + c, z + 1 - c, x, c))
DOWN2 = pairs(lambda p, y, z, x, c: (p, y + 3 * c, z + 3 * (1 - c), x, c))
ONE = pairs(lambda p, y, z, x, c: (p, y ^ (1 - c), z ^ c, x, c))
TWO = pairs(lambda p, y, z, x, c: (p, y ^ (2 * (1 - c)), z ^ (2 * c), x, c))
ONE2 = pairs(lambda p, y, z, x, c: (p, y ^ c, z ^ (1 - c), x, c))
TWO2 = pairs(lambda p, y, z, x, c: (p, y ^ (2 * c), z ^ (2 * (1 - c)), x, c))


def low(value):
    return value.astype(jnp.bfloat16)


def wide(value):
    return value.astype(jnp.float32)


def send(value, moves):
    return lax.ppermute(value, AXES, moves)


def after(value, anchor):
    return lax.optimization_barrier((value, anchor))[0]


def dot(left, right):
    return jnp.dot(left, right, preferred_element_type=jnp.float32)


def dot_t(left, right):
    return lax.dot_general(
        left, right, (((1,), (1,)), ((), ())), preferred_element_type=jnp.float32
    )


def t_dot(left, right):
    return lax.dot_general(
        left, right, (((0,), (0,)), ((), ())), preferred_element_type=jnp.float32
    )


def standardize(values):
    centered = values - jnp.mean(values, -1, keepdims=True)
    variance = jnp.mean(centered * centered, -1, keepdims=True)
    inverse = lax.rsqrt(variance + 1e-05)
    return centered * inverse, inverse


def standardize_back(grad, hat, inverse):
    return inverse * (
        grad
        - jnp.mean(grad, -1, keepdims=True)
        - hat * jnp.mean(grad * hat, -1, keepdims=True)
    )


def gelu_and_slope(value):
    square = value * value
    curve = jnp.tanh(0.7978845608028654 * value * (1.0 + 0.044715 * square))
    up = 0.5 + 0.5 * curve
    slope = up + (0.5 * value) * (1.0 - curve * curve) * (
        0.7978845608028654 + (3 * 0.044715 * 0.7978845608028654) * square
    )
    return value * up, slope


F32, BF16 = jnp.float32, jnp.bfloat16
WHOLE = pl.BlockSpec(memory_space=pltpu.VMEM)
SCALAR = pl.BlockSpec(memory_space=pltpu.SMEM)
ANYWHERE = pl.BlockSpec(memory_space=pl.ANY)
OUTSIDE = pl.BlockSpec(memory_space=pltpu.HBM)
CORE_AT, ON_AT, BACK_AT, FIRST_AT, RING_AT, RING2_AT, MEMBER_AT = range(7)


class Order:
    def __init__(self, flags):
        self.flags = flags

    def then(self, anchor):
        self.flags = after(self.flags, anchor)

    def call(
        self, kernel, outs, args, scratch=(), specs=None, out_specs=None, aliases=None, limit=LIMIT, only=None
    ):
        args = [self.flags, *args]
        whole = kernel
        if only is not None:

            def kernel(flag, *refs):
                @pl.when(flag[FIRST_AT] == only)
                def _():
                    whole(flag, *refs)

        results = pl.pallas_call(
            kernel,
            out_shape=[jax.ShapeDtypeStruct(shape, dtype) for shape, dtype in outs],
            in_specs=[SCALAR] + (specs or [WHOLE] * (len(args) - 1)),
            out_specs=out_specs or [WHOLE] * len(outs),
            scratch_shapes=list(scratch),
            input_output_aliases=aliases or {},
            compiler_params=pltpu.CompilerParams(vmem_limit_bytes=limit),
            cost_estimate=pl.CostEstimate(flops=1, bytes_accessed=1, transcendentals=0),
        )(*args)
        self.then(tuple(results))
        return results


def at_rows(index, size):
    return pl.ds(pl.multiple_of(index * size, size), size)


def chunk_at(index, core):
    return pl.ds(pl.multiple_of(index * CHUNK + core * HALF, HALF), HALF)


def put_pieces(out_ref, pieces, place):
    out_ref[at_rows(place, QUARTER), :] = pieces[0][...]
    out_ref[at_rows(1 - place, QUARTER), :] = pieces[1][...]


def split_rows(value_ref, mine_ref, other_ref, place):
    mine_ref[...] = value_ref[at_rows(place, QUARTER), :]
    other_ref[...] = value_ref[at_rows(1 - place, QUARTER), :]


def own_documents(docs, start, core):
    row = lax.broadcasted_iota(jnp.int32, (HALF, HALF), 0)
    col = lax.broadcasted_iota(jnp.int32, (HALF, HALF), 1)
    own = wide(docs[:, pl.ds(pl.multiple_of(start + core * HALF, HALF), HALF)])
    return jnp.sum(jnp.where(row == col, own, 0.0), -1, keepdims=True)


def masked(scores, docs_q, docs_k, core):
    allowed = docs_q == docs_k
    if core is not None:
        q_pos = lax.broadcasted_iota(jnp.int32, scores.shape, 0) + core * HALF
        k_pos = lax.broadcasted_iota(jnp.int32, scores.shape, 1)
        allowed = allowed & (k_pos <= q_pos)
    return jnp.where(allowed, scores * SCALE, -1e30)


def widen(order, parts, limit=LIMIT):
    def kernel(flag, *refs):
        start = 0
        for ref in refs[:-1]:
            refs[-1][:, start : start + ref.shape[1]] = wide(ref[...])
            start += ref.shape[1]

    shape = (parts[0].shape[0], sum(part.shape[1] for part in parts))
    return order.call(kernel, [(shape, F32)], parts, limit=limit)[0]


def widen_with_row(order, value, row):
    def kernel(flag, a, b, out):
        rows = a.shape[0]
        out[:rows, :] = wide(a[...])
        out[rows:, :] = jnp.broadcast_to(wide(b[...]), (8, b.shape[1]))

    shape = (value.shape[0] + 8, value.shape[1])
    return order.call(kernel, [(shape, F32)], [value, row])[0]


def prepare_memory(order, older, memory, gain, shift, key_w, value_w):
    held, width = older.shape[0] + memory.shape[0], older.shape[1]
    local = key_w.shape[1]

    def kernel(flag, older_ref, memory_ref, gain_ref, shift_ref, wk, wv, normed, k, v):
        gain_row, shift_row = wide(gain_ref[...]), wide(shift_ref[...])
        for i, source in enumerate((older_ref, memory_ref)):
            for start in range(0, source.shape[0], CHUNK):
                hat, _ = standardize(wide(source[start : start + CHUNK, :]))
                at = slice(i * source.shape[0] + start, i * source.shape[0] + start + CHUNK)
                normed[at, :] = low(hat * gain_row + shift_row)
                k[at, :] = low(dot(normed[at, :], wk[...]))
                v[at, :] = low(dot(normed[at, :], wv[...]))

    outs = [((held, width), BF16), ((held, local), BF16), ((held, local), BF16)]
    return order.call(kernel, outs, [older, memory, gain, shift, key_w, value_w])


def gather_projections(order, memory_low, memory_k, memory_v, own, twin_qkv, twin_o):
    width, local = own[0].shape
    held = memory_low.shape[0]

    def kernel(flag, normed, k, v, wq, wk, wv, wo, other, other_o, q_out, k_out, v_out, o_out, ks, vs):
        for i, (ref, out) in enumerate(((wq, q_out), (wk, k_out), (wv, v_out))):
            out[:, :local] = ref[...]
            out[:, local:] = low(other[:, i * local : (i + 1) * local])
        o_out[:local, :], o_out[local:, :] = wo[...], low(other_o[...])
        ks[:, :local], vs[:, :local] = k[...], v[...]
        for start in range(0, held, CHUNK):
            at = slice(start, start + CHUNK)
            ks[at, local:] = low(dot(normed[at, :], k_out[:, local:]))
            vs[at, local:] = low(dot(normed[at, :], v_out[:, local:]))

    outs = [((width, 2 * local), BF16)] * 3 + [((2 * local, width), BF16)]
    outs += [((held, 2 * local), BF16)] * 2
    return order.call(kernel, outs, [memory_low, memory_k, memory_v, *own, twin_qkv, twin_o])


def gather_feed(order, inner_w, inner_b, outer_w, twin_inner, twin_outer):
    width, units = inner_w.shape

    def kernel(flag, wi, bi, wf, other_i, other_f, i_out, b_out, f_out):
        i_out[:, :units], i_out[:, units:] = wi[...], low(other_i[:width, :])
        b_out[:, :units], b_out[:, units:] = wide(bi[...]), other_i[width : width + 1, :]
        f_out[:units, :], f_out[units:, :] = wf[...], low(other_f[...])

    outs = [((width, 2 * units), BF16), ((1, 2 * units), F32), ((2 * units, width), BF16)]
    return order.call(kernel, outs, [inner_w, inner_b, outer_w, twin_inner, twin_outer])


def project(order, inputs, pieces, index, weights, gain, shift, keep):
    given = len(pieces)
    width, columns = weights[0].shape

    def kernel(*refs):
        flag, x_in = refs[0], refs[1]
        piece_refs, rest = refs[2 : 2 + given], refs[2 + given :]
        gain_ref, shift_ref, wq, wk, wv, x, q, kv, *rest = rest
        own = wide(x_in[chunk_at(index, flag[CORE_AT]), :])
        if given:
            put_pieces(x, piece_refs, flag[ON_AT])
            x[...] = jnp.where(flag[FIRST_AT] == 1, own, x[...])
        else:
            x[...] = own
        hat, inverse = standardize(x[...])
        normed = low(hat * wide(gain_ref[...]) + wide(shift_ref[...]))
        if keep:
            rest[0][...], rest[1][...], rest[2][...] = hat, inverse, normed
        q[...] = low(dot(normed, wq[...]))
        kv[:, :columns] = wide(low(dot(normed, wk[...])))
        kv[:, columns:] = wide(low(dot(normed, wv[...])))

    outs = [((HALF, width), F32), ((HALF, columns), BF16), ((HALF, 2 * columns), F32)]
    if keep:
        outs += [((HALF, width), F32), ((HALF, 1), F32), ((HALF, width), BF16)]
    return order.call(kernel, outs, [inputs, *pieces, gain, shift, *weights])


def swap_halves(value):
    half = value.shape[1] // 2
    return jnp.concatenate([value[:, half:], value[:, :half]], 1)


def spans(past):
    sizes = [k.shape[0] for k, _ in past] + [CHUNK]
    return [sum(sizes[:i]) for i in range(len(sizes))], sizes


def attention(q, parts, starts, sizes, docs_ref, core, lse=None):
    docs_q = own_documents(docs_ref, starts[-1], core)
    mixed = []
    for h in range(q.shape[1] // HEAD_DIM):
        cols = slice(h * HEAD_DIM, (h + 1) * HEAD_DIM)
        scores = [
            masked(
                dot_t(q[:, cols], key[:, cols]),
                docs_q,
                wide(docs_ref[:, start : start + size]),
                core if i == len(parts) - 1 else None,
            )
            for i, ((key, _), start, size) in enumerate(zip(parts, starts, sizes))
        ]
        top = scores[0].max(-1, keepdims=True)
        for score in scores[1:]:
            top = jnp.maximum(top, score.max(-1, keepdims=True))
        total, value_sum = 0.0, 0.0
        for score, (_, value) in zip(scores, parts):
            exps = jnp.exp(score - top)
            total = total + exps.sum(-1, keepdims=True)
            value_sum = value_sum + dot(low(exps), value[:, cols])
        mixed.append(low(value_sum / total))
        if lse is not None:
            lse[:, h : h + 1] = top + jnp.log(total)
    return jnp.concatenate(mixed, 1)


def attend_inputs(order, inputs, index, weights, gain, shift, past, docs, output_w):
    starts, sizes = spans(past)
    width, columns = weights[0].shape

    def kernel(flag, x_in, gain_ref, shift_ref, wq, wk, wv, docs_ref, wo, *rest):
        past_refs, rest = rest[: 2 * len(past)], rest[2 * len(past) :]
        x, k, v, out, normed = rest
        core = flag[CORE_AT]
        x[...] = wide(x_in[chunk_at(index, core), :])
        hat, _ = standardize(wide(x_in[index * CHUNK : (index + 1) * CHUNK, :]))
        normed[...] = low(hat * wide(gain_ref[...]) + wide(shift_ref[...]))
        k[...] = low(dot(normed[...], wk[...]))
        v[...] = low(dot(normed[...], wv[...]))
        q = low(dot(normed[at_rows(core, HALF), :], wq[...]))
        parts = [(past_refs[2 * i], past_refs[2 * i + 1]) for i in range(len(past))] + [(k, v)]
        out[...] = dot(attention(q, parts, starts, sizes, docs_ref, core), wo[...])

    outs = [((HALF, width), F32)] + [((CHUNK, columns), BF16)] * 2 + [((HALF, width), F32)]
    args = [inputs, gain, shift, *weights, docs, output_w] + [item for pair in past for item in pair]
    return order.call(kernel, outs, args, [pltpu.VMEM((CHUNK, width), BF16)], only=1)


def attend_chunk(order, queries, kv, kv_twin, past, docs, output_w):
    starts, sizes = spans(past)
    columns, width = output_w.shape

    def kernel(flag, q, own, other, docs_ref, wo, *rest):
        past_refs, rest = rest[: 2 * len(past)], rest[2 * len(past) :]
        k, v, out, lse, mixed = rest
        core = flag[CORE_AT]
        k[at_rows(core, HALF), :] = low(own[:, :columns])
        v[at_rows(core, HALF), :] = low(own[:, columns:])
        k[at_rows(1 - core, HALF), :] = low(swap_halves(other[:, :columns]))
        v[at_rows(1 - core, HALF), :] = low(swap_halves(other[:, columns:]))
        parts = [(past_refs[2 * i], past_refs[2 * i + 1]) for i in range(len(past))] + [(k, v)]
        mixed[...] = attention(q, parts, starts, sizes, docs_ref, core, lse)
        out[...] = dot(mixed[...], wo[...])

    outs = [((CHUNK, columns), BF16)] * 2 + [((HALF, width), F32)]
    outs += [((HALF, columns // HEAD_DIM), F32), ((HALF, columns), BF16)]
    args = [queries, kv, kv_twin, docs, output_w] + [item for pair in past for item in pair]
    return order.call(kernel, outs, args)


def feed_chunk(order, layer_input, part, arrived, output_b, gain, shift, inner_w, inner_b, outer_w):
    ending = outer_w is not None
    width, units = inner_w.shape

    def kernel(flag, x, a, b, bo, gain_ref, shift_ref, wi, bi, *rest):
        if ending:
            wf, hidden, mine, other, acc = rest
        else:
            hidden, hat_ref, inverse_ref, normed_ref, acts_ref, slope_ref = rest
        hidden[...] = x[...] + (a[...] + b[...] + wide(bo[...]))
        hat, inverse = standardize(hidden[...])
        normed = low(hat * wide(gain_ref[...]) + wide(shift_ref[...]))
        if not ending:
            hat_ref[...], inverse_ref[...], normed_ref[...] = hat, inverse, normed
        for start in range(0, units, TILE):
            tile = slice(start, start + TILE)
            acts, slope = gelu_and_slope(dot(normed, wi[:, tile]) + bi[:, tile])
            if ending:
                term = dot(low(acts), wf[tile, :])
                acc[...] = term if start == 0 else acc[...] + term
            else:
                acts_ref[:, tile] = low(acts)
                slope_ref[:, tile] = slope
        if ending:
            split_rows(acc, mine, other, flag[ON_AT])

    outs = [((HALF, width), F32)]
    if ending:
        outs += [((QUARTER, width), F32)] * 2
    else:
        outs += [
            ((HALF, width), F32),
            ((HALF, 1), F32),
            ((HALF, width), BF16),
            ((HALF, units), BF16),
            ((HALF, units), F32),
        ]
    args = [layer_input, part, arrived, output_b, gain, shift, inner_w, inner_b]
    args += [outer_w] if ending else []
    scratch = [pltpu.VMEM((HALF, width), F32)] if ending else []
    return order.call(kernel, outs, args, scratch, only=1 if ending else None)


def feed_back_chunk(order, cotangent, index, pieces, kept, outer_w, inner_w, final):
    hat, slope = kept
    given = len(pieces)
    units, width = outer_w.shape
    own_units = units // 2

    def kernel(*refs):
        flag, cot = refs[0], refs[1]
        piece_refs, rest = refs[2 : 2 + given], refs[2 + given :]
        slope_ref, wf, wi, *rest = rest
        if final:
            hat_ref, grad_out, out, branch, pre_grad, sums, passed = rest
        else:
            grad_out, out = rest
        own_cot = wide(cot[chunk_at(index, flag[CORE_AT]), :])
        if given:
            put_pieces(grad_out, piece_refs, flag[BACK_AT])
            grad_out[...] = jnp.where(flag[FIRST_AT] == 1, grad_out[...], own_cot)
        else:
            grad_out[...] = own_cot
        branch_grad = low(grad_out[...])
        for start in range(0, units, TILE):
            tile = slice(start, start + TILE)
            grad = low(slope_ref[:, tile] * dot_t(branch_grad, wf[tile, :]))
            if final and start < own_units:
                pre_grad[:, tile] = grad
            elif final:
                passed[HALF:, start - own_units : start - own_units + TILE] = wide(grad)
            term = dot_t(grad, wi[:, tile])
            out[...] = term if start == 0 else out[...] + term
        if final:
            branch[...] = branch_grad
            passed[:HALF, :] = wide(branch_grad)
            sums[0:1, :] = jnp.sum(out[...] * hat_ref[...], 0, keepdims=True)
            sums[1:2, :] = jnp.sum(out[...], 0, keepdims=True)
            sums[2:3, :] = jnp.sum(wide(branch_grad), 0, keepdims=True)
            sums[3:4, :] = jnp.zeros_like(sums[3:4, :])

    outs = [((HALF, width), F32)] * 2
    args = [cotangent, *pieces, slope, outer_w, inner_w]
    if final:
        outs += [((HALF, width), BF16), ((HALF, own_units), BF16), ((4, width), F32)]
        outs += [((CHUNK, width), F32)]
        args += [hat]
    return order.call(kernel, outs, args, only=None if final else 0)


def attend_back_chunk(
    order, grad_out, part, arrived, kept_f, queries, kv, lse, past, docs, output_w, gain_f, later, final
):
    hat_f, inverse_f = kept_f
    starts, sizes = spans(past)
    last = len(past) > 1
    columns, width = output_w.shape
    heads, local = columns // HEAD_DIM, columns // 2
    held, size = sizes[0], starts[-1] + CHUNK
    first_key = 0 if final else held

    def kernel(*refs):
        refs = list(refs)

        def take(count):
            taken = refs[:count]
            del refs[:count]
            return taken

        flag, g_out, a, b, hf, invf, gf, wo, docs_ref, q, k, v, lse_ref = take(13)
        past_refs = take(2 * len(past))
        later_refs = take(len(later))
        hidden_grad, query_rows, own, other = take(4)
        passed = take(1) if last else []
        kept = take(3) if final else []
        (sums,) = take(1)
        core = flag[CORE_AT]
        grad = standardize_back((a[...] + b[...]) * wide(gf[...]), hf[...], invf[...])
        hidden_grad[...] = g_out[...] + grad
        attend_grad = low(hidden_grad[...])
        mixed_grad = low(dot_t(attend_grad, wo[...]))
        parts = [(past_refs[2 * i], past_refs[2 * i + 1]) for i in range(len(past))] + [(k, v)]
        docs_q = own_documents(docs_ref, starts[-1], core)
        for h in range(heads):
            cols = slice(h * HEAD_DIM, (h + 1) * HEAD_DIM)
            value_cols = slice(columns + h * HEAD_DIM, columns + (h + 1) * HEAD_DIM)
            grad = mixed_grad[:, cols]
            probs, probs_grads, inner = [], [], 0.0
            for (key, value), start, length in zip(parts, starts, sizes):
                score = masked(
                    dot_t(q[:, cols], key[:, cols]),
                    docs_q,
                    wide(docs_ref[:, start : start + length]),
                    core if key is k else None,
                )
                probs.append(jnp.exp(score - lse_ref[:, h : h + 1]))
                probs_grads.append(dot_t(grad, value[:, cols]))
                inner = inner + jnp.sum(probs[-1] * probs_grads[-1], -1, keepdims=True)
            query_row = 0.0
            for i, (key, value) in enumerate(parts):
                score_grad = low(probs[i] * (probs_grads[i] - inner))
                query_row = query_row + dot(score_grad, key[:, cols])
                if i == 0 and not final:
                    continue
                at = slice(starts[i] - first_key, starts[i] - first_key + sizes[i])
                sums[at, cols] = t_dot(score_grad, q[:, cols])
                sums[at, value_cols] = t_dot(low(probs[i]), grad)
            query_rows[:, cols] = low(query_row * SCALE)
        chunk = slice(starts[-1] - first_key, size - first_key)
        if last:
            passed[0][...] = sums[starts[1] - first_key : starts[2] - first_key, :]
        else:
            sums[chunk, :] = sums[chunk, :] + later_refs[0][...]
        base = (starts[-1] - first_key) // HALF
        own[...] = sums[at_rows(base + core, HALF), :]
        other[...] = sums[at_rows(base + 1 - core, HALF), :]
        if final:
            kept[0][...] = attend_grad
            for i in range(2):
                for j in range(2):
                    cols = slice(j * columns + i * local, j * columns + (i + 1) * local)
                    total = sums[:held, cols]
                    out_cols = slice(j * local, (j + 1) * local)
                    if not last:
                        total = total + later_refs[1 + i][:, out_cols]
                    kept[1 + i][:, out_cols] = total

    outs = [((HALF, width), F32), ((HALF, columns), BF16)] + [((HALF, 2 * columns), F32)] * 2
    if last:
        outs += [((CHUNK, 2 * columns), F32)]
    if final:
        outs += [((HALF, width), BF16)] + [((held, columns), F32)] * 2
    args = [grad_out, part, arrived, hat_f, inverse_f, gain_f, output_w, docs, queries, *kv, lse]
    args += [item for pair in past for item in pair] + list(later)
    scratch = [pltpu.VMEM((size - first_key, 2 * columns), F32)]
    return order.call(kernel, outs, args, scratch, only=None if final else 0)


def project_back(order, query_rows, own, arrived, weights, hat, final):
    width, columns = weights[0].shape

    def kernel(flag, dq, a, b, wq, wk, wv, *rest):
        key_rows = low((a[:, :columns] + swap_halves(b[:, :columns])) * SCALE)
        value_rows = low(a[:, columns:] + swap_halves(b[:, columns:]))
        out = rest[1] if final else rest[-1]
        out[...] = dot_t(dq[...], wq[...]) + dot_t(key_rows, wk[...])
        out[...] = out[...] + dot_t(value_rows, wv[...])
        if final:
            hat_ref, _, keys_out, values_out, sums = rest
            keys_out[...], values_out[...] = key_rows, value_rows
            sums[0:1, :] = jnp.sum(out[...] * hat_ref[...], 0, keepdims=True)
            sums[1:2, :] = jnp.sum(out[...], 0, keepdims=True)
        else:
            split_rows(out, rest[0], rest[1], flag[BACK_AT])

    args = [query_rows, own, arrived, *weights]
    if final:
        outs = [((HALF, width), F32)] + [((HALF, columns), BF16)] * 2 + [((2, width), F32)]
        return order.call(kernel, outs, args + [hat])
    outs = [((QUARTER, width), F32)] * 2
    return order.call(kernel, outs, args, [pltpu.VMEM((HALF, width), F32)], only=0)


def add(order, *terms):
    def kernel(flag, *refs):
        total = refs[0][...]
        for ref in refs[1:-1]:
            total = total + ref[...]
        refs[-1][...] = total

    return order.call(kernel, [(terms[0].shape, F32)], terms)[0]


def finish_forward(order, mine, arrived, hidden, outer_b):
    def kernel(flag, a, b, h, bias, out):
        out[...] = a[...] + b[...] + h[at_rows(flag[ON_AT], QUARTER), :] + wide(bias[...])

    return order.call(kernel, [(mine.shape, F32)], [mine, arrived, hidden, outer_b])[0]


def finish_backward(order, mine, arrived, hat, inverse, hidden_grad, gain):
    def kernel(flag, a, b, hat_ref, inverse_ref, h, gain_ref, out):
        at = at_rows(flag[BACK_AT], QUARTER)
        grad = (a[...] + b[...]) * wide(gain_ref[...])
        out[...] = h[at, :] + standardize_back(grad, hat_ref[at, :], inverse_ref[at, :])

    args = [mine, arrived, hat, inverse, hidden_grad, gain]
    return order.call(kernel, [(mine.shape, F32)], args)[0]


def pick(order, arrived, own, receiver):
    def kernel(flag, a, b, out):
        out[...] = jnp.where(flag[FIRST_AT] == receiver, a[...], b[...])

    return order.call(kernel, [(own.shape, F32)], [arrived, own])[0]


def squeeze(order, memory, older, weight, bias):
    local = weight.shape[-1]

    def kernel(flag, memory_ref, older_ref, w, b, out):
        row = lax.broadcasted_iota(jnp.int32, (COMP, memory.shape[0]), 0)
        col = lax.broadcasted_iota(jnp.int32, (COMP, memory.shape[0]), 1)
        total = wide(b[...])
        for r in range(RATE):
            chosen = low(wide((col == row * RATE + r).astype(jnp.int32)))
            total = total + dot(low(dot(chosen, memory_ref[...])), w[r])
        out[:COMP, :] = older_ref[COMP:, at_rows(flag[MEMBER_AT], local)]
        out[COMP:, :] = low(total)

    return order.call(kernel, [((2 * COMP, local), BF16)], [memory, older, weight, bias])[0]


def memory_sums(order, older, memory, keys_grad, values_grad, key_w, value_w):
    def kernel(flag, older_ref, memory_ref, kg, vg, wk, wv, out):
        out[...] = jnp.zeros_like(out)
        for i, source in enumerate((older_ref, memory_ref)):
            for start in range(0, source.shape[0], CHUNK):
                hat, _ = standardize(wide(source[start : start + CHUNK, :]))
                at = slice(i * source.shape[0] + start, i * source.shape[0] + start + CHUNK)
                grad = dot_t(kg[at, :], wk[...]) + dot_t(vg[at, :], wv[...])
                out[0:1, :] = out[0:1, :] + jnp.sum(grad * hat, 0, keepdims=True)
                out[1:2, :] = out[1:2, :] + jnp.sum(grad, 0, keepdims=True)

    width, local = key_w.shape
    args = [older, memory, keys_grad, values_grad, key_w, value_w]
    return order.call(kernel, [((2, width), F32)], args)[0]


def block_at(index):
    return at_rows(index % 4, BLOCK)


def sub_at(index):
    return at_rows(index % 4, SUB)


def ring_sum(order, operands, make, columns, outs, place, extra=None, more=0):
    def rows_of(count, added=0):
        return ((count + added, columns), F32)

    blocks = [pltpu.VMEM((2, BLOCK, columns), F32)]

    def both(upward, up_moves, downward, down_moves):
        upward, downward = after((upward, downward), order.flags)
        return send(upward, up_moves), send(downward, down_moves)

    def far_kernel(flag, *refs):
        for q in range(2):
            refs[-2 + q][...] = make(refs, q, flag[RING_AT] + 2)

    far = order.call(far_kernel, [rows_of(BLOCK)] * 2, operands)
    yield
    below, above = both(far[0], UP, far[1], DOWN)
    yield

    def next_kernel(flag, *refs):
        below_ref, above_ref, up_ref, down_ref = refs[-4:]
        here = flag[RING_AT]
        up_ref[:BLOCK, :] = make(refs, 0, here + 1) + below_ref[...]
        up_ref[BLOCK:, :] = make(refs, 1, here + 1)
        down_ref[:BLOCK, :] = make(refs, 0, here + 3)
        down_ref[BLOCK:, :] = make(refs, 1, here + 3) + above_ref[...]

    up, down = order.call(next_kernel, [rows_of(2 * BLOCK)] * 2, [*operands, below, above])
    yield
    below, above = both(up, UP, down, DOWN)
    yield

    def own_kernel(flag, *refs):
        below_ref, above_ref, far_p, far_q, up_ref, down_ref, own_ref, acc = refs[-8:]
        here, there = flag[RING_AT], flag[RING2_AT]
        for q in range(2):
            at = slice(q * BLOCK, (q + 1) * BLOCK)
            acc[q] = make(refs, q, here) + below_ref[at, :] + above_ref[at, :]
            half = slice(q * SUB, (q + 1) * SUB)
            (far_p, far_q)[q][...] = acc[q, sub_at(there + 2), :]
            up_ref[half, :] = acc[q, sub_at(there + 1), :]
            down_ref[half, :] = acc[q, sub_at(there + 3), :]
            own_ref[half, :] = acc[q, sub_at(there), :]

    far_p, far_q, up, down, own = order.call(
        own_kernel,
        [rows_of(SUB)] * 2 + [rows_of(2 * SUB)] * 3,
        [*operands, below, above],
        scratch=blocks,
    )
    yield
    below, above = both(far_p, UP2, far_q, DOWN2)
    yield

    def next_small(flag, up_in, down_in, below_ref, above_ref, up_ref, down_ref):
        up_ref[:SUB, :], up_ref[SUB:, :] = up_in[:SUB, :] + below_ref[...], up_in[SUB:, :]
        down_ref[:SUB, :], down_ref[SUB:, :] = down_in[:SUB, :], down_in[SUB:, :] + above_ref[...]

    up, down = order.call(next_small, [rows_of(2 * SUB)] * 2, [up, down, below, above])
    yield
    below, above = both(up, UP2, down, DOWN2)
    yield
    extras = [] if extra is None else [extra()]

    def own_small(flag, own_ref, below_ref, above_ref, *rest):
        out = rest[-1]
        out[: 2 * SUB, :] = own_ref[...] + below_ref[...] + above_ref[...]
        if more:
            out[2 * SUB :, :] = rest[0][...]

    own = order.call(own_small, [rows_of(2 * SUB, more)], [own, below, above, *extras])[0]
    yield
    below, above = both(own, UP2, own, DOWN2)
    yield

    def pass_on(count):
        def kernel(flag, own_ref, below_ref, above_ref, up_ref, down_ref):
            rest = slice(2 * count, None)
            up_ref[:count, :], down_ref[:count, :] = below_ref[:count, :], above_ref[count : 2 * count, :]
            if more:
                up_ref[count:, :] = below_ref[rest, :]
                down_ref[count:, :] = own_ref[rest, :] + below_ref[rest, :] + above_ref[rest, :]

        return kernel

    up, down = order.call(pass_on(SUB), [rows_of(SUB, more)] * 2, [own, below, above])
    yield
    far_p, far_q = both(up, UP2, down, DOWN2)
    yield

    def join(flag, own_ref, below_ref, above_ref, far_p_ref, far_q_ref, *rest):
        out, acc = rest[-2:]
        there = flag[RING2_AT]
        for q, far_ref in enumerate((far_p_ref, far_q_ref)):
            half = slice(q * SUB, (q + 1) * SUB)
            acc[q, sub_at(there), :] = own_ref[half, :]
            acc[q, sub_at(there + 3), :] = below_ref[half, :]
            acc[q, sub_at(there + 1), :] = above_ref[half, :]
            acc[q, sub_at(there + 2), :] = far_ref[:SUB, :]
            out[q * BLOCK : (q + 1) * BLOCK, :] = acc[q]
        if more:
            out[2 * BLOCK :, :] = rest[0][SUB:, :] + far_p_ref[SUB:, :]

    sums = [down] if more else []
    total = order.call(
        join, [rows_of(2 * BLOCK, more)], [own, below, above, far_p, far_q, *sums], blocks
    )[0]
    yield
    below, above = both(total, UP, total, DOWN)
    yield
    up, down = order.call(pass_on(BLOCK), [rows_of(BLOCK, more)] * 2, [total, below, above])
    yield
    far_p, far_q = both(up, UP, down, DOWN)
    yield

    copies = len(place(0, 0)) + len(place(1, 0))

    def run(moves, sems):
        started = [pltpu.make_async_copy(a, b, sems.at[i]) for i, (a, b) in enumerate(moves)]
        for copy in started:
            copy.start()
        for copy in started:
            copy.wait()

    def moves_of(piece, start, q, index, out_refs):
        return [
            (piece.at[start : start + BLOCK, cols], out_refs[out].at[to])
            for cols, out, to in place(q, index)
        ]

    def first_writes(flag, own_ref, below_ref, above_ref, *rest):
        out_refs, sems = rest[:-1], rest[-1]
        here = flag[RING_AT]
        moves = []
        for piece, index in ((own_ref, here), (below_ref, here + 3), (above_ref, here + 1)):
            for q in range(2):
                moves += moves_of(piece, q * BLOCK, q, index, out_refs)
        run(moves, sems)

    outs = [(shape, F32) for shape in outs]
    results = order.call(
        first_writes,
        outs,
        [total, below, above],
        [pltpu.SemaphoreType.DMA((3 * copies,))],
        out_specs=[ANYWHERE] * len(outs),
    )
    yield

    def last_writes(flag, far_p_ref, far_q_ref, *rest):
        out_refs, sems = rest[len(outs) : -1], rest[-1]
        index = flag[RING_AT] + 2
        moves = moves_of(far_p_ref, 0, 0, index, out_refs)
        moves += moves_of(far_q_ref, 0, 1, index, out_refs)
        run(moves, sems)

    results = order.call(
        last_writes,
        outs,
        [far_p, far_q, *results],
        [pltpu.SemaphoreType.DMA((copies,))],
        specs=[WHOLE] * 2 + [ANYWHERE] * len(outs),
        out_specs=[ANYWHERE] * len(outs),
        aliases={3 + i: i for i in range(len(outs))},
    )
    if not more:
        return results

    def last_sum(flag, down_ref, far_ref, out):
        out[...] = down_ref[BLOCK:, :] + far_ref[BLOCK:, :]

    return [*results, order.call(last_sum, [rows_of(more)], [down, far_p])[0]]


class Task:
    def __init__(self, steps):
        self.steps, self.result, self.ended = steps, None, False

    def step(self, count=1):
        for _ in range(count):
            if not self.ended:
                try:
                    next(self.steps)
                except StopIteration as end:
                    self.result, self.ended = end.value, True
        return self.result

    def finish(self):
        while not self.ended:
            self.step()
        return self.result


def body(
    inputs,
    memories,
    compressed,
    documents,
    cotangent,
    compressed_cotangent,
    query_weight,
    key_weight,
    value_weight,
    output_weight,
    output_bias,
    inner_weight,
    inner_bias,
    outer_weight,
    outer_bias,
    conv_weight,
    conv_bias,
    attn_gain,
    attn_shift,
    ffn_gain,
    ffn_shift,
):
    section = lax.axis_index("pipe")
    group = lax.axis_index("dp")
    member = lax.axis_index("tensor")
    core, chip = member % 2, member // 2
    on_place = jnp.where(section == 0, chip, 1 - chip)
    y, z = group // 4, group % 4
    ring, ring2 = jnp.where(core == 0, y, z), jnp.where(core == 0, z, y)
    order = Order(
        jnp.stack([core, on_place, 1 - on_place, 1 - section, ring, ring2, member]).astype(jnp.int32)
    )
    width = inputs.shape[1]
    local = query_weight.shape[2]
    units = inner_weight.shape[2]
    held = documents.shape[1] - SEG
    chunks = range(SEG // CHUNK)
    both = CHUNK * len(chunks) // 2
    own_qkv = (query_weight[0], key_weight[0], value_weight[0])
    key_w, value_w = key_weight[0], value_weight[0]
    norm_a, norm_f = (attn_gain, attn_shift), (ffn_gain, ffn_shift)
    memory, older = memories[0, 0], compressed[0, 0]
    squeeze_cot = compressed_cotangent[0, 0]

    twin_qkv = send(widen(order, own_qkv), CORE)
    twin_o = send(widen(order, [output_weight[0]]), CORE)
    memory_low, memory_k, memory_v = prepare_memory(order, older, memory, *norm_a, key_w, value_w)
    inner_wide = widen_with_row(order, inner_weight[0], inner_bias)
    outer_wide = widen(order, [outer_weight[0]])
    *qkv_w, output_w, memory_k, memory_v = gather_projections(
        order, memory_low, memory_k, memory_v, (*own_qkv, output_weight[0]), twin_qkv, twin_o
    )
    past_memory = (memory_k, memory_v)

    def make_conv(refs, q, index):
        memory_ref, cot = refs[:2]
        row = lax.broadcasted_iota(jnp.int32, (SEG, COMP), 0)
        col = lax.broadcasted_iota(jnp.int32, (SEG, COMP), 1)
        chosen = low(wide((row == col * RATE + q).astype(jnp.int32)))
        return t_dot(memory_ref[:, block_at(index)], low(dot(chosen, cot[...])))

    def place_conv(q, index):
        return [(slice(None), 0, (q, block_at(index)))]

    conv = Task(
        ring_sum(order, [memory, squeeze_cot], make_conv, local, [(RATE, width, local)], place_conv)
    )

    inner_wide, outer_wide = after((inner_wide, outer_wide), order.flags)
    twin_inner, twin_outer = send(inner_wide, CORE), send(outer_wide, CORE)
    attended, past = [], [past_memory]
    for i in chunks:
        made = attend_inputs(order, inputs, i, qkv_w, *norm_a, past, documents, output_w)
        past = past + [tuple(made[1:3])]
        attended.append((made[0], made[3], send(made[3], CHIP)))
    inner_w, inner_b, outer_w = gather_feed(
        order, inner_weight[0], inner_bias, outer_weight[0], twin_inner, twin_outer
    )
    weights_f = (output_bias, *norm_f, inner_w, inner_b)
    hidden, mine, arrived, total, arriving = ([None, None] for _ in range(5))
    for i in chunks:
        conv.step(2)
        hidden[i], mine[i], other = feed_chunk(
            order, *attended[i], *weights_f, outer_w
        )
        arrived[i] = send(other, CHIP)
    for i in chunks:
        total[i] = finish_forward(order, mine[i], arrived[i], hidden[i], outer_bias)
        arriving[i] = send(total[i], ONWARD)


    forward = []
    for i in chunks:
        piece = pick(order, arriving[i], total[i], 0)
        forward.append([piece, send(piece, CHIP)])
    kept_p, kept_a, pasts = [], [], [[past_memory]]
    for i in chunks:
        made = project(order, inputs, forward[i], i, qkv_w, *norm_a, True)
        kept_p.append((*made, send(made[2], CORE)))
    for i in chunks:
        x, q, kv = kept_p[i][:3]
        made = attend_chunk(order, q, kv, kept_p[i][-1], pasts[i], documents, output_w)
        pasts.append(pasts[i] + [tuple(made[:2])])
        kept_a.append((*made, send(made[2], CHIP)))
    kept_f, fed = [], []
    for i in chunks:
        conv.step(2)
        kept_f.append(
            feed_chunk(order, kept_p[i][0], kept_a[i][2], kept_a[i][-1], *weights_f, None)
        )
        grad_out, out = feed_back_chunk(
            order, cotangent, i, [], (kept_f[i][1], kept_f[i][5]), outer_w, inner_w, False
        )
        fed.append((grad_out, out, send(out, CHIP)))

    def pack_rows(flag, *refs):
        out = refs[-1]
        for i, ref in enumerate(refs[:-1]):
            out[i * HALF : (i + 1) * HALF, :] = wide(ref[:, -width:])

    def attend_back(i, grad_out, out, arrived, later, final, core_moves):
        made = attend_back_chunk(
            order,
            grad_out,
            out,
            arrived,
            kept_f[i][1:3],
            kept_p[i][1],
            kept_a[i][:2],
            kept_a[i][3],
            pasts[i],
            documents,
            output_w,
            ffn_gain,
            later,
            final,
        )
        return made, send(made[3], core_moves)

    back, arrived, mine, total, backward = ([None, None] for _ in range(5))

    def begin_back(i, later):
        back[i], arrived[i] = attend_back(i, *fed[i], later, False, CORE)

    def middle_back(i):
        mine[i], other = project_back(
            order, back[i][1], back[i][2], arrived[i], qkv_w, None, False
        )
        arrived[i] = send(other, CHIP)

    def end_back(i):
        total[i] = finish_backward(
            order, mine[i], arrived[i], kept_p[i][3], kept_p[i][4], back[i][0], attn_gain
        )
        arriving[i] = send(total[i], BACK)

    def receive_back(i):
        piece = pick(order, arriving[i], total[i], 1)
        backward[i] = [piece, send(piece, CHIP)]

    conv.step(2)
    begin_back(1, [])
    conv.step(2)
    begin_back(0, [back[1][4]])
    middle_back(1)
    middle_back(0)
    args = [kept_f[i][4] for i in chunks] + [kept_f[i][3] for i in chunks]
    args += [kept_p[i][5] for i in chunks]
    twin_rows = send(order.call(pack_rows, [((len(args) * HALF, width), F32)], args)[0], CORE)


    conv.step(2)
    end_back(1)
    end_back(0)
    receive_back(1)
    receive_back(0)

    def unpack_rows(flag, *refs):
        parts, arrived_ref, outs = refs[:6], refs[6], refs[7:]
        for i, out in enumerate(outs):
            out[:HALF, :] = parts[2 * i][:, :width]
            out[HALF : 2 * HALF, :] = parts[2 * i + 1][:, :width]
            out[2 * HALF :, :] = low(arrived_ref[2 * i * HALF : 2 * (i + 1) * HALF, :])

    acts_all, normed_f_all, normed_all = order.call(
        unpack_rows, [((SEG, width), BF16)] * 3, [*args, twin_rows]
    )
    made = [None, None]
    for i in reversed(chunks):
        made[i] = feed_back_chunk(
            order, cotangent, i, backward[i], (kept_f[i][1], kept_f[i][5]), outer_w, inner_w, True
        )
        arrived[i] = send(made[i][5], CORE)
        fed[i] = (made[i][0], made[i][1], send(made[i][1], CHIP))

    def unpack_feed(flag, b0, b1, p0, p1, a0, a1, branch, pre, sums):
        for i, (ref, out) in enumerate(((b0, branch), (b1, branch), (p0, pre), (p1, pre))):
            start = i % 2 * HALF
            out[start : start + HALF, :] = ref[...]
        for i, ref in enumerate((a0, a1)):
            at = slice((2 + i) * HALF, (3 + i) * HALF)
            branch[at, :], pre[at, :] = low(ref[:HALF, :]), low(ref[HALF:, :])
        sums[...] = jnp.sum(wide(pre[...]), 0, keepdims=True)

    branch_all, pre_all, pre_sum = order.call(
        unpack_feed,
        [((SEG, width), BF16), ((SEG, units), BF16), ((1, units), F32)],
        [made[0][2], made[1][2], made[0][3], made[1][3], *arrived],
    )

    def make_feed(refs, q, index):
        acts, branch, normed, pre = refs[:4]
        left, right = (normed, pre) if q else (acts, branch)
        return t_dot(left[:, block_at(index)], right[...])

    def place_feed(q, index):
        return [(slice(None), q, (block_at(index),))]

    feeding = Task(
        ring_sum(
            order,
            [acts_all, branch_all, normed_f_all, pre_all],
            make_feed,
            width,
            [(width, width)] * 2,
            place_feed,
        )
    )
    def assemble(own):
        arrived = send(own, CORE)
        yield

        def kernel(flag, a, b, out):
            for i in chunks:
                at = slice(i * HALF, (i + 1) * HALF)
                out[chunk_at(i, flag[CORE_AT]), :] = a[at, :]
                out[chunk_at(i, 1 - flag[CORE_AT]), :] = b[at, :]

        return order.call(kernel, [((SEG, width), F32)], [own, arrived])[0]

    def layer_output():
        def kernel(flag, a0, a1, wf, out):
            for i, ref in enumerate((a0, a1)):
                out[i * HALF : (i + 1) * HALF, :] = dot(ref[...], wf[...])

        args = [kept_f[i][4] for i in chunks] + [outer_w]
        out = order.call(kernel, [((both, width), F32)], args)[0]
        yield
        arrived = send(after(out, order.flags), CHIP)
        yield

        def kernel(flag, a, b, bias, *refs):
            out, acc = refs[-2:]
            for i in chunks:
                hidden_ref, *pieces = refs[3 * i : 3 * i + 3]
                put_pieces(acc, pieces, flag[ON_AT])
                at = slice(i * HALF, (i + 1) * HALF)
                total = hidden_ref[...] + (a[at, :] + b[at, :] + wide(bias[...]))
                out[at, :] = jnp.where(flag[FIRST_AT] == 1, acc[...], total)

        args = [out, arrived, outer_bias]
        for i in chunks:
            args += [kept_f[i][0], *forward[i]]
        scratch = [pltpu.VMEM((HALF, width), F32)]
        own = order.call(kernel, [((both, width), F32)], args, scratch)[0]
        return (yield from assemble(own))

    def pack_attend(flag, *refs):
        *heads, attend_grad, out = refs
        for j, ref in enumerate(heads):
            out[:HALF, j * local : (j + 1) * local] = wide(ref[:, local:])
        out[HALF:, :] = wide(attend_grad[...])

    feeding.step(2)
    projected, heads, twin_heads = ([None, None] for _ in range(3))

    def begin_last(i, later):
        back[i], arrived[i] = attend_back(i, *fed[i], later, True, CORE)

    def end_last(i):
        projected[i] = project_back(
            order, back[i][1], back[i][2], arrived[i], qkv_w, kept_p[i][3], True
        )
        attend_grad = back[i][5 if i else 4]
        heads[i] = [back[i][1], projected[i][1], projected[i][2], kept_a[i][4], attend_grad]
        packed = order.call(pack_attend, [((CHUNK, width), F32)], heads[i])[0]
        twin_heads[i] = send(packed, CORE)

    begin_last(1, [])
    end_last(1)
    feeding.step(2)
    conv.step(2)
    begin_last(0, [back[1][4], *back[1][6:8]])
    kept = [back[0][4:], back[1][5:]]
    twin_memory = send(kept[0][2], CORE)
    end_last(0)
    outward = Task(layer_output())
    outward.step(2)
    feeding.step(2)

    def unpack_attend(flag, *refs):
        *outs, attend_out = refs[12:]
        for i in chunks:
            *parts, attend_grad, arrived_ref = refs[6 * i : 6 * i + 6]
            own, twin = i * HALF, (2 + i) * HALF
            for j, (ref, out) in enumerate(zip(parts, outs)):
                out[own : own + HALF, :] = ref[:, :local]
                out[twin : twin + HALF, :] = low(arrived_ref[:HALF, j * local : (j + 1) * local])
            attend_out[own : own + HALF, :] = attend_grad[...]
            attend_out[twin : twin + HALF, :] = low(arrived_ref[HALF:, :])

    def unpack_memory(flag, mine_ref, memory_ref, keys_out, values_out):
        keys_out[...] = low((mine_ref[:, :local] + memory_ref[:, :local]) * SCALE)
        values_out[...] = low(mine_ref[:, local:] + memory_ref[:, local:])

    *heads_all, attend_all = order.call(
        unpack_attend,
        [((SEG, local), BF16)] * 4 + [((SEG, width), BF16)],
        [item for i in chunks for item in (*heads[i], twin_heads[i])],
    )
    memory_kg, memory_vg = order.call(
        unpack_memory, [((held, local), BF16)] * 2, [kept[0][1], twin_memory]
    )
    def small_sums():
        sums_m = memory_sums(order, older, memory, memory_kg, memory_vg, key_w, value_w)

        def pack(flag, a0, a1, m, f0, f1, g0, g1, pre, cot, out):
            out[0:2, :] = a0[...] + a1[...] + m[...]
            out[2:4, :] = f0[0:2, :] + f1[0:2, :]
            out[4:5, :] = jnp.sum(wide(g0[...]) + wide(g1[...]), 0, keepdims=True)
            out[5:6, :] = f0[2:3, :] + f1[2:3, :]
            out[6:7, :] = pre[...]
            out[7:8, :] = jnp.zeros_like(out[7:8, :])
            out[7:8, :local] = jnp.sum(wide(cot[...]), 0, keepdims=True)

        args = [projected[0][3], projected[1][3], sums_m, made[0][4], made[1][4]]
        args += [kept[0][0], kept[1][0], pre_sum, squeeze_cot]
        own = order.call(pack, [((8, width), F32)], args)[0]
        arrived = send(own, CORE)
        yield
        pair = add(order, own, arrived)
        arrived = send(pair, CHIP)
        yield

        def choose(flag, a, b, own_ref, out):
            out[...] = jnp.zeros_like(out)
            for i in range(2):
                at, to = slice(i * width // 2, (i + 1) * width // 2), slice(0, width // 2)
                out[8 * i : 8 * i + 4, to] = a[0:4, at] + b[0:4, at]
                out[8 * i + 4 : 8 * i + 6, to] = a[4:6, at]
                out[8 * i + 6 : 8 * i + 8, to] = own_ref[6:8, at]

        return order.call(choose, [((16, 2 * local), F32)], [pair, arrived, own])[0]

    sums = Task(small_sums())

    def make_attend(refs, q, index):
        at = block_at(index)
        memory_ref, normed = refs[0], refs[1]
        dq, dk, dv, mixed, attend_grad, memory_keys, memory_values = refs[2:9]
        if q:
            one = t_dot(mixed[...], attend_grad[:, at])
            two = t_dot(memory_ref[:, at], memory_values[...]) + t_dot(normed[:, at], dv[...])
        else:
            one = t_dot(normed[:, at], dq[...])
            two = t_dot(memory_ref[:, at], memory_keys[...]) + t_dot(normed[:, at], dk[...])
        return jnp.concatenate([one, two], 1)

    def place_attend(q, index):
        at = block_at(index)
        one, two = (slice(i * local, (i + 1) * local) for i in range(2))
        if q:
            return [(one, 3, (slice(None), at)), (two, 2, (at,))]
        return [(one, 0, (at,)), (two, 1, (at,))]

    attending = Task(
        ring_sum(
            order,
            [
                memory_low,
                normed_all,
                *heads_all,
                attend_all,
                memory_kg,
                memory_vg,
            ],
            make_attend,
            2 * local,
            [(width, local)] * 3 + [(local, width)],
            place_attend,
            sums.finish,
            16,
        )
    )

    def input_gradient():
        def kernel(flag, a0, a1, out):
            out[:HALF, :], out[HALF:, :] = a0[...], a1[...]

        args = [projected[i][0] for i in chunks]
        out = order.call(kernel, [((both, width), F32)], args)[0]
        yield
        arrived = send(after(out, order.flags), CHIP)
        yield

        def kernel(flag, a, b, gain, *refs):
            out, acc = refs[-2:]
            for i in chunks:
                hat, inverse, hidden_grad, *pieces = refs[5 * i : 5 * i + 5]
                put_pieces(acc, pieces, flag[BACK_AT])
                at = slice(i * HALF, (i + 1) * HALF)
                grad = (a[at, :] + b[at, :]) * wide(gain[...])
                grad = hidden_grad[...] + standardize_back(grad, hat[...], inverse[...])
                out[at, :] = jnp.where(flag[FIRST_AT] == 1, grad, acc[...])

        args = [out, arrived, attn_gain]
        for i in chunks:
            args += [kept_p[i][3], kept_p[i][4], back[i][0], *backward[i]]
        scratch = [pltpu.VMEM((HALF, width), F32)]
        own = order.call(kernel, [((both, width), F32)], args, scratch)[0]
        return (yield from assemble(own))

    inward = Task(input_gradient())
    attending.step(2)
    feeding.step(2)
    outward.step()
    feeding.step(2)
    attending.step(2)
    conv.finish()
    feeding.step(2)
    attending.step(2)
    outward.finish()
    feeding.step(2)
    sums.step()
    attending.step(2)
    sums.step()
    sums.finish()
    inward.step(2)
    attending.step(2)
    attending.step(2)
    feeding.step(2)
    feeding.step()
    attending.step(2)
    outer_g, inner_g = feeding.finish()
    inward.step()
    new_compressed = squeeze(order, memory, older, conv_weight[0], conv_bias)
    attending.step(2)
    attending.step()
    inward.finish()
    query_g, key_g, value_g, output_g, total = attending.finish()

    def unpack(flag, rows_ref, *outs):
        for r, out in enumerate(outs):
            size = min(out.shape[1], width // 2)
            out[:, :size] = rows_ref[r : r + 1, :size]
            if size < out.shape[1]:
                out[:, size:] = rows_ref[8 + r : 9 + r, :size]

    total = order.call(unpack, [((1, width), F32)] * 7 + [((1, local), F32)], [total])
    return (
        outward.result[None],
        new_compressed[None, None],
        inward.result[None],
        query_g[None],
        key_g[None],
        value_g[None],
        output_g[None],
        total[4],
        inner_g[None],
        total[6],
        outer_g[None],
        total[5],
        conv.finish()[0][None],
        total[7],
        total[0],
        total[1],
        total[2],
        total[3],
    )


def solution(mesh):
    return jax.shard_map(
        body,
        mesh=mesh,
        in_specs=(
            P("dp", None),
            P("pipe", "dp", None, None),
            P("pipe", "dp", None, None),
            P("dp", None),
            P("dp", None),
            P("pipe", "dp", None, "tensor"),
            P("pipe", None, "tensor"),
            P("pipe", None, "tensor"),
            P("pipe", None, "tensor"),
            P("pipe", "tensor", None),
            P("pipe", None),
            P("pipe", None, "tensor"),
            P("pipe", "tensor"),
            P("pipe", "tensor", None),
            P("pipe", None),
            P("pipe", None, None, "tensor"),
            P("pipe", "tensor"),
            P("pipe", None),
            P("pipe", None),
            P("pipe", None),
            P("pipe", None),
        ),
        out_specs=(
            P("pipe", "dp", None),
            P("pipe", "dp", None, "tensor"),
            P("pipe", "dp", None),
            P("pipe", None, "tensor"),
            P("pipe", None, "tensor"),
            P("pipe", None, "tensor"),
            P("pipe", "tensor", None),
            P("pipe", None),
            P("pipe", None, "tensor"),
            P("pipe", "tensor"),
            P("pipe", "tensor", None),
            P("pipe", None),
            P("pipe", None, None, "tensor"),
            P("pipe", "tensor"),
            P("pipe", None),
            P("pipe", None),
            P("pipe", None),
            P("pipe", None),
        ),
        check_vma=False,
    )
```

```python
import jax
import jax.numpy as jnp
from jax import lax
from jax.experimental import pallas as pl
from jax.experimental.pallas import tpu as pltpu
from jax.sharding import PartitionSpec as P

HEAD_DIM = 128
SEG = 512
RATE = 2
COMP = 256
CHUNK = 256
HALF = 128
QUARTER = 64
TILE = 256
BLOCK = 256
SUB = 64
HEADS = 2
SCALE = HEAD_DIM ** (-0.5)
LIMIT = 10 * 2**20
AXES = ("pipe", "dp", "tensor")


def pairs(move):
    found = []
    for p in range(2):
        for y in range(4):
            for z in range(4):
                for x in range(2):
                    for c in range(2):
                        there = move(p, y, z, x, c)
                        if there is None:
                            continue
                        q, v, w, u, d = there
                        source = ((p * 4 + y) * 4 + z) * 4 + x * 2 + c
                        target = ((q * 4 + v % 4) * 4 + w % 4) * 4 + u * 2 + d
                        found.append((source, target))
    return found


CORE = pairs(lambda p, y, z, x, c: (p, y, z, x, 1 - c))
CHIP = pairs(lambda p, y, z, x, c: (p, y, z, 1 - x, c))
ONWARD = pairs(lambda p, y, z, x, c: (1, y, z, 1 - x, c) if p == 0 else None)
BACK = pairs(lambda p, y, z, x, c: (0, y, z, 1 - x, c) if p == 1 else None)
UP = pairs(lambda p, y, z, x, c: (p, y + 1 - c, z + c, x, c))
DOWN = pairs(lambda p, y, z, x, c: (p, y + 3 * (1 - c), z + 3 * c, x, c))
UP2 = pairs(lambda p, y, z, x, c: (p, y + c, z + 1 - c, x, c))
DOWN2 = pairs(lambda p, y, z, x, c: (p, y + 3 * c, z + 3 * (1 - c), x, c))
ONE = pairs(lambda p, y, z, x, c: (p, y ^ (1 - c), z ^ c, x, c))
TWO = pairs(lambda p, y, z, x, c: (p, y ^ (2 * (1 - c)), z ^ (2 * c), x, c))
ONE2 = pairs(lambda p, y, z, x, c: (p, y ^ c, z ^ (1 - c), x, c))
TWO2 = pairs(lambda p, y, z, x, c: (p, y ^ (2 * c), z ^ (2 * (1 - c)), x, c))


def low(value):
    return value.astype(jnp.bfloat16)


def wide(value):
    return value.astype(jnp.float32)


def send(value, moves):
    return lax.ppermute(value, AXES, moves)


def after(value, anchor):
    return lax.optimization_barrier((value, anchor))[0]


def dot(left, right):
    return jnp.dot(left, right, preferred_element_type=jnp.float32)


def dot_t(left, right):
    return lax.dot_general(
        left, right, (((1,), (1,)), ((), ())), preferred_element_type=jnp.float32
    )


def t_dot(left, right):
    return lax.dot_general(
        left, right, (((0,), (0,)), ((), ())), preferred_element_type=jnp.float32
    )


def standardize(values):
    centered = values - jnp.mean(values, -1, keepdims=True)
    variance = jnp.mean(centered * centered, -1, keepdims=True)
    inverse = lax.rsqrt(variance + 1e-05)
    return centered * inverse, inverse


def standardize_back(grad, hat, inverse):
    return inverse * (
        grad
        - jnp.mean(grad, -1, keepdims=True)
        - hat * jnp.mean(grad * hat, -1, keepdims=True)
    )


def gelu_and_slope(value):
    square = value * value
    curve = jnp.tanh(0.7978845608028654 * value * (1.0 + 0.044715 * square))
    up = 0.5 + 0.5 * curve
    slope = up + (0.5 * value) * (1.0 - curve * curve) * (
        0.7978845608028654 + (3 * 0.044715 * 0.7978845608028654) * square
    )
    return value * up, slope


F32, BF16 = jnp.float32, jnp.bfloat16
WHOLE = pl.BlockSpec(memory_space=pltpu.VMEM)
SCALAR = pl.BlockSpec(memory_space=pltpu.SMEM)
ANYWHERE = pl.BlockSpec(memory_space=pl.ANY)
OUTSIDE = pl.BlockSpec(memory_space=pltpu.HBM)
CORE_AT, ON_AT, BACK_AT, FIRST_AT, RING_AT, RING2_AT, MEMBER_AT = range(7)


class Order:
    def __init__(self, flags):
        self.flags = flags

    def then(self, anchor):
        self.flags = after(self.flags, anchor)

    def call(
        self, kernel, outs, args, scratch=(), specs=None, out_specs=None, aliases=None, limit=LIMIT, only=None
    ):
        args = [self.flags, *args]
        whole = kernel
        if only is not None:

            def kernel(flag, *refs):
                @pl.when(flag[FIRST_AT] == only)
                def _():
                    whole(flag, *refs)

        results = pl.pallas_call(
            kernel,
            out_shape=[jax.ShapeDtypeStruct(shape, dtype) for shape, dtype in outs],
            in_specs=[SCALAR] + (specs or [WHOLE] * (len(args) - 1)),
            out_specs=out_specs or [WHOLE] * len(outs),
            scratch_shapes=list(scratch),
            input_output_aliases=aliases or {},
            compiler_params=pltpu.CompilerParams(vmem_limit_bytes=limit),
            cost_estimate=pl.CostEstimate(flops=1, bytes_accessed=1, transcendentals=0),
        )(*args)
        self.then(tuple(results))
        return results


def at_rows(index, size):
    return pl.ds(pl.multiple_of(index * size, size), size)


def chunk_at(index, core):
    return pl.ds(pl.multiple_of(index * CHUNK + core * HALF, HALF), HALF)


def put_pieces(out_ref, pieces, place):
    out_ref[at_rows(place, QUARTER), :] = pieces[0][...]
    out_ref[at_rows(1 - place, QUARTER), :] = pieces[1][...]


def split_rows(value_ref, mine_ref, other_ref, place):
    mine_ref[...] = value_ref[at_rows(place, QUARTER), :]
    other_ref[...] = value_ref[at_rows(1 - place, QUARTER), :]


def own_documents(docs, start, core):
    row = lax.broadcasted_iota(jnp.int32, (HALF, HALF), 0)
    col = lax.broadcasted_iota(jnp.int32, (HALF, HALF), 1)
    own = wide(docs[:, pl.ds(pl.multiple_of(start + core * HALF, HALF), HALF)])
    return jnp.sum(jnp.where(row == col, own, 0.0), -1, keepdims=True)


def masked(scores, docs_q, docs_k, core):
    allowed = docs_q == docs_k
    if core is not None:
        q_pos = lax.broadcasted_iota(jnp.int32, scores.shape, 0) + core * HALF
        k_pos = lax.broadcasted_iota(jnp.int32, scores.shape, 1)
        allowed = allowed & (k_pos <= q_pos)
    return jnp.where(allowed, scores * SCALE, -1e30)


def widen(order, parts, limit=LIMIT):
    def kernel(flag, *refs):
        start = 0
        for ref in refs[:-1]:
            refs[-1][:, start : start + ref.shape[1]] = wide(ref[...])
            start += ref.shape[1]

    shape = (parts[0].shape[0], sum(part.shape[1] for part in parts))
    return order.call(kernel, [(shape, F32)], parts, limit=limit)[0]


def widen_with_row(order, value, row):
    def kernel(flag, a, b, out):
        rows = a.shape[0]
        out[:rows, :] = wide(a[...])
        out[rows:, :] = jnp.broadcast_to(wide(b[...]), (8, b.shape[1]))

    shape = (value.shape[0] + 8, value.shape[1])
    return order.call(kernel, [(shape, F32)], [value, row])[0]


def prepare_memory(order, older, memory, gain, shift, key_w, value_w):
    held, width = older.shape[0] + memory.shape[0], older.shape[1]
    local = key_w.shape[1]

    def kernel(flag, older_ref, memory_ref, gain_ref, shift_ref, wk, wv, normed, k, v):
        gain_row, shift_row = wide(gain_ref[...]), wide(shift_ref[...])
        for i, source in enumerate((older_ref, memory_ref)):
            for start in range(0, source.shape[0], CHUNK):
                hat, _ = standardize(wide(source[start : start + CHUNK, :]))
                at = slice(i * source.shape[0] + start, i * source.shape[0] + start + CHUNK)
                normed[at, :] = low(hat * gain_row + shift_row)
                k[at, :] = low(dot(normed[at, :], wk[...]))
                v[at, :] = low(dot(normed[at, :], wv[...]))

    outs = [((held, width), BF16), ((held, local), BF16), ((held, local), BF16)]
    return order.call(kernel, outs, [older, memory, gain, shift, key_w, value_w])


def gather_projections(order, memory_low, memory_k, memory_v, own, twin_qkv, twin_o):
    width, local = own[0].shape
    held = memory_low.shape[0]

    def kernel(flag, normed, k, v, wq, wk, wv, wo, other, other_o, q_out, k_out, v_out, o_out, ks, vs):
        for i, (ref, out) in enumerate(((wq, q_out), (wk, k_out), (wv, v_out))):
            out[:, :local] = ref[...]
            out[:, local:] = low(other[:, i * local : (i + 1) * local])
        o_out[:local, :], o_out[local:, :] = wo[...], low(other_o[...])
        ks[:, :local], vs[:, :local] = k[...], v[...]
        for start in range(0, held, CHUNK):
            at = slice(start, start + CHUNK)
            ks[at, local:] = low(dot(normed[at, :], k_out[:, local:]))
            vs[at, local:] = low(dot(normed[at, :], v_out[:, local:]))

    outs = [((width, 2 * local), BF16)] * 3 + [((2 * local, width), BF16)]
    outs += [((held, 2 * local), BF16)] * 2
    return order.call(kernel, outs, [memory_low, memory_k, memory_v, *own, twin_qkv, twin_o])


def gather_feed(order, inner_w, inner_b, outer_w, twin_inner, twin_outer):
    width, units = inner_w.shape

    def kernel(flag, wi, bi, wf, other_i, other_f, i_out, b_out, f_out):
        i_out[:, :units], i_out[:, units:] = wi[...], low(other_i[:width, :])
        b_out[:, :units], b_out[:, units:] = wide(bi[...]), other_i[width : width + 1, :]
        f_out[:units, :], f_out[units:, :] = wf[...], low(other_f[...])

    outs = [((width, 2 * units), BF16), ((1, 2 * units), F32), ((2 * units, width), BF16)]
    return order.call(kernel, outs, [inner_w, inner_b, outer_w, twin_inner, twin_outer])


def project(order, inputs, pieces, index, weights, gain, shift, keep):
    given = len(pieces)
    width, columns = weights[0].shape

    def kernel(*refs):
        flag, x_in = refs[0], refs[1]
        piece_refs, rest = refs[2 : 2 + given], refs[2 + given :]
        gain_ref, shift_ref, wq, wk, wv, x, q, kv, *rest = rest
        own = wide(x_in[chunk_at(index, flag[CORE_AT]), :])
        if given:
            put_pieces(x, piece_refs, flag[ON_AT])
            x[...] = jnp.where(flag[FIRST_AT] == 1, own, x[...])
        else:
            x[...] = own
        hat, inverse = standardize(x[...])
        normed = low(hat * wide(gain_ref[...]) + wide(shift_ref[...]))
        if keep:
            rest[0][...], rest[1][...], rest[2][...] = hat, inverse, normed
        q[...] = low(dot(normed, wq[...]))
        kv[:, :columns] = wide(low(dot(normed, wk[...])))
        kv[:, columns:] = wide(low(dot(normed, wv[...])))

    outs = [((HALF, width), F32), ((HALF, columns), BF16), ((HALF, 2 * columns), F32)]
    if keep:
        outs += [((HALF, width), F32), ((HALF, 1), F32), ((HALF, width), BF16)]
    return order.call(kernel, outs, [inputs, *pieces, gain, shift, *weights])


def swap_halves(value):
    half = value.shape[1] // 2
    return jnp.concatenate([value[:, half:], value[:, :half]], 1)


def spans(past):
    sizes = [k.shape[0] for k, _ in past] + [CHUNK]
    return [sum(sizes[:i]) for i in range(len(sizes))], sizes


def attention(q, parts, starts, sizes, docs_ref, core, lse=None):
    docs_q = own_documents(docs_ref, starts[-1], core)
    mixed = []
    for h in range(q.shape[1] // HEAD_DIM):
        cols = slice(h * HEAD_DIM, (h + 1) * HEAD_DIM)
        scores = [
            masked(
                dot_t(q[:, cols], key[:, cols]),
                docs_q,
                wide(docs_ref[:, start : start + size]),
                core if i == len(parts) - 1 else None,
            )
            for i, ((key, _), start, size) in enumerate(zip(parts, starts, sizes))
        ]
        top = scores[0].max(-1, keepdims=True)
        for score in scores[1:]:
            top = jnp.maximum(top, score.max(-1, keepdims=True))
        total, value_sum = 0.0, 0.0
        for score, (_, value) in zip(scores, parts):
            exps = jnp.exp(score - top)
            total = total + exps.sum(-1, keepdims=True)
            value_sum = value_sum + dot(low(exps), value[:, cols])
        mixed.append(low(value_sum / total))
        if lse is not None:
            lse[:, h : h + 1] = top + jnp.log(total)
    return jnp.concatenate(mixed, 1)


def attend_inputs(order, inputs, index, weights, gain, shift, past, docs, output_w):
    starts, sizes = spans(past)
    width, columns = weights[0].shape

    def kernel(flag, x_in, gain_ref, shift_ref, wq, wk, wv, docs_ref, wo, *rest):
        past_refs, rest = rest[: 2 * len(past)], rest[2 * len(past) :]
        x, k, v, out, normed = rest
        core = flag[CORE_AT]
        x[...] = wide(x_in[chunk_at(index, core), :])
        hat, _ = standardize(wide(x_in[index * CHUNK : (index + 1) * CHUNK, :]))
        normed[...] = low(hat * wide(gain_ref[...]) + wide(shift_ref[...]))
        k[...] = low(dot(normed[...], wk[...]))
        v[...] = low(dot(normed[...], wv[...]))
        q = low(dot(normed[at_rows(core, HALF), :], wq[...]))
        parts = [(past_refs[2 * i], past_refs[2 * i + 1]) for i in range(len(past))] + [(k, v)]
        out[...] = dot(attention(q, parts, starts, sizes, docs_ref, core), wo[...])

    outs = [((HALF, width), F32)] + [((CHUNK, columns), BF16)] * 2 + [((HALF, width), F32)]
    args = [inputs, gain, shift, *weights, docs, output_w] + [item for pair in past for item in pair]
    return order.call(kernel, outs, args, [pltpu.VMEM((CHUNK, width), BF16)], only=1)


def attend_chunk(order, queries, kv, kv_twin, past, docs, output_w):
    starts, sizes = spans(past)
    columns, width = output_w.shape

    def kernel(flag, q, own, other, docs_ref, wo, *rest):
        past_refs, rest = rest[: 2 * len(past)], rest[2 * len(past) :]
        k, v, out, lse, mixed = rest
        core = flag[CORE_AT]
        k[at_rows(core, HALF), :] = low(own[:, :columns])
        v[at_rows(core, HALF), :] = low(own[:, columns:])
        k[at_rows(1 - core, HALF), :] = low(swap_halves(other[:, :columns]))
        v[at_rows(1 - core, HALF), :] = low(swap_halves(other[:, columns:]))
        parts = [(past_refs[2 * i], past_refs[2 * i + 1]) for i in range(len(past))] + [(k, v)]
        mixed[...] = attention(q, parts, starts, sizes, docs_ref, core, lse)
        out[...] = dot(mixed[...], wo[...])

    outs = [((CHUNK, columns), BF16)] * 2 + [((HALF, width), F32)]
    outs += [((HALF, columns // HEAD_DIM), F32), ((HALF, columns), BF16)]
    args = [queries, kv, kv_twin, docs, output_w] + [item for pair in past for item in pair]
    return order.call(kernel, outs, args)


def feed_chunk(order, layer_input, part, arrived, output_b, gain, shift, inner_w, inner_b, outer_w):
    ending = outer_w is not None
    width, units = inner_w.shape

    def kernel(flag, x, a, b, bo, gain_ref, shift_ref, wi, bi, *rest):
        if ending:
            wf, hidden, mine, other, acc = rest
        else:
            hidden, hat_ref, inverse_ref, normed_ref, acts_ref, slope_ref = rest
        hidden[...] = x[...] + (a[...] + b[...] + wide(bo[...]))
        hat, inverse = standardize(hidden[...])
        normed = low(hat * wide(gain_ref[...]) + wide(shift_ref[...]))
        if not ending:
            hat_ref[...], inverse_ref[...], normed_ref[...] = hat, inverse, normed
        for start in range(0, units, TILE):
            tile = slice(start, start + TILE)
            acts, slope = gelu_and_slope(dot(normed, wi[:, tile]) + bi[:, tile])
            if ending:
                term = dot(low(acts), wf[tile, :])
                acc[...] = term if start == 0 else acc[...] + term
            else:
                acts_ref[:, tile] = low(acts)
                slope_ref[:, tile] = slope
        if ending:
            split_rows(acc, mine, other, flag[ON_AT])

    outs = [((HALF, width), F32)]
    if ending:
        outs += [((QUARTER, width), F32)] * 2
    else:
        outs += [
            ((HALF, width), F32),
            ((HALF, 1), F32),
            ((HALF, width), BF16),
            ((HALF, units), BF16),
            ((HALF, units), F32),
        ]
    args = [layer_input, part, arrived, output_b, gain, shift, inner_w, inner_b]
    args += [outer_w] if ending else []
    scratch = [pltpu.VMEM((HALF, width), F32)] if ending else []
    return order.call(kernel, outs, args, scratch, only=1 if ending else None)


def feed_back_chunk(order, cotangent, index, pieces, kept, outer_w, inner_w, final):
    hat, slope = kept
    given = len(pieces)
    units, width = outer_w.shape
    own_units = units // 2

    def kernel(*refs):
        flag, cot = refs[0], refs[1]
        piece_refs, rest = refs[2 : 2 + given], refs[2 + given :]
        slope_ref, wf, wi, *rest = rest
        if final:
            hat_ref, grad_out, out, branch, pre_grad, sums, passed = rest
        else:
            grad_out, out = rest
        own_cot = wide(cot[chunk_at(index, flag[CORE_AT]), :])
        if given:
            put_pieces(grad_out, piece_refs, flag[BACK_AT])
            grad_out[...] = jnp.where(flag[FIRST_AT] == 1, grad_out[...], own_cot)
        else:
            grad_out[...] = own_cot
        branch_grad = low(grad_out[...])
        for start in range(0, units, TILE):
            tile = slice(start, start + TILE)
            grad = low(slope_ref[:, tile] * dot_t(branch_grad, wf[tile, :]))
            if final and start < own_units:
                pre_grad[:, tile] = grad
            elif final:
                passed[HALF:, start - own_units : start - own_units + TILE] = wide(grad)
            term = dot_t(grad, wi[:, tile])
            out[...] = term if start == 0 else out[...] + term
        if final:
            branch[...] = branch_grad
            passed[:HALF, :] = wide(branch_grad)
            sums[0:1, :] = jnp.sum(out[...] * hat_ref[...], 0, keepdims=True)
            sums[1:2, :] = jnp.sum(out[...], 0, keepdims=True)
            sums[2:3, :] = jnp.sum(wide(branch_grad), 0, keepdims=True)
            sums[3:4, :] = jnp.zeros_like(sums[3:4, :])

    outs = [((HALF, width), F32)] * 2
    args = [cotangent, *pieces, slope, outer_w, inner_w]
    if final:
        outs += [((HALF, width), BF16), ((HALF, own_units), BF16), ((4, width), F32)]
        outs += [((CHUNK, width), F32)]
        args += [hat]
    return order.call(kernel, outs, args, only=None if final else 0)


def attend_back_chunk(
    order, grad_out, part, arrived, kept_f, queries, kv, lse, past, docs, output_w, gain_f, later, final
):
    hat_f, inverse_f = kept_f
    starts, sizes = spans(past)
    last = len(past) > 1
    columns, width = output_w.shape
    heads, local = columns // HEAD_DIM, columns // 2
    held, size = sizes[0], starts[-1] + CHUNK
    first_key = 0 if final else held

    def kernel(*refs):
        refs = list(refs)

        def take(count):
            taken = refs[:count]
            del refs[:count]
            return taken

        flag, g_out, a, b, hf, invf, gf, wo, docs_ref, q, k, v, lse_ref = take(13)
        past_refs = take(2 * len(past))
        later_refs = take(len(later))
        hidden_grad, query_rows, own, other = take(4)
        passed = take(1) if last else []
        kept = take(3) if final else []
        (sums,) = take(1)
        core = flag[CORE_AT]
        grad = standardize_back((a[...] + b[...]) * wide(gf[...]), hf[...], invf[...])
        hidden_grad[...] = g_out[...] + grad
        attend_grad = low(hidden_grad[...])
        mixed_grad = low(dot_t(attend_grad, wo[...]))
        parts = [(past_refs[2 * i], past_refs[2 * i + 1]) for i in range(len(past))] + [(k, v)]
        docs_q = own_documents(docs_ref, starts[-1], core)
        for h in range(heads):
            cols = slice(h * HEAD_DIM, (h + 1) * HEAD_DIM)
            value_cols = slice(columns + h * HEAD_DIM, columns + (h + 1) * HEAD_DIM)
            grad = mixed_grad[:, cols]
            probs, probs_grads, inner = [], [], 0.0
            for (key, value), start, length in zip(parts, starts, sizes):
                score = masked(
                    dot_t(q[:, cols], key[:, cols]),
                    docs_q,
                    wide(docs_ref[:, start : start + length]),
                    core if key is k else None,
                )
                probs.append(jnp.exp(score - lse_ref[:, h : h + 1]))
                probs_grads.append(dot_t(grad, value[:, cols]))
                inner = inner + jnp.sum(probs[-1] * probs_grads[-1], -1, keepdims=True)
            query_row = 0.0
            for i, (key, value) in enumerate(parts):
                score_grad = low(probs[i] * (probs_grads[i] - inner))
                query_row = query_row + dot(score_grad, key[:, cols])
                if i == 0 and not final:
                    continue
                at = slice(starts[i] - first_key, starts[i] - first_key + sizes[i])
                sums[at, cols] = t_dot(score_grad, q[:, cols])
                sums[at, value_cols] = t_dot(low(probs[i]), grad)
            query_rows[:, cols] = low(query_row * SCALE)
        chunk = slice(starts[-1] - first_key, size - first_key)
        if last:
            passed[0][...] = sums[starts[1] - first_key : starts[2] - first_key, :]
        else:
            sums[chunk, :] = sums[chunk, :] + later_refs[0][...]
        base = (starts[-1] - first_key) // HALF
        own[...] = sums[at_rows(base + core, HALF), :]
        other[...] = sums[at_rows(base + 1 - core, HALF), :]
        if final:
            kept[0][...] = attend_grad
            for i in range(2):
                for j in range(2):
                    cols = slice(j * columns + i * local, j * columns + (i + 1) * local)
                    total = sums[:held, cols]
                    out_cols = slice(j * local, (j + 1) * local)
                    if not last:
                        total = total + later_refs[1 + i][:, out_cols]
                    kept[1 + i][:, out_cols] = total

    outs = [((HALF, width), F32), ((HALF, columns), BF16)] + [((HALF, 2 * columns), F32)] * 2
    if last:
        outs += [((CHUNK, 2 * columns), F32)]
    if final:
        outs += [((HALF, width), BF16)] + [((held, columns), F32)] * 2
    args = [grad_out, part, arrived, hat_f, inverse_f, gain_f, output_w, docs, queries, *kv, lse]
    args += [item for pair in past for item in pair] + list(later)
    scratch = [pltpu.VMEM((size - first_key, 2 * columns), F32)]
    return order.call(kernel, outs, args, scratch, only=None if final else 0)


def project_back(order, query_rows, own, arrived, weights, hat, final):
    width, columns = weights[0].shape

    def kernel(flag, dq, a, b, wq, wk, wv, *rest):
        key_rows = low((a[:, :columns] + swap_halves(b[:, :columns])) * SCALE)
        value_rows = low(a[:, columns:] + swap_halves(b[:, columns:]))
        out = rest[1] if final else rest[-1]
        out[...] = dot_t(dq[...], wq[...]) + dot_t(key_rows, wk[...])
        out[...] = out[...] + dot_t(value_rows, wv[...])
        if final:
            hat_ref, _, keys_out, values_out, sums = rest
            keys_out[...], values_out[...] = key_rows, value_rows
            sums[0:1, :] = jnp.sum(out[...] * hat_ref[...], 0, keepdims=True)
            sums[1:2, :] = jnp.sum(out[...], 0, keepdims=True)
        else:
            split_rows(out, rest[0], rest[1], flag[BACK_AT])

    args = [query_rows, own, arrived, *weights]
    if final:
        outs = [((HALF, width), F32)] + [((HALF, columns), BF16)] * 2 + [((2, width), F32)]
        return order.call(kernel, outs, args + [hat])
    outs = [((QUARTER, width), F32)] * 2
    return order.call(kernel, outs, args, [pltpu.VMEM((HALF, width), F32)], only=0)


def add(order, *terms):
    def kernel(flag, *refs):
        total = refs[0][...]
        for ref in refs[1:-1]:
            total = total + ref[...]
        refs[-1][...] = total

    return order.call(kernel, [(terms[0].shape, F32)], terms)[0]


def finish_forward(order, mine, arrived, hidden, outer_b):
    def kernel(flag, a, b, h, bias, out):
        out[...] = a[...] + b[...] + h[at_rows(flag[ON_AT], QUARTER), :] + wide(bias[...])

    return order.call(kernel, [(mine.shape, F32)], [mine, arrived, hidden, outer_b])[0]


def finish_backward(order, mine, arrived, hat, inverse, hidden_grad, gain):
    def kernel(flag, a, b, hat_ref, inverse_ref, h, gain_ref, out):
        at = at_rows(flag[BACK_AT], QUARTER)
        grad = (a[...] + b[...]) * wide(gain_ref[...])
        out[...] = h[at, :] + standardize_back(grad, hat_ref[at, :], inverse_ref[at, :])

    args = [mine, arrived, hat, inverse, hidden_grad, gain]
    return order.call(kernel, [(mine.shape, F32)], args)[0]


def pick(order, arrived, own, receiver):
    def kernel(flag, a, b, out):
        out[...] = jnp.where(flag[FIRST_AT] == receiver, a[...], b[...])

    return order.call(kernel, [(own.shape, F32)], [arrived, own])[0]


def squeeze(order, memory, older, weight, bias):
    local = weight.shape[-1]

    def kernel(flag, memory_ref, older_ref, w, b, out):
        row = lax.broadcasted_iota(jnp.int32, (COMP, memory.shape[0]), 0)
        col = lax.broadcasted_iota(jnp.int32, (COMP, memory.shape[0]), 1)
        total = wide(b[...])
        for r in range(RATE):
            chosen = low(wide((col == row * RATE + r).astype(jnp.int32)))
            total = total + dot(low(dot(chosen, memory_ref[...])), w[r])
        out[:COMP, :] = older_ref[COMP:, at_rows(flag[MEMBER_AT], local)]
        out[COMP:, :] = low(total)

    return order.call(kernel, [((2 * COMP, local), BF16)], [memory, older, weight, bias])[0]


def memory_sums(order, older, memory, keys_grad, values_grad, key_w, value_w):
    def kernel(flag, older_ref, memory_ref, kg, vg, wk, wv, out):
        out[...] = jnp.zeros_like(out)
        for i, source in enumerate((older_ref, memory_ref)):
            for start in range(0, source.shape[0], CHUNK):
                hat, _ = standardize(wide(source[start : start + CHUNK, :]))
                at = slice(i * source.shape[0] + start, i * source.shape[0] + start + CHUNK)
                grad = dot_t(kg[at, :], wk[...]) + dot_t(vg[at, :], wv[...])
                out[0:1, :] = out[0:1, :] + jnp.sum(grad * hat, 0, keepdims=True)
                out[1:2, :] = out[1:2, :] + jnp.sum(grad, 0, keepdims=True)

    width, local = key_w.shape
    args = [older, memory, keys_grad, values_grad, key_w, value_w]
    return order.call(kernel, [((2, width), F32)], args)[0]


def block_at(index):
    return at_rows(index % 4, BLOCK)


def sub_at(index):
    return at_rows(index % 4, SUB)


def ring_sum(order, operands, make, columns, outs, place, extra=None, more=0):
    def rows_of(count, added=0):
        return ((count + added, columns), F32)

    blocks = [pltpu.VMEM((2, BLOCK, columns), F32)]

    def both(upward, up_moves, downward, down_moves):
        upward, downward = after((upward, downward), order.flags)
        return send(upward, up_moves), send(downward, down_moves)

    def far_kernel(flag, *refs):
        for q in range(2):
            refs[-2 + q][...] = make(refs, q, flag[RING_AT] + 2)

    far = order.call(far_kernel, [rows_of(BLOCK)] * 2, operands)
    yield
    below, above = both(far[0], UP, far[1], DOWN)
    yield

    def next_kernel(flag, *refs):
        below_ref, above_ref, up_ref, down_ref = refs[-4:]
        here = flag[RING_AT]
        up_ref[:BLOCK, :] = make(refs, 0, here + 1) + below_ref[...]
        up_ref[BLOCK:, :] = make(refs, 1, here + 1)
        down_ref[:BLOCK, :] = make(refs, 0, here + 3)
        down_ref[BLOCK:, :] = make(refs, 1, here + 3) + above_ref[...]

    up, down = order.call(next_kernel, [rows_of(2 * BLOCK)] * 2, [*operands, below, above])
    yield
    below, above = both(up, UP, down, DOWN)
    yield

    def own_kernel(flag, *refs):
        below_ref, above_ref, far_p, far_q, up_ref, down_ref, own_ref, acc = refs[-8:]
        here, there = flag[RING_AT], flag[RING2_AT]
        for q in range(2):
            at = slice(q * BLOCK, (q + 1) * BLOCK)
            acc[q] = make(refs, q, here) + below_ref[at, :] + above_ref[at, :]
            half = slice(q * SUB, (q + 1) * SUB)
            (far_p, far_q)[q][...] = acc[q, sub_at(there + 2), :]
            up_ref[half, :] = acc[q, sub_at(there + 1), :]
            down_ref[half, :] = acc[q, sub_at(there + 3), :]
            own_ref[half, :] = acc[q, sub_at(there), :]

    far_p, far_q, up, down, own = order.call(
        own_kernel,
        [rows_of(SUB)] * 2 + [rows_of(2 * SUB)] * 3,
        [*operands, below, above],
        scratch=blocks,
    )
    yield
    below, above = both(far_p, UP2, far_q, DOWN2)
    yield

    def next_small(flag, up_in, down_in, below_ref, above_ref, up_ref, down_ref):
        up_ref[:SUB, :], up_ref[SUB:, :] = up_in[:SUB, :] + below_ref[...], up_in[SUB:, :]
        down_ref[:SUB, :], down_ref[SUB:, :] = down_in[:SUB, :], down_in[SUB:, :] + above_ref[...]

    up, down = order.call(next_small, [rows_of(2 * SUB)] * 2, [up, down, below, above])
    yield
    below, above = both(up, UP2, down, DOWN2)
    yield
    extras = [] if extra is None else [extra()]

    def own_small(flag, own_ref, below_ref, above_ref, *rest):
        out = rest[-1]
        out[: 2 * SUB, :] = own_ref[...] + below_ref[...] + above_ref[...]
        if more:
            out[2 * SUB :, :] = rest[0][...]

    own = order.call(own_small, [rows_of(2 * SUB, more)], [own, below, above, *extras])[0]
    yield
    below, above = both(own, UP2, own, DOWN2)
    yield

    def pass_on(count):
        def kernel(flag, own_ref, below_ref, above_ref, up_ref, down_ref):
            rest = slice(2 * count, None)
            up_ref[:count, :], down_ref[:count, :] = below_ref[:count, :], above_ref[count : 2 * count, :]
            if more:
                up_ref[count:, :] = below_ref[rest, :]
                down_ref[count:, :] = own_ref[rest, :] + below_ref[rest, :] + above_ref[rest, :]

        return kernel

    up, down = order.call(pass_on(SUB), [rows_of(SUB, more)] * 2, [own, below, above])
    yield
    far_p, far_q = both(up, UP2, down, DOWN2)
    yield

    def join(flag, own_ref, below_ref, above_ref, far_p_ref, far_q_ref, *rest):
        out, acc = rest[-2:]
        there = flag[RING2_AT]
        for q, far_ref in enumerate((far_p_ref, far_q_ref)):
            half = slice(q * SUB, (q + 1) * SUB)
            acc[q, sub_at(there), :] = own_ref[half, :]
            acc[q, sub_at(there + 3), :] = below_ref[half, :]
            acc[q, sub_at(there + 1), :] = above_ref[half, :]
            acc[q, sub_at(there + 2), :] = far_ref[:SUB, :]
            out[q * BLOCK : (q + 1) * BLOCK, :] = acc[q]
        if more:
            out[2 * BLOCK :, :] = rest[0][SUB:, :] + far_p_ref[SUB:, :]

    sums = [down] if more else []
    total = order.call(
        join, [rows_of(2 * BLOCK, more)], [own, below, above, far_p, far_q, *sums], blocks
    )[0]
    yield
    below, above = both(total, UP, total, DOWN)
    yield
    up, down = order.call(pass_on(BLOCK), [rows_of(BLOCK, more)] * 2, [total, below, above])
    yield
    far_p, far_q = both(up, UP, down, DOWN)
    yield

    copies = len(place(0, 0)) + len(place(1, 0))

    def run(moves, sems):
        started = [pltpu.make_async_copy(a, b, sems.at[i]) for i, (a, b) in enumerate(moves)]
        for copy in started:
            copy.start()
        for copy in started:
            copy.wait()

    def moves_of(piece, start, q, index, out_refs):
        return [
            (piece.at[start : start + BLOCK, cols], out_refs[out].at[to])
            for cols, out, to in place(q, index)
        ]

    def first_writes(flag, own_ref, below_ref, above_ref, *rest):
        out_refs, sems = rest[:-1], rest[-1]
        here = flag[RING_AT]
        moves = []
        for piece, index in ((own_ref, here), (below_ref, here + 3), (above_ref, here + 1)):
            for q in range(2):
                moves += moves_of(piece, q * BLOCK, q, index, out_refs)
        run(moves, sems)

    outs = [(shape, F32) for shape in outs]
    results = order.call(
        first_writes,
        outs,
        [total, below, above],
        [pltpu.SemaphoreType.DMA((3 * copies,))],
        out_specs=[ANYWHERE] * len(outs),
    )
    yield

    def last_writes(flag, far_p_ref, far_q_ref, *rest):
        out_refs, sems = rest[len(outs) : -1], rest[-1]
        index = flag[RING_AT] + 2
        moves = moves_of(far_p_ref, 0, 0, index, out_refs)
        moves += moves_of(far_q_ref, 0, 1, index, out_refs)
        run(moves, sems)

    results = order.call(
        last_writes,
        outs,
        [far_p, far_q, *results],
        [pltpu.SemaphoreType.DMA((copies,))],
        specs=[WHOLE] * 2 + [ANYWHERE] * len(outs),
        out_specs=[ANYWHERE] * len(outs),
        aliases={3 + i: i for i in range(len(outs))},
    )
    if not more:
        return results

    def last_sum(flag, down_ref, far_ref, out):
        out[...] = down_ref[BLOCK:, :] + far_ref[BLOCK:, :]

    return [*results, order.call(last_sum, [rows_of(more)], [down, far_p])[0]]


class Task:
    def __init__(self, steps):
        self.steps, self.result, self.ended = steps, None, False

    def step(self, count=1):
        for _ in range(count):
            if not self.ended:
                try:
                    next(self.steps)
                except StopIteration as end:
                    self.result, self.ended = end.value, True
        return self.result

    def finish(self):
        while not self.ended:
            self.step()
        return self.result


def body(
    inputs,
    memories,
    compressed,
    documents,
    cotangent,
    compressed_cotangent,
    query_weight,
    key_weight,
    value_weight,
    output_weight,
    output_bias,
    inner_weight,
    inner_bias,
    outer_weight,
    outer_bias,
    conv_weight,
    conv_bias,
    attn_gain,
    attn_shift,
    ffn_gain,
    ffn_shift,
):
    section = lax.axis_index("pipe")
    group = lax.axis_index("dp")
    member = lax.axis_index("tensor")
    core, chip = member % 2, member // 2
    on_place = jnp.where(section == 0, chip, 1 - chip)
    y, z = group // 4, group % 4
    ring, ring2 = jnp.where(core == 0, y, z), jnp.where(core == 0, z, y)
    order = Order(
        jnp.stack([core, on_place, 1 - on_place, 1 - section, ring, ring2, member]).astype(jnp.int32)
    )
    width = inputs.shape[1]
    local = query_weight.shape[2]
    units = inner_weight.shape[2]
    held = documents.shape[1] - SEG
    chunks = range(SEG // CHUNK)
    both = CHUNK * len(chunks) // 2
    own_qkv = (query_weight[0], key_weight[0], value_weight[0])
    key_w, value_w = key_weight[0], value_weight[0]
    norm_a, norm_f = (attn_gain, attn_shift), (ffn_gain, ffn_shift)
    memory, older = memories[0, 0], compressed[0, 0]
    squeeze_cot = compressed_cotangent[0, 0]

    twin_qkv = send(widen(order, own_qkv), CORE)
    twin_o = send(widen(order, [output_weight[0]]), CORE)
    memory_low, memory_k, memory_v = prepare_memory(order, older, memory, *norm_a, key_w, value_w)
    inner_wide = widen_with_row(order, inner_weight[0], inner_bias)
    outer_wide = widen(order, [outer_weight[0]])
    *qkv_w, output_w, memory_k, memory_v = gather_projections(
        order, memory_low, memory_k, memory_v, (*own_qkv, output_weight[0]), twin_qkv, twin_o
    )
    past_memory = (memory_k, memory_v)

    def make_conv(refs, q, index):
        memory_ref, cot = refs[:2]
        row = lax.broadcasted_iota(jnp.int32, (SEG, COMP), 0)
        col = lax.broadcasted_iota(jnp.int32, (SEG, COMP), 1)
        chosen = low(wide((row == col * RATE + q).astype(jnp.int32)))
        return t_dot(memory_ref[:, block_at(index)], low(dot(chosen, cot[...])))

    def place_conv(q, index):
        return [(slice(None), 0, (q, block_at(index)))]

    conv = Task(
        ring_sum(order, [memory, squeeze_cot], make_conv, local, [(RATE, width, local)], place_conv)
    )

    inner_wide, outer_wide = after((inner_wide, outer_wide), order.flags)
    twin_inner, twin_outer = send(inner_wide, CORE), send(outer_wide, CORE)
    attended, past = [], [past_memory]
    for i in chunks:
        made = attend_inputs(order, inputs, i, qkv_w, *norm_a, past, documents, output_w)
        past = past + [tuple(made[1:3])]
        attended.append((made[0], made[3], send(made[3], CHIP)))
    inner_w, inner_b, outer_w = gather_feed(
        order, inner_weight[0], inner_bias, outer_weight[0], twin_inner, twin_outer
    )
    weights_f = (output_bias, *norm_f, inner_w, inner_b)
    hidden, mine, arrived, total, arriving = ([None, None] for _ in range(5))
    for i in chunks:
        conv.step(2)
        hidden[i], mine[i], other = feed_chunk(
            order, *attended[i], *weights_f, outer_w
        )
        arrived[i] = send(other, CHIP)
    for i in chunks:
        total[i] = finish_forward(order, mine[i], arrived[i], hidden[i], outer_bias)
        arriving[i] = send(total[i], ONWARD)


    forward = []
    for i in chunks:
        piece = pick(order, arriving[i], total[i], 0)
        forward.append([piece, send(piece, CHIP)])
    kept_p, kept_a, pasts = [], [], [[past_memory]]
    for i in chunks:
        made = project(order, inputs, forward[i], i, qkv_w, *norm_a, True)
        kept_p.append((*made, send(made[2], CORE)))
    for i in chunks:
        x, q, kv = kept_p[i][:3]
        made = attend_chunk(order, q, kv, kept_p[i][-1], pasts[i], documents, output_w)
        pasts.append(pasts[i] + [tuple(made[:2])])
        kept_a.append((*made, send(made[2], CHIP)))
    kept_f, fed = [], []
    for i in chunks:
        if i:
            conv.step(2)
        kept_f.append(
            feed_chunk(order, kept_p[i][0], kept_a[i][2], kept_a[i][-1], *weights_f, None)
        )
        grad_out, out = feed_back_chunk(
            order, cotangent, i, [], (kept_f[i][1], kept_f[i][5]), outer_w, inner_w, False
        )
        fed.append((grad_out, out, send(out, CHIP)))

    def pack_rows(flag, *refs):
        out = refs[-1]
        for i, ref in enumerate(refs[:-1]):
            out[i * HALF : (i + 1) * HALF, :] = wide(ref[:, -width:])

    def attend_back(i, grad_out, out, arrived, later, final, core_moves):
        made = attend_back_chunk(
            order,
            grad_out,
            out,
            arrived,
            kept_f[i][1:3],
            kept_p[i][1],
            kept_a[i][:2],
            kept_a[i][3],
            pasts[i],
            documents,
            output_w,
            ffn_gain,
            later,
            final,
        )
        return made, send(made[3], core_moves)

    back, arrived, mine, total, backward = ([None, None] for _ in range(5))

    def begin_back(i, later):
        back[i], arrived[i] = attend_back(i, *fed[i], later, False, CORE)

    def middle_back(i):
        mine[i], other = project_back(
            order, back[i][1], back[i][2], arrived[i], qkv_w, None, False
        )
        arrived[i] = send(other, CHIP)

    def end_back(i):
        total[i] = finish_backward(
            order, mine[i], arrived[i], kept_p[i][3], kept_p[i][4], back[i][0], attn_gain
        )
        arriving[i] = send(total[i], BACK)

    def receive_back(i):
        piece = pick(order, arriving[i], total[i], 1)
        backward[i] = [piece, send(piece, CHIP)]

    conv.step(2)
    begin_back(1, [])
    conv.step(2)
    begin_back(0, [back[1][4]])
    middle_back(1)
    middle_back(0)
    args = [kept_f[i][4] for i in chunks] + [kept_f[i][3] for i in chunks]
    args += [kept_p[i][5] for i in chunks]
    twin_rows = send(order.call(pack_rows, [((len(args) * HALF, width), F32)], args)[0], CORE)


    conv.step(2)
    end_back(1)
    end_back(0)
    receive_back(1)
    receive_back(0)

    def unpack_rows(flag, *refs):
        parts, arrived_ref, outs = refs[:6], refs[6], refs[7:]
        for i, out in enumerate(outs):
            out[:HALF, :] = parts[2 * i][:, :width]
            out[HALF : 2 * HALF, :] = parts[2 * i + 1][:, :width]
            out[2 * HALF :, :] = low(arrived_ref[2 * i * HALF : 2 * (i + 1) * HALF, :])

    acts_all, normed_f_all, normed_all = order.call(
        unpack_rows, [((SEG, width), BF16)] * 3, [*args, twin_rows]
    )
    made = [None, None]
    for i in reversed(chunks):
        made[i] = feed_back_chunk(
            order, cotangent, i, backward[i], (kept_f[i][1], kept_f[i][5]), outer_w, inner_w, True
        )
        arrived[i] = send(made[i][5], CORE)
        fed[i] = (made[i][0], made[i][1], send(made[i][1], CHIP))

    def unpack_feed(flag, b0, b1, p0, p1, a0, a1, branch, pre, sums):
        for i, (ref, out) in enumerate(((b0, branch), (b1, branch), (p0, pre), (p1, pre))):
            start = i % 2 * HALF
            out[start : start + HALF, :] = ref[...]
        for i, ref in enumerate((a0, a1)):
            at = slice((2 + i) * HALF, (3 + i) * HALF)
            branch[at, :], pre[at, :] = low(ref[:HALF, :]), low(ref[HALF:, :])
        sums[...] = jnp.sum(wide(pre[...]), 0, keepdims=True)

    branch_all, pre_all, pre_sum = order.call(
        unpack_feed,
        [((SEG, width), BF16), ((SEG, units), BF16), ((1, units), F32)],
        [made[0][2], made[1][2], made[0][3], made[1][3], *arrived],
    )

    def make_feed(refs, q, index):
        acts, branch, normed, pre = refs[:4]
        left, right = (normed, pre) if q else (acts, branch)
        return t_dot(left[:, block_at(index)], right[...])

    def place_feed(q, index):
        return [(slice(None), q, (block_at(index),))]

    feeding = Task(
        ring_sum(
            order,
            [acts_all, branch_all, normed_f_all, pre_all],
            make_feed,
            width,
            [(width, width)] * 2,
            place_feed,
        )
    )
    def assemble(own):
        arrived = send(own, CORE)
        yield

        def kernel(flag, a, b, out):
            for i in chunks:
                at = slice(i * HALF, (i + 1) * HALF)
                out[chunk_at(i, flag[CORE_AT]), :] = a[at, :]
                out[chunk_at(i, 1 - flag[CORE_AT]), :] = b[at, :]

        return order.call(kernel, [((SEG, width), F32)], [own, arrived])[0]

    def layer_output():
        def kernel(flag, a0, a1, wf, out):
            for i, ref in enumerate((a0, a1)):
                out[i * HALF : (i + 1) * HALF, :] = dot(ref[...], wf[...])

        args = [kept_f[i][4] for i in chunks] + [outer_w]
        out = order.call(kernel, [((both, width), F32)], args)[0]
        yield
        arrived = send(after(out, order.flags), CHIP)
        yield

        def kernel(flag, a, b, bias, *refs):
            out, acc = refs[-2:]
            for i in chunks:
                hidden_ref, *pieces = refs[3 * i : 3 * i + 3]
                put_pieces(acc, pieces, flag[ON_AT])
                at = slice(i * HALF, (i + 1) * HALF)
                total = hidden_ref[...] + (a[at, :] + b[at, :] + wide(bias[...]))
                out[at, :] = jnp.where(flag[FIRST_AT] == 1, acc[...], total)

        args = [out, arrived, outer_bias]
        for i in chunks:
            args += [kept_f[i][0], *forward[i]]
        scratch = [pltpu.VMEM((HALF, width), F32)]
        own = order.call(kernel, [((both, width), F32)], args, scratch)[0]
        return (yield from assemble(own))

    def pack_attend(flag, *refs):
        *heads, attend_grad, out = refs
        for j, ref in enumerate(heads):
            out[:HALF, j * local : (j + 1) * local] = wide(ref[:, local:])
        out[HALF:, :] = wide(attend_grad[...])

    feeding.step(2)
    projected, heads, twin_heads = ([None, None] for _ in range(3))

    def begin_last(i, later):
        back[i], arrived[i] = attend_back(i, *fed[i], later, True, CORE)

    def end_last(i):
        projected[i] = project_back(
            order, back[i][1], back[i][2], arrived[i], qkv_w, kept_p[i][3], True
        )
        attend_grad = back[i][5 if i else 4]
        heads[i] = [back[i][1], projected[i][1], projected[i][2], kept_a[i][4], attend_grad]
        packed = order.call(pack_attend, [((CHUNK, width), F32)], heads[i])[0]
        twin_heads[i] = send(packed, CORE)

    conv.step(2)
    begin_last(1, [])
    end_last(1)
    feeding.step(2)
    conv.step(2)
    begin_last(0, [back[1][4], *back[1][6:8]])
    kept = [back[0][4:], back[1][5:]]
    twin_memory = send(kept[0][2], CORE)
    end_last(0)
    outward = Task(layer_output())
    outward.step(2)
    feeding.step(2)

    def unpack_attend(flag, *refs):
        *outs, attend_out = refs[12:]
        for i in chunks:
            *parts, attend_grad, arrived_ref = refs[6 * i : 6 * i + 6]
            own, twin = i * HALF, (2 + i) * HALF
            for j, (ref, out) in enumerate(zip(parts, outs)):
                out[own : own + HALF, :] = ref[:, :local]
                out[twin : twin + HALF, :] = low(arrived_ref[:HALF, j * local : (j + 1) * local])
            attend_out[own : own + HALF, :] = attend_grad[...]
            attend_out[twin : twin + HALF, :] = low(arrived_ref[HALF:, :])

    def unpack_memory(flag, mine_ref, memory_ref, keys_out, values_out):
        keys_out[...] = low((mine_ref[:, :local] + memory_ref[:, :local]) * SCALE)
        values_out[...] = low(mine_ref[:, local:] + memory_ref[:, local:])

    *heads_all, attend_all = order.call(
        unpack_attend,
        [((SEG, local), BF16)] * 4 + [((SEG, width), BF16)],
        [item for i in chunks for item in (*heads[i], twin_heads[i])],
    )
    memory_kg, memory_vg = order.call(
        unpack_memory, [((held, local), BF16)] * 2, [kept[0][1], twin_memory]
    )
    def small_sums():
        sums_m = memory_sums(order, older, memory, memory_kg, memory_vg, key_w, value_w)

        def pack(flag, a0, a1, m, f0, f1, g0, g1, pre, cot, out):
            out[0:2, :] = a0[...] + a1[...] + m[...]
            out[2:4, :] = f0[0:2, :] + f1[0:2, :]
            out[4:5, :] = jnp.sum(wide(g0[...]) + wide(g1[...]), 0, keepdims=True)
            out[5:6, :] = f0[2:3, :] + f1[2:3, :]
            out[6:7, :] = pre[...]
            out[7:8, :] = jnp.zeros_like(out[7:8, :])
            out[7:8, :local] = jnp.sum(wide(cot[...]), 0, keepdims=True)

        args = [projected[0][3], projected[1][3], sums_m, made[0][4], made[1][4]]
        args += [kept[0][0], kept[1][0], pre_sum, squeeze_cot]
        own = order.call(pack, [((8, width), F32)], args)[0]
        arrived = send(own, CORE)
        yield
        pair = add(order, own, arrived)
        arrived = send(pair, CHIP)
        yield

        def choose(flag, a, b, own_ref, out):
            out[...] = jnp.zeros_like(out)
            for i in range(2):
                at, to = slice(i * width // 2, (i + 1) * width // 2), slice(0, width // 2)
                out[8 * i : 8 * i + 4, to] = a[0:4, at] + b[0:4, at]
                out[8 * i + 4 : 8 * i + 6, to] = a[4:6, at]
                out[8 * i + 6 : 8 * i + 8, to] = own_ref[6:8, at]

        return order.call(choose, [((16, 2 * local), F32)], [pair, arrived, own])[0]

    sums = Task(small_sums())

    def make_attend(refs, q, index):
        at = block_at(index)
        memory_ref, normed = refs[0], refs[1]
        dq, dk, dv, mixed, attend_grad, memory_keys, memory_values = refs[2:9]
        if q:
            one = t_dot(mixed[...], attend_grad[:, at])
            two = t_dot(memory_ref[:, at], memory_values[...]) + t_dot(normed[:, at], dv[...])
        else:
            one = t_dot(normed[:, at], dq[...])
            two = t_dot(memory_ref[:, at], memory_keys[...]) + t_dot(normed[:, at], dk[...])
        return jnp.concatenate([one, two], 1)

    def place_attend(q, index):
        at = block_at(index)
        one, two = (slice(i * local, (i + 1) * local) for i in range(2))
        if q:
            return [(one, 3, (slice(None), at)), (two, 2, (at,))]
        return [(one, 0, (at,)), (two, 1, (at,))]

    attending = Task(
        ring_sum(
            order,
            [
                memory_low,
                normed_all,
                *heads_all,
                attend_all,
                memory_kg,
                memory_vg,
            ],
            make_attend,
            2 * local,
            [(width, local)] * 3 + [(local, width)],
            place_attend,
            sums.finish,
            16,
        )
    )

    def input_gradient():
        def kernel(flag, a0, a1, out):
            out[:HALF, :], out[HALF:, :] = a0[...], a1[...]

        args = [projected[i][0] for i in chunks]
        out = order.call(kernel, [((both, width), F32)], args)[0]
        yield
        arrived = send(after(out, order.flags), CHIP)
        yield

        def kernel(flag, a, b, gain, *refs):
            out, acc = refs[-2:]
            for i in chunks:
                hat, inverse, hidden_grad, *pieces = refs[5 * i : 5 * i + 5]
                put_pieces(acc, pieces, flag[BACK_AT])
                at = slice(i * HALF, (i + 1) * HALF)
                grad = (a[at, :] + b[at, :]) * wide(gain[...])
                grad = hidden_grad[...] + standardize_back(grad, hat[...], inverse[...])
                out[at, :] = jnp.where(flag[FIRST_AT] == 1, grad, acc[...])

        args = [out, arrived, attn_gain]
        for i in chunks:
            args += [kept_p[i][3], kept_p[i][4], back[i][0], *backward[i]]
        scratch = [pltpu.VMEM((HALF, width), F32)]
        own = order.call(kernel, [((both, width), F32)], args, scratch)[0]
        return (yield from assemble(own))

    inward = Task(input_gradient())
    attending.step(2)
    feeding.step(2)
    outward.step()
    feeding.step(2)
    attending.step(2)
    conv.finish()
    feeding.step(2)
    attending.step(2)
    outward.finish()
    feeding.step(2)
    sums.step()
    attending.step(2)
    sums.step()
    sums.finish()
    inward.step(2)
    attending.step(2)
    attending.step(2)
    feeding.step(2)
    feeding.step()
    attending.step(2)
    outer_g, inner_g = feeding.finish()
    inward.step()
    new_compressed = squeeze(order, memory, older, conv_weight[0], conv_bias)
    attending.step(2)
    attending.step()
    inward.finish()
    query_g, key_g, value_g, output_g, total = attending.finish()

    def unpack(flag, rows_ref, *outs):
        for r, out in enumerate(outs):
            size = min(out.shape[1], width // 2)
            out[:, :size] = rows_ref[r : r + 1, :size]
            if size < out.shape[1]:
                out[:, size:] = rows_ref[8 + r : 9 + r, :size]

    total = order.call(unpack, [((1, width), F32)] * 7 + [((1, local), F32)], [total])
    return (
        outward.result[None],
        new_compressed[None, None],
        inward.result[None],
        query_g[None],
        key_g[None],
        value_g[None],
        output_g[None],
        total[4],
        inner_g[None],
        total[6],
        outer_g[None],
        total[5],
        conv.finish()[0][None],
        total[7],
        total[0],
        total[1],
        total[2],
        total[3],
    )


def solution(mesh):
    return jax.shard_map(
        body,
        mesh=mesh,
        in_specs=(
            P("dp", None),
            P("pipe", "dp", None, None),
            P("pipe", "dp", None, None),
            P("dp", None),
            P("dp", None),
            P("pipe", "dp", None, "tensor"),
            P("pipe", None, "tensor"),
            P("pipe", None, "tensor"),
            P("pipe", None, "tensor"),
            P("pipe", "tensor", None),
            P("pipe", None),
            P("pipe", None, "tensor"),
            P("pipe", "tensor"),
            P("pipe", "tensor", None),
            P("pipe", None),
            P("pipe", None, None, "tensor"),
            P("pipe", "tensor"),
            P("pipe", None),
            P("pipe", None),
            P("pipe", None),
            P("pipe", None),
        ),
        out_specs=(
            P("pipe", "dp", None),
            P("pipe", "dp", None, "tensor"),
            P("pipe", "dp", None),
            P("pipe", None, "tensor"),
            P("pipe", None, "tensor"),
            P("pipe", None, "tensor"),
            P("pipe", "tensor", None),
            P("pipe", None),
            P("pipe", None, "tensor"),
            P("pipe", "tensor"),
            P("pipe", "tensor", None),
            P("pipe", None),
            P("pipe", None, None, "tensor"),
            P("pipe", "tensor"),
            P("pipe", None),
            P("pipe", None),
            P("pipe", None),
            P("pipe", None),
        ),
        check_vma=False,
    )
```
